32 devices in a mesh: blk: 16 (over z, y, x), day: 2 (over core).
Axes of the slice: x: 2, y: 2, z: 4, core: 2. Of those that a mesh axis runs over, the one named last changes fastest.
Arguments:
- input_field: float32 [2, 6, 128, 4096], P(None, 'day', 'blk'), may hold values from -6 to 6
- active_mask: int32 [128], P('blk'), may hold values from 0 to 1, as said below
- neighbours: int32 [128, 8], P('blk'), may hold values from -1 to 127, as said below
- time_taps: float32 [4], replicated, may hold values from 0.1 to 0.5
- space_taps: float32 [2, 5], replicated, may hold values from 0.1 to 0.5
- coregion_factor: float32 [2, 2], replicated, may hold values from -2.5 to 2.5
Outputs:
- covariance_product: float32 [2, 6, 128, 4096], P(None, 'day', 'blk')
The draws below stay inside these ranges and needn't reach their ends.
Inputs may be any that keep to these rules, and one draw needn't show every extreme that they name: `active_mask`: device i along blk holds in its 8 slots, in a drawn order, the map positions i * 8 to i * 8 + 7 of a map of 4 rows of 32 positions numbered row by row; every position of the first two map rows is active, others are active at random. Entries name the global slot (device index along blk times 8 plus local slot) of the active map block beside the block in that direction, -1 where there is none or it is inactive; all entries of an inactive slot are -1. East and west neighbours are held by the same device or one place away along blk; north and south ones by the device 4 places away; the four diagonal ones by the device 4 places away or one place nearer or farther than that, and all these cases occur.
All inputs are finite; a program needn't handle non-finite values.
Results may differ from the reference program's by a relative error of at most 0.0003.
Values sent between devices are 32-bit elements; how exact they have to be, the bound alone decides.
No kernel may reach another device: no remote copies, remote signals or barrier semaphores. Data moves between devices by JAX's collectives and lax.ppermute only.
A program may use at most 64 MiB of HBM per device.

```python
import jax
import jax.numpy as jnp
from jax import lax

COMPS = 2
SIDE = 64
CELLS = 4096
SPACE_HALF = 4
TIME_HALF = 3
REACH = 4
BLOCKS_DEV = 8
DAYS = 6
SLOTS = 128
MAP_ROWS = 4
MAP_COLS = 32


def block_layout(key):
    devices_along = MAP_ROWS * REACH
    order_key, active_key = jax.random.split(jax.random.fold_in(key, 11))
    scores = jax.random.randint(order_key, (devices_along, BLOCKS_DEV), 0, 1048576) * BLOCKS_DEV + jnp.arange(BLOCKS_DEV, dtype=jnp.int32)[None, :]
    position_of_slot = jnp.argsort(scores, axis=1).astype(jnp.int32)
    slot_of_position = jnp.argsort(position_of_slot, axis=1).astype(jnp.int32)
    device_ids = jnp.arange(devices_along, dtype=jnp.int32)[:, None]
    global_position = (device_ids * BLOCKS_DEV + position_of_slot).reshape(-1)
    slot_at_position = (device_ids * BLOCKS_DEV + slot_of_position).reshape(-1)
    coins = jax.random.randint(active_key, (SLOTS,), 0, 10)
    map_row_of = jnp.arange(SLOTS, dtype=jnp.int32) // MAP_COLS
    active_at = ((coins < 8) | (map_row_of < 2)).astype(jnp.int32)
    active_slot = active_at[global_position]
    map_row = global_position // MAP_COLS
    map_col = global_position % MAP_COLS
    moves = [(0, 1), (0, -1), (-1, 0), (1, 0), (-1, 1), (-1, -1), (1, 1), (1, -1)]
    columns = []
    for row_move, col_move in moves:
        next_row = map_row + row_move
        next_col = map_col + col_move
        inside = (next_row >= 0) & (next_row < MAP_ROWS) & (next_col >= 0) & (next_col < MAP_COLS)
        next_position = jnp.clip(next_row, 0, MAP_ROWS - 1) * MAP_COLS + jnp.clip(next_col, 0, MAP_COLS - 1)
        usable = inside & (active_at[next_position] == 1) & (active_slot == 1)
        columns.append(jnp.where(usable, slot_at_position[next_position], -1))
    return (active_slot.astype(jnp.int32), jnp.stack(columns, axis=1).astype(jnp.int32))


def draw_active_mask(key, part):
    return block_layout(key)[0]


def draw_neighbours(key, part):
    return block_layout(key)[1]


def block_levels(own_key, extent, cuts, low, high):
    factor_of, own = 1.0, jax.random.fold_in(own_key, 6)
    for dim, parts in cuts:
        heights = jnp.exp(jax.random.uniform(jax.random.fold_in(own, dim), (parts,), jnp.float32, low / len(cuts), high / len(cuts)))
        factor_of = factor_of * jnp.repeat(heights, extent[dim] // parts).reshape([-1 if axis == dim else 1 for axis in range(len(extent))])
    return factor_of


def bell_draw(stream_key, extent, deviation, most, cuts=(), kind=jnp.bfloat16):
    gain = block_levels(stream_key, extent, cuts, -0.22, 0.18) if cuts else 1.0
    array = jax.random.normal(stream_key, extent, jnp.float32) * deviation * gain
    return jnp.minimum(jnp.maximum(array, -most), most).astype(kind)


def setup_inputs(seed: int = 0) -> dict:
    splits = jax.random.split(jax.random.key(seed), 7)
    return {
        "input_field": bell_draw(splits[0], (COMPS, DAYS, SLOTS, CELLS), 1.0, 6.0, ((1, 2), (2, 16)), jnp.float32),
        "active_mask": draw_active_mask(jax.random.fold_in(splits[6], 71), 0),
        "neighbours": draw_neighbours(jax.random.fold_in(splits[6], 71), 0),
        "time_taps": jnp.clip(jax.random.uniform(splits[3], (TIME_HALF + 1,), jnp.float32, 0.1, 0.5), 0.1, 0.5),
        "space_taps": jnp.clip(jax.random.uniform(splits[4], (2, SPACE_HALF + 1), jnp.float32, 0.1, 0.5), 0.1, 0.5),
        "coregion_factor": bell_draw(splits[5], (COMPS, COMPS), 0.8, 2.5, (), jnp.float32),
    }


def full_taps(tap_list, half_width):
    return [tap_list[abs(offset - half_width)] for offset in range(2 * half_width + 1)]


def coupling(coregion_factor):
    rows_list = []
    for first in range(2):
        rows_list.append(jnp.stack([coregion_factor[first, 0] * coregion_factor[second, 0] + coregion_factor[first, 1] * coregion_factor[second, 1] for second in range(2)]))
    return jnp.stack(rows_list)


def mix_outputs(weights, filtered):
    return jnp.stack([weights[0, 0] * filtered[0] + weights[0, 1] * filtered[1], weights[1, 0] * filtered[0] + weights[1, 1] * filtered[1]])


def cut_strips(blocks, half_width):
    leading = blocks.shape[:-2]
    east_strip = blocks[..., :, blocks.shape[-1] - half_width:]
    west_strip = blocks[..., :, :half_width]
    north_strip = blocks[..., :half_width, :]
    south_strip = blocks[..., blocks.shape[-2] - half_width:, :]
    return [strip_piece.reshape(leading + (-1,)) for strip_piece in (east_strip, west_strip, north_strip, south_strip)]


def frame(blocks, fetch_strip, half_width, block_side):
    leading = blocks.shape[:-2]
    east_face = fetch_strip(0, 1).reshape(leading + (block_side, half_width))
    west_face = fetch_strip(1, 0).reshape(leading + (block_side, half_width))
    north_face = fetch_strip(2, 3).reshape(leading + (half_width, block_side))
    south_face = fetch_strip(3, 2).reshape(leading + (half_width, block_side))
    north_east = fetch_strip(4, 3).reshape(leading + (half_width, block_side))[..., :half_width]
    north_west = fetch_strip(5, 3).reshape(leading + (half_width, block_side))[..., block_side - half_width:]
    south_east = fetch_strip(6, 2).reshape(leading + (half_width, block_side))[..., :half_width]
    south_west = fetch_strip(7, 2).reshape(leading + (half_width, block_side))[..., block_side - half_width:]
    upper_rows = jnp.concatenate([north_west, north_face, north_east], axis=-1)
    middle = jnp.concatenate([west_face, blocks, east_face], axis=-1)
    bottom = jnp.concatenate([south_west, south_face, south_east], axis=-1)
    return jnp.concatenate([upper_rows, middle, bottom], axis=-2)


def smooth(padded, taps_across, taps_down, block_side):
    across = None
    for offset in range(len(taps_across)):
        addend = taps_across[offset] * padded[..., :, offset:offset + block_side]
        across = addend if across is None else across + addend
    downward = None
    for offset in range(len(taps_down)):
        addend = taps_down[offset] * across[..., offset:offset + block_side, :]
        downward = addend if downward is None else downward + addend
    return downward


def reference(input_field, active_mask, neighbours, time_taps, space_taps, coregion_factor):
    live_mask = active_mask.astype(jnp.float32)
    weights = coupling(coregion_factor)
    taps_across = full_taps(space_taps[0], SPACE_HALF)
    taps_down = full_taps(space_taps[1], SPACE_HALF)

    def one_day(day_index):
        filtered = None
        for offset in range(-TIME_HALF, TIME_HALF + 1):
            shifted = day_index + offset
            inside = ((shifted >= 0) & (shifted < DAYS)).astype(jnp.float32)
            picked = lax.dynamic_index_in_dim(input_field, jnp.clip(shifted, 0, DAYS - 1).astype(jnp.int32), 1, keepdims=False)
            addend = (time_taps[abs(offset)] * inside) * (picked * live_mask[None, :, None])
            filtered = addend if filtered is None else filtered + addend
        mixed_field = mix_outputs(weights, filtered)
        blocks = mixed_field.reshape((COMPS, SLOTS, SIDE, SIDE))
        strip_list = cut_strips(blocks, SPACE_HALF)

        def fetch_strip(direction, strip):
            target = neighbours[:, direction]
            present = (target >= 0).astype(jnp.float32)[None, :, None]
            return jnp.take(strip_list[strip], jnp.clip(target, 0, SLOTS - 1), axis=1) * present

        padded = frame(blocks, fetch_strip, SPACE_HALF, SIDE)
        result = smooth(padded, taps_across, taps_down, SIDE)
        return result.reshape((COMPS, SLOTS, CELLS)) * live_mask[None, :, None]

    stacked = lax.map(one_day, jnp.arange(DAYS, dtype=jnp.int32))
    return jnp.moveaxis(stacked, 0, 1)
```

```python
import functools

import jax
import jax.numpy as jnp
from jax import lax
from jax.experimental import pallas as pl
from jax.experimental.pallas import tpu as pltpu
from jax.sharding import PartitionSpec as P

SIDE = 64
SPACE_HALF = 4
TIME_HALF = 3
REACH = 4
LANES = 128
EAST, WEST, NORTH, SOUTH, NORTH_EAST, NORTH_WEST, SOUTH_EAST, SOUTH_WEST = range(8)
STRIP = SPACE_HALF * SIDE
PARAMS = pltpu.CompilerParams(vmem_limit_bytes=12 * 1024 * 1024)
SMEM = pl.BlockSpec(memory_space=pltpu.SMEM)


def iotas(slots):
    lane = lax.broadcasted_iota(jnp.int32, (slots, LANES), 1)
    sublane = lax.broadcasted_iota(jnp.int32, (slots, LANES), 0)
    return lane, sublane


def live_vector(mask_ref, sublane):
    live = jnp.zeros(sublane.shape, jnp.float32)
    for slot in range(sublane.shape[0]):
        live = jnp.where(sublane == slot, mask_ref[slot].astype(jnp.float32), live)
    return live


def entry(neighbours, direction, shape):
    return jnp.broadcast_to(neighbours[:, direction : direction + 1], shape)


def pick(source, index):
    return jnp.take_along_axis(source, index, axis=0)


def roll(x, shift):
    return pltpu.roll(x, shift % LANES if isinstance(shift, int) else shift, 1)


def on_device(target, device, slots):
    return (target >= 0) & (target // slots == device)


def filter_kernel(pair, place_ref, mask_ref, taps_ref, factor_ref, nb_ref, x_ref, *rest):
    *other_refs, mixed_ref, first_ref, second_ref = rest
    slots, cells = mixed_ref.shape[1:]
    days = x_ref.shape[1]
    me, day = place_ref[0], place_ref[1]
    lane, sublane = iotas(slots)
    column = jnp.bitwise_and(lane, SIDE - 1)
    live = live_vector(mask_ref, sublane)
    taps = [taps_ref[lag] for lag in range(TIME_HALF + 1)]
    weights = [
        [
            live * (factor_ref[a, 0] * factor_ref[b, 0] + factor_ref[a, 1] * factor_ref[b, 1])
            for b in range(2)
        ]
        for a in range(2)
    ]
    nb = nb_ref[...]

    def end_slot(directions, devices):
        hit = None
        for direction, device in zip(directions, devices):
            one = on_device(entry(nb, direction, lane.shape), device, slots)
            hit = one if hit is None else hit | one
        return jnp.max(jnp.where(hit, sublane, 0), axis=0, keepdims=True)

    east_end = end_slot((EAST, NORTH_EAST, SOUTH_EAST), (me + 1, me + 1 - REACH, me + 1 + REACH))
    west_end = end_slot((WEST, NORTH_WEST, SOUTH_WEST), (me - 1, me - 1 - REACH, me - 1 + REACH))
    end_index = jnp.where(
        column >= SIDE // 2,
        jnp.broadcast_to(east_end, lane.shape),
        jnp.broadcast_to(west_end, lane.shape),
    )
    order = [day * (days - 1 - 2 * s) + s if pair else s for s in range(days)]
    group = column // SPACE_HALF
    groups = SIDE // SPACE_HALF
    is_row = [sublane == a * days + order[t] for a in range(2) for t in range(days)]

    def part(tile, step):
        filtered = []
        where = pl.ds(pl.multiple_of((tile * groups + step) * LANES, LANES), LANES)
        for comp in range(2):
            own = [x_ref[comp, order[s], :, where] for s in range(days)]
            totals = []
            for t in range(days):
                total = taps[0] * own[t]
                for s in range(days):
                    if s != t:
                        total = total + taps[abs(s - t)] * own[s]
                totals.append(total)
            later = [other_refs[-1][comp, order[s], :, where] for s in range(days)]
            for t in range(days):
                for s in range(t + 1):
                    totals[t] = totals[t] + taps[days + s - t] * later[s]
            if not pair:
                earlier = [other_refs[0][comp, s, :, where] for s in range(days)]
                for t in range(days):
                    for s in range(t, days):
                        totals[t] = totals[t] + taps[days + t - s] * earlier[s]
            filtered.append(totals)
        edge = jnp.zeros(lane.shape, jnp.float32)
        for a in range(2):
            for t in range(days):
                value = weights[a][0] * filtered[0][t] + weights[a][1] * filtered[1][t]
                mixed_ref[a * days + order[t], :, where] = value
                edge = jnp.where(is_row[a * days + t], pick(value, end_index), edge)
        return edge

    parity = jnp.bitwise_and(me, 1) == 0
    for tile in range(cells // (groups * LANES)):

        def body(step, held):
            east, west = held
            edge = part(tile, step)
            back = jnp.bitwise_and(LANES - SPACE_HALF * step, LANES - 1)
            east = jnp.where(group == groups - 1 - step, roll(edge, back), east)
            west = jnp.where(group == step, roll(edge, SPACE_HALF * step), west)
            return east, west

        zero = jnp.zeros(lane.shape, jnp.float32)
        east, west = lax.fori_loop(0, groups, body, (zero, zero))
        place = slice(tile * LANES, (tile + 1) * LANES)
        first_ref[:, place] = jnp.where(parity, east, west)
        second_ref[:, place] = jnp.where(parity, west, east)


def west_east(parity, first_ref, second_ref, tile):
    place = slice(tile * LANES, (tile + 1) * LANES)
    first, second = first_ref[:, place], second_ref[:, place]
    return jnp.where(parity, second, first), jnp.where(parity, first, second)


def unpacked(column, west, east, step):
    return jnp.where(
        column >= SIDE // 2, roll(west, SPACE_HALF * step), roll(east, -SPACE_HALF * step)
    )


def corner_kernel(place_ref, top_ref, bottom_ref, first_ref, second_ref, one_ref, two_ref):
    me = place_ref[0]
    lane, _ = iotas(first_ref.shape[0])
    column = jnp.bitwise_and(lane, SIDE - 1)
    parity = jnp.bitwise_and(me, 1) == 0
    upper = jnp.bitwise_and(me // REACH, 1) == 0
    count = top_ref.shape[0]
    groups = SIDE // SPACE_HALF
    last = first_ref.shape[1] // LANES - 1
    top, bottom = top_ref[...], bottom_ref[...]
    one_ref[:count] = jnp.where(upper, bottom, top)
    two_ref[:count] = jnp.where(upper, top, bottom)
    for half in range(STRIP // LANES):
        place = slice(half * LANES, (half + 1) * LANES)
        north = unpacked(column, *west_east(parity, first_ref, second_ref, 0), half)
        south = unpacked(
            column,
            *west_east(parity, first_ref, second_ref, last),
            groups - STRIP // LANES + half,
        )
        one_ref[count, :, place] = jnp.where(upper, south, north)
        two_ref[count, :, place] = jnp.where(upper, north, south)


def smooth_kernel(
    place_ref, mask_ref, taps_ref, nb_ref, mixed_ref, first_ref, second_ref, one_ref, two_ref,
    out_ref, side_ref,
):
    me = place_ref[0]
    count, slots, cells = mixed_ref.shape
    lane, sublane = iotas(slots)
    column = jnp.bitwise_and(lane, SIDE - 1)
    rightmost = column >= SIDE // 2
    low_half = lane < SIDE
    parity = jnp.bitwise_and(me, 1) == 0
    upper = jnp.bitwise_and(me // REACH, 1) == 0
    live = live_vector(mask_ref, sublane)
    across_taps = [taps_ref[0, lag] for lag in range(SPACE_HALF + 1)]
    down_taps = [taps_ref[1, lag] for lag in range(SPACE_HALF + 1)]
    crossing_west = [column >= SIDE - k for k in range(SPACE_HALF + 1)]
    crossing_east = [column < k for k in range(SPACE_HALF + 1)]
    nb = nb_ref[...]
    groups = SIDE // SPACE_HALF
    tiles = cells // LANES
    rows = STRIP // LANES

    def sides(west, east, device):
        target = jnp.where(rightmost, entry(nb, west, lane.shape), entry(nb, east, lane.shape))
        near = on_device(target, device, slots)
        return jnp.bitwise_and(target, slots - 1), near, (target >= 0) & ~near

    beside = sides(WEST, EAST, me)
    beside_north = sides(NORTH_WEST, NORTH_EAST, me - REACH)
    beside_south = sides(SOUTH_WEST, SOUTH_EAST, me + REACH)
    north_entry = entry(nb, NORTH, lane.shape)
    south_entry = entry(nb, SOUTH, lane.shape)

    for tile in range(tiles // groups):
        west, east = west_east(parity, first_ref, second_ref, tile)
        for step in range(groups):
            start = (tile * groups + step) * LANES
            side_ref[:, start : start + LANES] = unpacked(column, west, east, step)

    def across(centre, source, far, plan):
        index, near, remote = plan
        halo = jnp.where(near, pick(source, index), 0.0)
        halo = jnp.where(remote, far, halo)
        halo = roll(halo, SIDE)
        total = across_taps[0] * centre
        for k in range(1, SPACE_HALF + 1):
            left = roll(jnp.where(crossing_west[k], halo, centre), k)
            right = roll(jnp.where(crossing_east[k], halo, centre), -k)
            total = total + across_taps[k] * (left + right)
        return total

    def body(item, _):
        lines, odd = [], []
        item_row = jnp.full(lane.shape, item, jnp.int32)

        def fetch(position):
            if rows <= position < rows + tiles:
                start = (position - rows) * LANES
                centre = mixed_ref[item, :, start : start + LANES]
                far = pick(side_ref[:, start : start + LANES], item_row)
                return across(centre, centre, far, beside)
            north = position < rows
            start = (position if north else position - rows - tiles) * LANES
            place = slice(start, start + LANES)
            one, two = one_ref[item, :, place], two_ref[item, :, place]
            far_one, far_two = one_ref[count, :, place], two_ref[count, :, place]
            flag = jnp.logical_not(upper) if north else upper
            source = jnp.where(flag, one, two)
            far = pick(jnp.where(flag, far_one, far_two), item_row)
            target = north_entry if north else south_entry
            centre = jnp.where(
                target >= 0, pick(source, jnp.bitwise_and(target, slots - 1)), 0.0
            )
            return across(centre, source, far, beside_north if north else beside_south)

        for position in range(tiles + 2 * rows):
            lines.append(fetch(position))
            if position:
                odd.append(roll(jnp.where(low_half, lines[position], lines[position - 1]), SIDE))
            if position >= 2 * rows:
                p = position - 2 * rows
                total = down_taps[0] * lines[p + 2]
                total = total + down_taps[1] * (odd[p + 1] + odd[p + 2])
                total = total + down_taps[2] * (lines[p + 1] + lines[p + 3])
                total = total + down_taps[3] * (odd[p] + odd[p + 3])
                total = total + down_taps[4] * (lines[p] + lines[p + 4])
                out_ref[item, :, p * LANES : (p + 1) * LANES] = live * total
        return 0

    lax.fori_loop(0, count, body, 0)


def exchange(first, second, pairs_first, pairs_second):
    return lax.ppermute(first, "blk", pairs_first), lax.ppermute(second, "blk", pairs_second)


def both_ways(pairs):
    return [pair for a, b in pairs for pair in ((a, b), (b, a))]


def shards(input_field, active_mask, neighbours, time_taps, space_taps, coregion_factor):
    comps, days, slots, cells = input_field.shape
    count = comps * days
    blk = lax.axis_size("blk")
    day = lax.axis_size("day")
    place = jnp.stack([lax.axis_index("blk"), lax.axis_index("day")]).astype(jnp.int32)
    pair = day == 2
    if pair:
        others = [lax.ppermute(input_field, "day", [(0, 1), (1, 0)])]
    else:
        up = [(i, i + 1) for i in range(day - 1)]
        others = [
            lax.ppermute(input_field, "day", up),
            lax.ppermute(input_field, "day", [(b, a) for a, b in up]),
        ]
    packed = jax.ShapeDtypeStruct((slots, STRIP), jnp.float32)
    whole = pl.BlockSpec(memory_space=pltpu.VMEM)
    mixed, first, second = pl.pallas_call(
        functools.partial(filter_kernel, pair),
        out_shape=(jax.ShapeDtypeStruct((count, slots, cells), jnp.float32), packed, packed),
        in_specs=[SMEM] * 4 + [whole] * (2 + len(others)),
        out_specs=(whole,) * 3,
        compiler_params=PARAMS,
        name="time_filter",
    )(place, active_mask, time_taps, coregion_factor, neighbours, input_field, *others)

    columns = range(blk)
    even = both_ways([(i, i + 1) for i in columns if i % 2 == 0])
    odd = both_ways([(i, i + 1) for i in columns if i % 2 == 1 and i % REACH != REACH - 1])
    first, second = exchange(first, second, even, odd)

    strip_spec = lambda at: pl.BlockSpec((count, slots, STRIP), lambda i: (0, 0, at))
    upright = jax.ShapeDtypeStruct((count + 1, slots, STRIP), jnp.float32)
    one, two = pl.pallas_call(
        corner_kernel,
        grid=(1,),
        out_shape=(upright, upright),
        in_specs=[SMEM, strip_spec(0), strip_spec(cells // STRIP - 1), whole, whole],
        out_specs=(whole, whole),
        compiler_params=PARAMS,
        name="corners",
    )(place, mixed, mixed, first, second)

    rows = blk // REACH
    upper = [(i, i + REACH) for i in columns if i // REACH % 2 == 0 and i // REACH + 1 < rows]
    lower = [(i, i + REACH) for i in columns if i // REACH % 2 == 1 and i // REACH + 1 < rows]
    one, two = exchange(one, two, both_ways(upper), both_ways(lower))

    result = pl.pallas_call(
        smooth_kernel,
        out_shape=jax.ShapeDtypeStruct((count, slots, cells), jnp.float32),
        in_specs=[SMEM] * 3 + [whole] * 6,
        out_specs=whole,
        scratch_shapes=[pltpu.VMEM((slots, cells), jnp.float32)],
        compiler_params=PARAMS,
        name="spatial_filter",
    )(place, active_mask, space_taps, neighbours, mixed, first, second, one, two)
    return result.reshape(input_field.shape)


def solution(mesh):
    in_specs = (P(None, "day", "blk", None), P("blk"), P("blk", None), P(), P(), P())
    out_specs = P(None, "day", "blk", None)
    return jax.shard_map(shards, mesh=mesh, in_specs=in_specs, out_specs=out_specs, check_vma=False)
```

```python
import functools

import jax
import jax.numpy as jnp
from jax import lax
from jax.experimental import pallas as pl
from jax.experimental.pallas import tpu as pltpu
from jax.sharding import PartitionSpec as P

SIDE = 64
SPACE_HALF = 4
TIME_HALF = 3
REACH = 4
LANES = 128
EAST, WEST, NORTH, SOUTH, NORTH_EAST, NORTH_WEST, SOUTH_EAST, SOUTH_WEST = range(8)
STRIP = SPACE_HALF * SIDE
PARAMS = pltpu.CompilerParams(vmem_limit_bytes=12 * 1024 * 1024)
SMEM = pl.BlockSpec(memory_space=pltpu.SMEM)


def iotas(slots):
    lane = lax.broadcasted_iota(jnp.int32, (slots, LANES), 1)
    sublane = lax.broadcasted_iota(jnp.int32, (slots, LANES), 0)
    return lane, sublane


def live_vector(mask_ref, sublane):
    live = jnp.zeros(sublane.shape, jnp.float32)
    for slot in range(sublane.shape[0]):
        live = jnp.where(sublane == slot, mask_ref[slot].astype(jnp.float32), live)
    return live


def entry(neighbours, direction, shape):
    return jnp.broadcast_to(neighbours[:, direction : direction + 1], shape)


def pick(source, index):
    return jnp.take_along_axis(source, index, axis=0)


def roll(x, shift):
    return pltpu.roll(x, shift % LANES if isinstance(shift, int) else shift, 1)


def on_device(target, device, slots):
    return (target >= 0) & (target // slots == device)


def filter_kernel(pair, place_ref, mask_ref, taps_ref, factor_ref, nb_ref, x_ref, *rest):
    *other_refs, mixed_ref, first_ref, second_ref = rest
    slots, cells = mixed_ref.shape[1:]
    days = x_ref.shape[1]
    me, day = place_ref[0], place_ref[1]
    lane, sublane = iotas(slots)
    column = jnp.bitwise_and(lane, SIDE - 1)
    live = live_vector(mask_ref, sublane)
    taps = [taps_ref[lag] for lag in range(TIME_HALF + 1)]
    weights = [
        [
            live * (factor_ref[a, 0] * factor_ref[b, 0] + factor_ref[a, 1] * factor_ref[b, 1])
            for b in range(2)
        ]
        for a in range(2)
    ]
    nb = nb_ref[...]

    def end_slot(directions, devices):
        hit = None
        for direction, device in zip(directions, devices):
            one = on_device(entry(nb, direction, lane.shape), device, slots)
            hit = one if hit is None else hit | one
        return jnp.max(jnp.where(hit, sublane, 0), axis=0, keepdims=True)

    east_end = end_slot((EAST, NORTH_EAST, SOUTH_EAST), (me + 1, me + 1 - REACH, me + 1 + REACH))
    west_end = end_slot((WEST, NORTH_WEST, SOUTH_WEST), (me - 1, me - 1 - REACH, me - 1 + REACH))
    end_index = jnp.where(
        column >= SIDE // 2,
        jnp.broadcast_to(east_end, lane.shape),
        jnp.broadcast_to(west_end, lane.shape),
    )
    order = [day * (days - 1 - 2 * s) + s if pair else s for s in range(days)]
    group = column // SPACE_HALF
    groups = SIDE // SPACE_HALF
    is_row = [sublane == a * days + order[t] for a in range(2) for t in range(days)]

    def part(tile, step):
        filtered = []
        where = pl.ds(pl.multiple_of((tile * groups + step) * LANES, LANES), LANES)
        for comp in range(2):
            own = [x_ref[comp, order[s], :, where] for s in range(days)]
            totals = []
            for t in range(days):
                total = taps[0] * own[t]
                for s in range(days):
                    if s != t:
                        total = total + taps[abs(s - t)] * own[s]
                totals.append(total)
            later = [other_refs[-1][comp, order[s], :, where] for s in range(days)]
            for t in range(days):
                for s in range(t + 1):
                    totals[t] = totals[t] + taps[days + s - t] * later[s]
            if not pair:
                earlier = [other_refs[0][comp, s, :, where] for s in range(days)]
                for t in range(days):
                    for s in range(t, days):
                        totals[t] = totals[t] + taps[days + t - s] * earlier[s]
            filtered.append(totals)
        edge = jnp.zeros(lane.shape, jnp.float32)
        for a in range(2):
            for t in range(days):
                value = weights[a][0] * filtered[0][t] + weights[a][1] * filtered[1][t]
                mixed_ref[a * days + order[t], :, where] = value
                edge = jnp.where(is_row[a * days + t], pick(value, end_index), edge)
        return edge

    parity = jnp.bitwise_and(me, 1) == 0
    for tile in range(cells // (groups * LANES)):

        def body(step, held):
            east, west = held
            edge = part(tile, step)
            back = jnp.bitwise_and(LANES - SPACE_HALF * step, LANES - 1)
            east = jnp.where(group == groups - 1 - step, roll(edge, back), east)
            west = jnp.where(group == step, roll(edge, SPACE_HALF * step), west)
            return east, west

        zero = jnp.zeros(lane.shape, jnp.float32)
        east, west = lax.fori_loop(0, groups, body, (zero, zero))
        place = slice(tile * LANES, (tile + 1) * LANES)
        first_ref[:, place] = jnp.where(parity, east, west)
        second_ref[:, place] = jnp.where(parity, west, east)


def west_east(parity, first_ref, second_ref, tile):
    place = slice(tile * LANES, (tile + 1) * LANES)
    first, second = first_ref[:, place], second_ref[:, place]
    return jnp.where(parity, second, first), jnp.where(parity, first, second)


def unpacked(column, west, east, step):
    return jnp.where(
        column >= SIDE // 2, roll(west, SPACE_HALF * step), roll(east, -SPACE_HALF * step)
    )


def corner_kernel(place_ref, top_ref, bottom_ref, first_ref, second_ref, one_ref, two_ref):
    me = place_ref[0]
    lane, _ = iotas(first_ref.shape[0])
    column = jnp.bitwise_and(lane, SIDE - 1)
    parity = jnp.bitwise_and(me, 1) == 0
    upper = jnp.bitwise_and(me // REACH, 1) == 0
    count = top_ref.shape[0]
    groups = SIDE // SPACE_HALF
    last = first_ref.shape[1] // LANES - 1
    top, bottom = top_ref[...], bottom_ref[...]
    one_ref[:count] = jnp.where(upper, bottom, top)
    two_ref[:count] = jnp.where(upper, top, bottom)
    for half in range(STRIP // LANES):
        place = slice(half * LANES, (half + 1) * LANES)
        north = unpacked(column, *west_east(parity, first_ref, second_ref, 0), half)
        south = unpacked(
            column,
            *west_east(parity, first_ref, second_ref, last),
            groups - STRIP // LANES + half,
        )
        one_ref[count, :, place] = jnp.where(upper, south, north)
        two_ref[count, :, place] = jnp.where(upper, north, south)


def bands_kernel(taps_ref, bands_ref):
    shape = (2 * LANES, LANES)
    source = lax.broadcasted_iota(jnp.int32, shape, 0)
    target = lax.broadcasted_iota(jnp.int32, shape, 1)
    same = jnp.bitwise_and(source // SIDE, 1) == target // SIDE
    source_column = jnp.bitwise_and(source, SIDE - 1)
    outside = jnp.where(source_column >= SIDE // 2, source_column - SIDE, source_column + SIDE)
    position = jnp.where(source < LANES, source_column, outside)
    distance = jnp.abs(position - jnp.bitwise_and(target, SIDE - 1))
    bands = jnp.zeros(shape, jnp.float32)
    for lag in range(SPACE_HALF + 1):
        bands = jnp.where(same & (distance == lag), taps_ref[0, lag], bands)
    coarse, fine = two_parts(bands)
    bands_ref[: 2 * LANES, :LANES] = coarse
    bands_ref[: 2 * LANES, LANES:] = fine
    bands_ref[2 * LANES :, :LANES] = coarse
    bands_ref[2 * LANES :, LANES:] = jnp.zeros_like(fine)


def two_parts(x):
    coarse = x.astype(jnp.bfloat16)
    return coarse, (x - coarse.astype(jnp.float32)).astype(jnp.bfloat16)


def smooth_kernel(
    place_ref, mask_ref, taps_ref, nb_ref, bands_ref, mixed_ref, first_ref, second_ref, one_ref, two_ref,
    out_ref, side_ref,
):
    me = place_ref[0]
    count, slots, cells = mixed_ref.shape
    lane, sublane = iotas(slots)
    column = jnp.bitwise_and(lane, SIDE - 1)
    rightmost = column >= SIDE // 2
    low_half = lane < SIDE
    parity = jnp.bitwise_and(me, 1) == 0
    upper = jnp.bitwise_and(me // REACH, 1) == 0
    live = live_vector(mask_ref, sublane)
    down_taps = [taps_ref[1, lag] for lag in range(SPACE_HALF + 1)]
    nb = nb_ref[...]
    groups = SIDE // SPACE_HALF
    tiles = cells // LANES
    rows = STRIP // LANES

    def sides(west, east, device):
        target = jnp.where(rightmost, entry(nb, west, lane.shape), entry(nb, east, lane.shape))
        near = on_device(target, device, slots)
        return jnp.bitwise_and(target, slots - 1), near, (target >= 0) & ~near

    beside = sides(WEST, EAST, me)
    beside_north = sides(NORTH_WEST, NORTH_EAST, me - REACH)
    beside_south = sides(SOUTH_WEST, SOUTH_EAST, me + REACH)
    north_entry = entry(nb, NORTH, lane.shape)
    south_entry = entry(nb, SOUTH, lane.shape)

    for tile in range(tiles // groups):
        west, east = west_east(parity, first_ref, second_ref, tile)
        for step in range(groups):
            side_ref[tile * groups + step] = unpacked(column, west, east, step)

    def with_halo(centre, source, far, plan):
        index, near, remote = plan
        halo = jnp.where(near, pick(source, index), 0.0)
        return centre, jnp.where(remote, far, halo)

    def body(item, _):
        odd = []
        item_row = jnp.full(lane.shape, item, jnp.int32)

        def fetch(position):
            if rows <= position < rows + tiles:
                start = (position - rows) * LANES
                centre = mixed_ref[item, :, start : start + LANES]
                far = jnp.broadcast_to(
                    side_ref[position - rows, pl.ds(item, 1)], lane.shape
                )
                return with_halo(centre, centre, far, beside)
            north = position < rows
            start = (position if north else position - rows - tiles) * LANES
            place = slice(start, start + LANES)
            one, two = one_ref[item, :, place], two_ref[item, :, place]
            far_one, far_two = one_ref[count, :, place], two_ref[count, :, place]
            flag = jnp.logical_not(upper) if north else upper
            source = jnp.where(flag, one, two)
            far = pick(jnp.where(flag, far_one, far_two), item_row)
            target = north_entry if north else south_entry
            centre = jnp.where(
                target >= 0, pick(source, jnp.bitwise_and(target, slots - 1)), 0.0
            )
            return with_halo(centre, source, far, beside_north if north else beside_south)

        fetched = [fetch(position) for position in range(tiles + 2 * rows)]
        centre_parts = two_parts(jnp.concatenate([centre for centre, _ in fetched], axis=0))
        halo_parts = two_parts(jnp.concatenate([halo for _, halo in fetched], axis=0))
        across = jnp.dot(
            jnp.concatenate(
                [part for both in zip(centre_parts, halo_parts) for part in both], axis=1
            ),
            bands_ref[...],
            preferred_element_type=jnp.float32,
        )
        across = across[:, :LANES] + across[:, LANES:]
        lines = [across[slots * p : slots * (p + 1)] for p in range(tiles + 2 * rows)]
        for position in range(tiles + 2 * rows):
            if position:
                odd.append(roll(jnp.where(low_half, lines[position], lines[position - 1]), SIDE))
            if position >= 2 * rows:
                p = position - 2 * rows
                total = down_taps[0] * lines[p + 2]
                total = total + down_taps[1] * (odd[p + 1] + odd[p + 2])
                total = total + down_taps[2] * (lines[p + 1] + lines[p + 3])
                total = total + down_taps[3] * (odd[p] + odd[p + 3])
                total = total + down_taps[4] * (lines[p] + lines[p + 4])
                out_ref[item, :, p * LANES : (p + 1) * LANES] = live * total
        return 0

    lax.fori_loop(0, count, body, 0)


def exchange(first, second, pairs_first, pairs_second):
    return lax.ppermute(first, "blk", pairs_first), lax.ppermute(second, "blk", pairs_second)


def both_ways(pairs):
    return [pair for a, b in pairs for pair in ((a, b), (b, a))]


def shards(input_field, active_mask, neighbours, time_taps, space_taps, coregion_factor):
    comps, days, slots, cells = input_field.shape
    count = comps * days
    blk = lax.axis_size("blk")
    day = lax.axis_size("day")
    place = jnp.stack([lax.axis_index("blk"), lax.axis_index("day")]).astype(jnp.int32)
    pair = day == 2
    if pair:
        others = [lax.ppermute(input_field, "day", [(0, 1), (1, 0)])]
    else:
        up = [(i, i + 1) for i in range(day - 1)]
        others = [
            lax.ppermute(input_field, "day", up),
            lax.ppermute(input_field, "day", [(b, a) for a, b in up]),
        ]
    packed = jax.ShapeDtypeStruct((slots, STRIP), jnp.float32)
    whole = pl.BlockSpec(memory_space=pltpu.VMEM)
    mixed, first, second = pl.pallas_call(
        functools.partial(filter_kernel, pair),
        out_shape=(jax.ShapeDtypeStruct((count, slots, cells), jnp.float32), packed, packed),
        in_specs=[SMEM] * 4 + [whole] * (2 + len(others)),
        out_specs=(whole,) * 3,
        compiler_params=PARAMS,
        name="time_filter",
    )(place, active_mask, time_taps, coregion_factor, neighbours, input_field, *others)

    columns = range(blk)
    even = both_ways([(i, i + 1) for i in columns if i % 2 == 0])
    odd = both_ways([(i, i + 1) for i in columns if i % 2 == 1 and i % REACH != REACH - 1])
    first, second = exchange(first, second, even, odd)

    strip_spec = lambda at: pl.BlockSpec((count, slots, STRIP), lambda i: (0, 0, at))
    upright = jax.ShapeDtypeStruct((count + 1, slots, STRIP), jnp.float32)
    one, two = pl.pallas_call(
        corner_kernel,
        grid=(1,),
        out_shape=(upright, upright),
        in_specs=[SMEM, strip_spec(0), strip_spec(cells // STRIP - 1), whole, whole],
        out_specs=(whole, whole),
        compiler_params=PARAMS,
        name="corners",
    )(place, mixed, mixed, first, second)

    rows = blk // REACH
    upper = [(i, i + REACH) for i in columns if i // REACH % 2 == 0 and i // REACH + 1 < rows]
    lower = [(i, i + REACH) for i in columns if i // REACH % 2 == 1 and i // REACH + 1 < rows]
    one, two = exchange(one, two, both_ways(upper), both_ways(lower))

    bands = pl.pallas_call(
        bands_kernel,
        out_shape=jax.ShapeDtypeStruct((4 * LANES, 2 * LANES), jnp.bfloat16),
        in_specs=[SMEM],
        out_specs=whole,
        compiler_params=PARAMS,
        name="bands",
    )(space_taps)
    result = pl.pallas_call(
        smooth_kernel,
        out_shape=jax.ShapeDtypeStruct((count, slots, cells), jnp.float32),
        in_specs=[SMEM] * 3 + [whole] * 7,
        out_specs=whole,
        scratch_shapes=[pltpu.VMEM((cells // LANES, slots, LANES), jnp.float32)],
        compiler_params=PARAMS,
        name="spatial_filter",
    )(place, active_mask, space_taps, neighbours, bands, mixed, first, second, one, two)
    return result.reshape(input_field.shape)


def solution(mesh):
    in_specs = (P(None, "day", "blk", None), P("blk"), P("blk", None), P(), P(), P())
    out_specs = P(None, "day", "blk", None)
    return jax.shard_map(shards, mesh=mesh, in_specs=in_specs, out_specs=out_specs, check_vma=False)
```

```python
import functools

import jax
import jax.numpy as jnp
from jax import lax
from jax.experimental import pallas as pl
from jax.experimental.pallas import tpu as pltpu
from jax.sharding import PartitionSpec as P

SIDE = 64
SPACE_HALF = 4
TIME_HALF = 3
REACH = 4
LANES = 128
EAST, WEST, NORTH, SOUTH, NORTH_EAST, NORTH_WEST, SOUTH_EAST, SOUTH_WEST = range(8)
STRIP = SPACE_HALF * SIDE
PARAMS = pltpu.CompilerParams(vmem_limit_bytes=12 * 1024 * 1024)
SMEM = pl.BlockSpec(memory_space=pltpu.SMEM)


def iotas(slots):
    lane = lax.broadcasted_iota(jnp.int32, (slots, LANES), 1)
    sublane = lax.broadcasted_iota(jnp.int32, (slots, LANES), 0)
    return lane, sublane


def live_vector(mask_ref, sublane):
    live = jnp.zeros(sublane.shape, jnp.float32)
    for slot in range(sublane.shape[0]):
        live = jnp.where(sublane == slot, mask_ref[slot].astype(jnp.float32), live)
    return live


def entry(neighbours, direction, shape):
    return jnp.broadcast_to(neighbours[:, direction : direction + 1], shape)


def pick(source, index):
    return jnp.take_along_axis(source, index, axis=0)


def roll(x, shift):
    return pltpu.roll(x, shift % LANES if isinstance(shift, int) else shift, 1)


def on_device(target, device, slots):
    return (target >= 0) & (target // slots == device)


def order_of(pair, day, days):
    return [day * (days - 1 - 2 * s) + s if pair else s for s in range(days)]


def coupling_of(factor_ref):
    return [
        [
            factor_ref[a, 0] * factor_ref[b, 0] + factor_ref[a, 1] * factor_ref[b, 1]
            for b in range(2)
        ]
        for a in range(2)
    ]


def same_days(taps, values):
    totals = []
    for t in range(len(values)):
        total = taps[0] * values[t]
        for s in range(len(values)):
            if s != t:
                total = total + taps[abs(s - t)] * values[s]
        totals.append(total)
    return totals


def add_later(taps, totals, values):
    for t in range(len(totals)):
        for s in range(t + 1):
            totals[t] = totals[t] + taps[len(totals) + s - t] * values[s]


def add_earlier(taps, totals, values):
    for t in range(len(totals)):
        for s in range(t, len(totals)):
            totals[t] = totals[t] + taps[len(totals) + t - s] * values[s]


def own_kernel(place_ref, mask_ref, taps_ref, nb_ref, x_ref, own_ref, edge_ref):
    comps, days, slots, chunk = x_ref.shape
    step = pl.program_id(0)
    me = place_ref[0]
    lane, sublane = iotas(slots)
    column = jnp.bitwise_and(lane, SIDE - 1)
    live = live_vector(mask_ref, sublane)
    taps = [taps_ref[lag] for lag in range(TIME_HALF + 1)]
    nb = nb_ref[...]

    def end_slot(directions, devices):
        hit = None
        for direction, device in zip(directions, devices):
            one = on_device(entry(nb, direction, lane.shape), device, slots)
            hit = one if hit is None else hit | one
        return jnp.max(jnp.where(hit, sublane, 0), axis=0, keepdims=True)

    east_end = end_slot((EAST, NORTH_EAST, SOUTH_EAST), (me + 1, me + 1 - REACH, me + 1 + REACH))
    west_end = end_slot((WEST, NORTH_WEST, SOUTH_WEST), (me - 1, me - 1 - REACH, me - 1 + REACH))
    end_index = jnp.where(
        column >= SIDE // 2,
        jnp.broadcast_to(east_end, lane.shape),
        jnp.broadcast_to(west_end, lane.shape),
    )
    group = column // SPACE_HALF
    groups = SIDE // SPACE_HALF
    is_row = [sublane == row for row in range(comps * days)]
    per_step = chunk // LANES
    first = jnp.bitwise_and(step * per_step, groups - 1)
    place = pl.ds(pl.multiple_of(step * per_step // groups * LANES, LANES), LANES)

    @pl.when(first == 0)
    def _():
        edge_ref[0, :, place] = jnp.zeros(lane.shape, jnp.float32)
        edge_ref[1, :, place] = jnp.zeros(lane.shape, jnp.float32)

    east, west = edge_ref[0, :, place], edge_ref[1, :, place]
    for tile in range(per_step):
        where = slice(tile * LANES, (tile + 1) * LANES)
        edge = jnp.zeros(lane.shape, jnp.float32)
        for comp in range(comps):
            values = [live * x_ref[comp, t, :, where] for t in range(days)]
            for t, total in enumerate(same_days(taps, values)):
                own_ref[comp * days + t, :, where] = total
            for t in range(days):
                edge = jnp.where(is_row[comp * days + t], pick(values[t], end_index), edge)
        at = first + tile
        east = jnp.where(
            group == groups - 1 - at,
            roll(edge, jnp.bitwise_and(LANES - SPACE_HALF * at, LANES - 1)),
            east,
        )
        west = jnp.where(group == at, roll(edge, SPACE_HALF * at), west)
    edge_ref[0, :, place] = east
    edge_ref[1, :, place] = west


def strip_kernel(pair, place_ref, mask_ref, taps_ref, factor_ref, *refs):
    count = 1 if pair else 2
    out_refs = refs[len(refs) - count :]
    inputs = refs[: len(refs) - count]
    per_side = len(inputs) // count
    comps, days, slots, _ = inputs[0].shape
    _, sublane = iotas(slots)
    live = live_vector(mask_ref, sublane)[:, :1]
    taps = [taps_ref[lag] for lag in range(TIME_HALF + 1)]
    coupling = coupling_of(factor_ref)
    order = order_of(pair, place_ref[1], days)
    for side in range(count):
        x_ref, *other_refs = inputs[side * per_side : (side + 1) * per_side]
        mine, theirs = [], []
        for comp in range(comps):
            values = [x_ref[comp, order[s]] for s in range(days)]
            later = [other_refs[-1][comp, order[s]] for s in range(days)]
            totals = same_days(taps, values)
            add_later(taps, totals, later)
            if pair:
                others = same_days(taps, later)
                add_earlier(taps, others, values)
                theirs.append(others)
            else:
                add_earlier(taps, totals, [other_refs[0][comp, s] for s in range(days)])
            mine.append(totals)
        for base, filtered in enumerate([mine, theirs] if pair else [mine]):
            for a in range(comps):
                for t in range(days):
                    value = coupling[a][0] * filtered[0][t] + coupling[a][1] * filtered[1][t]
                    at = base * comps * days + a * days + order[t]
                    out_refs[side][at] = live * value


def mix_kernel(pair, place_ref, mask_ref, taps_ref, factor_ref, own_ref, *rest):
    *other_refs, mixed_ref = rest
    slots, chunk = mixed_ref.shape[1:]
    comps, days = other_refs[0].shape[:2]
    _, sublane = iotas(slots)
    live = live_vector(mask_ref, sublane)
    taps = [taps_ref[lag] for lag in range(TIME_HALF + 1)]
    coupling = coupling_of(factor_ref)
    weights = [[live * value for value in row] for row in coupling]
    order = order_of(pair, place_ref[1], days)

    def body(tile, _):
        where = pl.ds(pl.multiple_of(tile * LANES, LANES), LANES)
        filtered = []
        for comp in range(comps):
            totals = [own_ref[comp * days + order[t], :, where] for t in range(days)]
            add_later(taps, totals, [other_refs[-1][comp, order[s], :, where] for s in range(days)])
            if not pair:
                add_earlier(taps, totals, [other_refs[0][comp, s, :, where] for s in range(days)])
            filtered.append(totals)
        for a in range(comps):
            for t in range(days):
                mixed_ref[a * days + order[t], :, where] = (
                    weights[a][0] * filtered[0][t] + weights[a][1] * filtered[1][t]
                )
        return 0

    lax.fori_loop(0, chunk // LANES, body, 0, unroll=4)


def unpacked(column, west, east, step):
    return jnp.where(
        column >= SIDE // 2, roll(west, SPACE_HALF * step), roll(east, -SPACE_HALF * step)
    )


def halo_kernel(days, last_day, place_ref, taps_ref, factor_ref, *refs):
    *pieces, side_ref, corner_ref = refs
    day = place_ref[1]
    slots = side_ref.shape[1]
    lane, _ = iotas(slots)
    column = jnp.bitwise_and(lane, SIDE - 1)
    groups = SIDE // SPACE_HALF
    coupling = coupling_of(factor_ref)
    shape = (slots, 3 * slots)
    row = lax.broadcasted_iota(jnp.int32, shape, 0)
    source = lax.broadcasted_iota(jnp.int32, shape, 1)
    block, inner = source // slots, jnp.bitwise_and(source, slots - 1)
    out_comp = (row >= days).astype(jnp.int32)
    in_comp = (inner >= days).astype(jnp.int32)
    lag = jnp.abs(row - out_comp * days - (inner - in_comp * days) - (block - 1) * days)
    tap = jnp.zeros(shape, jnp.float32)
    for k in range(TIME_HALF + 1):
        tap = jnp.where(lag == k, taps_ref[k], tap)
    weight = jnp.zeros(shape, jnp.float32)
    for a in range(2):
        for b in range(2):
            weight = jnp.where((out_comp == a) & (in_comp == b), coupling[a][b], weight)
    known = (inner < 2 * days) & (row < 2 * days)
    known = known & ((block != 0) | (day > 0)) & ((block != 2) | (day < last_day))
    matrix = jnp.where(known, tap * weight, 0.0)
    raw = jnp.concatenate(
        [
            jnp.concatenate([pieces[3 * k + j][0, 0] for j in range(3)], axis=0)
            for k in range(len(pieces) // 3)
        ],
        axis=1,
    )
    filtered = jnp.dot(
        matrix, raw, preferred_element_type=jnp.float32, precision=lax.Precision.HIGHEST
    )
    tiles = [filtered[:, k * LANES : (k + 1) * LANES] for k in range(filtered.shape[1] // LANES)]
    per_side = side_ref.shape[0] // groups
    for tile in range(per_side):
        for step in range(groups):
            side_ref[tile * groups + step] = unpacked(
                column, tiles[tile], tiles[per_side + tile], step
            )
    north_west, north_east, south_west, south_east = tiles[2 * per_side :]
    rows = STRIP // LANES
    for half in range(rows):
        corner_ref[half] = unpacked(column, north_west, north_east, groups - rows + half)
        corner_ref[rows + half] = unpacked(column, south_west, south_east, half)


def bands_kernel(taps_ref, bands_ref):
    shape = (2 * LANES, LANES)
    source = lax.broadcasted_iota(jnp.int32, shape, 0)
    target = lax.broadcasted_iota(jnp.int32, shape, 1)
    same = jnp.bitwise_and(source // SIDE, 1) == target // SIDE
    source_column = jnp.bitwise_and(source, SIDE - 1)
    outside = jnp.where(source_column >= SIDE // 2, source_column - SIDE, source_column + SIDE)
    position = jnp.where(source < LANES, source_column, outside)
    distance = jnp.abs(position - jnp.bitwise_and(target, SIDE - 1))
    bands = jnp.zeros(shape, jnp.float32)
    for lag in range(SPACE_HALF + 1):
        bands = jnp.where(same & (distance == lag), taps_ref[0, lag], bands)
    coarse, fine = two_parts(bands)
    bands_ref[: 2 * LANES, :LANES] = coarse
    bands_ref[: 2 * LANES, LANES:] = fine
    bands_ref[2 * LANES :, :LANES] = coarse
    bands_ref[2 * LANES :, LANES:] = jnp.zeros_like(fine)


def two_parts(x):
    coarse = x.astype(jnp.bfloat16)
    return coarse, (x - coarse.astype(jnp.float32)).astype(jnp.bfloat16)


def smooth_kernel(
    pair, place_ref, mask_ref, taps_ref, nb_ref, bands_ref, mixed_ref, side_ref, corner_ref, one_ref,
    two_ref, out_ref,
):
    me = place_ref[0]
    count, slots, cells = mixed_ref.shape
    lane, sublane = iotas(slots)
    column = jnp.bitwise_and(lane, SIDE - 1)
    rightmost = column >= SIDE // 2
    low_half = lane < SIDE
    swapped = (place_ref[1] != 0) if pair else False
    live = live_vector(mask_ref, sublane)
    down_taps = [taps_ref[1, lag] for lag in range(SPACE_HALF + 1)]
    nb = nb_ref[...]
    tiles = cells // LANES
    rows = STRIP // LANES

    def sides(west, east, device):
        target = jnp.where(rightmost, entry(nb, west, lane.shape), entry(nb, east, lane.shape))
        near = on_device(target, device, slots)
        return jnp.bitwise_and(target, slots - 1), near, (target >= 0) & ~near

    beside = sides(WEST, EAST, me)
    beside_north = sides(NORTH_WEST, NORTH_EAST, me - REACH)
    beside_south = sides(SOUTH_WEST, SOUTH_EAST, me + REACH)
    north_entry = entry(nb, NORTH, lane.shape)
    south_entry = entry(nb, SOUTH, lane.shape)

    def with_halo(centre, source, far, plan):
        index, near, remote = plan
        halo = jnp.where(near, pick(source, index), 0.0)
        return centre, jnp.where(remote, far, halo)

    def body(item, _):
        odd = []

        def fetch(position):
            if rows <= position < rows + tiles:
                start = (position - rows) * LANES
                centre = mixed_ref[item, :, start : start + LANES]
                far = jnp.broadcast_to(
                    side_ref[position - rows, pl.ds(item, 1)], lane.shape
                )
                return with_halo(centre, centre, far, beside)
            north = position < rows
            start = (position if north else position - rows - tiles) * LANES
            place = slice(start, start + LANES)
            one, two = one_ref[item, :, place], two_ref[item, :, place]
            if pair:
                source = jnp.where(swapped if north else jnp.logical_not(swapped), two, one)
            else:
                source = one if north else two
            at = position if north else position - tiles
            far = jnp.broadcast_to(corner_ref[at, pl.ds(item, 1)], lane.shape)
            target = north_entry if north else south_entry
            centre = jnp.where(
                target >= 0, pick(source, jnp.bitwise_and(target, slots - 1)), 0.0
            )
            return with_halo(centre, source, far, beside_north if north else beside_south)

        fetched = [fetch(position) for position in range(tiles + 2 * rows)]
        centre_parts = two_parts(jnp.concatenate([centre for centre, _ in fetched], axis=0))
        halo_parts = two_parts(jnp.concatenate([halo for _, halo in fetched], axis=0))
        across = jnp.dot(
            jnp.concatenate(
                [part for both in zip(centre_parts, halo_parts) for part in both], axis=1
            ),
            bands_ref[...],
            preferred_element_type=jnp.float32,
        )
        across = across[:, :LANES] + across[:, LANES:]
        lines = [across[slots * p : slots * (p + 1)] for p in range(tiles + 2 * rows)]
        for position in range(tiles + 2 * rows):
            if position:
                odd.append(roll(jnp.where(low_half, lines[position], lines[position - 1]), SIDE))
            if position >= 2 * rows:
                p = position - 2 * rows
                total = down_taps[0] * lines[p + 2]
                total = total + down_taps[1] * (odd[p + 1] + odd[p + 2])
                total = total + down_taps[2] * (lines[p + 1] + lines[p + 3])
                total = total + down_taps[3] * (odd[p] + odd[p + 3])
                total = total + down_taps[4] * (lines[p] + lines[p + 4])
                out_ref[item, :, p * LANES : (p + 1) * LANES] = live * total
        return 0

    lax.fori_loop(0, count, body, 0)


def shards(input_field, active_mask, neighbours, time_taps, space_taps, coregion_factor):
    comps, days, slots, cells = input_field.shape
    count = comps * days
    blk = lax.axis_size("blk")
    day = lax.axis_size("day")
    place = jnp.stack([lax.axis_index("blk"), lax.axis_index("day")]).astype(jnp.int32)
    pair = day == 2
    if pair:
        others = [lax.ppermute(input_field, "day", [(0, 1), (1, 0)])]
    else:
        up = [(i, i + 1) for i in range(day - 1)]
        others = [
            lax.ppermute(input_field, "day", up),
            lax.ppermute(input_field, "day", [(b, a) for a, b in up]),
        ]
    whole = pl.BlockSpec(memory_space=pltpu.VMEM)

    chunk = min(cells, 8 * LANES)
    own, edges = pl.pallas_call(
        own_kernel,
        grid=(cells // chunk,),
        out_shape=(
            jax.ShapeDtypeStruct((count, slots, cells), jnp.float32),
            jax.ShapeDtypeStruct((2, slots, STRIP), jnp.float32),
        ),
        in_specs=[SMEM] * 3
        + [
            pl.BlockSpec(neighbours.shape, lambda i: (0, 0)),
            pl.BlockSpec((comps, days, slots, chunk), lambda i: (0, 0, 0, i)),
        ],
        out_specs=(
            pl.BlockSpec((count, slots, chunk), lambda i: (0, 0, i)),
            pl.BlockSpec((2, slots, STRIP), lambda i: (0, 0, 0)),
        ),
        compiler_params=PARAMS,
        name="own_days",
    )(place, active_mask, time_taps, neighbours, input_field)
    gathered = lax.all_gather(edges, ("blk", "day"))

    bands = pl.pallas_call(
        bands_kernel,
        out_shape=jax.ShapeDtypeStruct((4 * LANES, 2 * LANES), jnp.bfloat16),
        in_specs=[SMEM],
        out_specs=whole,
        compiler_params=PARAMS,
        name="bands",
    )(space_taps)

    last = cells // STRIP - 1
    arrays = [input_field, *others]

    def strip_spec(at):
        return pl.BlockSpec(
            (comps, days, slots, STRIP), lambda i, place_ref: (0, 0, 0, at(place_ref))
        )

    if pair:
        sides = [strip_spec(lambda place_ref: (1 - place_ref[1]) * last)]
        strips = jax.ShapeDtypeStruct((2 * count, slots, STRIP), jnp.float32)
    else:
        sides = [strip_spec(lambda place_ref: last), strip_spec(lambda place_ref: 0)]
        strips = jax.ShapeDtypeStruct((count, slots, STRIP), jnp.float32)
    sent = pl.pallas_call(
        functools.partial(strip_kernel, pair),
        out_shape=(strips,) * len(sides),
        grid_spec=pltpu.PrefetchScalarGridSpec(
            num_scalar_prefetch=1,
            grid=(1,),
            in_specs=[SMEM] * 3 + [spec for spec in sides for _ in arrays],
            out_specs=(pl.BlockSpec(strips.shape, lambda i, place_ref: (0, 0, 0)),) * len(sides),
        ),
        compiler_params=PARAMS,
        name="strips",
    )(place, active_mask, time_taps, coregion_factor, *(arrays * len(sides)))
    south = [(i, i + REACH) for i in range(blk - REACH)]
    north = [(b, a) for a, b in south]
    if pair:
        both = [(2 * a, 2 * b) for a, b in south] + [(2 * a + 1, 2 * b + 1) for a, b in north]
        one = lax.ppermute(sent[0], ("blk", "day"), both)
        two = lax.ppermute(one[count:], "day", [(0, 1), (1, 0)])
    else:
        one = lax.ppermute(sent[0], "blk", south)
        two = lax.ppermute(sent[1], "blk", north)

    mixed = pl.pallas_call(
        functools.partial(mix_kernel, pair),
        out_shape=jax.ShapeDtypeStruct((count, slots, cells), jnp.float32),
        in_specs=[SMEM] * 4 + [whole] * (1 + len(others)),
        out_specs=whole,
        compiler_params=PARAMS,
        name="mix",
    )(place, active_mask, time_taps, coregion_factor, own, *others)

    def piece_specs(offset, side, width, at):
        def index(shift):
            def index_map(i, place_ref):
                device = jnp.clip(place_ref[0] + offset, 0, blk - 1)
                return device * day + jnp.clip(place_ref[1] + shift, 0, day - 1), side, 0, at

            return index_map

        return [pl.BlockSpec((1, 1, slots, width), index(shift)) for shift in (-1, 0, 1)]

    tail_tile = STRIP // LANES - 1
    pieces = (
        piece_specs(-1, 0, STRIP, 0)
        + piece_specs(1, 1, STRIP, 0)
        + piece_specs(-1 - REACH, 0, LANES, tail_tile)
        + piece_specs(1 - REACH, 1, LANES, tail_tile)
        + piece_specs(REACH - 1, 0, LANES, 0)
        + piece_specs(REACH + 1, 1, LANES, 0)
    )
    side_shape = (cells // LANES, slots, LANES)
    corner_shape = (2 * STRIP // LANES, slots, LANES)
    beside, corners = pl.pallas_call(
        functools.partial(halo_kernel, days, day - 1),
        out_shape=(
            jax.ShapeDtypeStruct(side_shape, jnp.float32),
            jax.ShapeDtypeStruct(corner_shape, jnp.float32),
        ),
        grid_spec=pltpu.PrefetchScalarGridSpec(
            num_scalar_prefetch=1,
            grid=(1,),
            in_specs=[SMEM] * 2 + pieces,
            out_specs=(
                pl.BlockSpec(side_shape, lambda i, place_ref: (0, 0, 0)),
                pl.BlockSpec(corner_shape, lambda i, place_ref: (0, 0, 0)),
            ),
        ),
        compiler_params=PARAMS,
        name="halos",
    )(place, time_taps, coregion_factor, *([gathered] * len(pieces)))

    result = pl.pallas_call(
        functools.partial(smooth_kernel, pair),
        out_shape=jax.ShapeDtypeStruct((count, slots, cells), jnp.float32),
        in_specs=[SMEM] * 3 + [whole] * 7,
        out_specs=whole,
        compiler_params=PARAMS,
        name="spatial_filter",
    )(place, active_mask, space_taps, neighbours, bands, mixed, beside, corners, one, two)
    return result.reshape(input_field.shape)


def solution(mesh):
    in_specs = (P(None, "day", "blk", None), P("blk"), P("blk", None), P(), P(), P())
    out_specs = P(None, "day", "blk", None)
    return jax.shard_map(shards, mesh=mesh, in_specs=in_specs, out_specs=out_specs, check_vma=False)
```

```python
import functools

import jax
import jax.numpy as jnp
from jax import lax
from jax.experimental import pallas as pl
from jax.experimental.pallas import tpu as pltpu
from jax.sharding import PartitionSpec as P

SIDE = 64
SPACE_HALF = 4
TIME_HALF = 3
REACH = 4
LANES = 128
EAST, WEST, NORTH, SOUTH, NORTH_EAST, NORTH_WEST, SOUTH_EAST, SOUTH_WEST = range(8)
STRIP = SPACE_HALF * SIDE
PARAMS = pltpu.CompilerParams(vmem_limit_bytes=12 * 1024 * 1024)
SMEM = pl.BlockSpec(memory_space=pltpu.SMEM)


def iotas(slots):
    lane = lax.broadcasted_iota(jnp.int32, (slots, LANES), 1)
    sublane = lax.broadcasted_iota(jnp.int32, (slots, LANES), 0)
    return lane, sublane


def live_vector(mask_ref, sublane):
    live = jnp.zeros(sublane.shape, jnp.float32)
    for slot in range(sublane.shape[0]):
        live = jnp.where(sublane == slot, mask_ref[slot].astype(jnp.float32), live)
    return live


def entry(neighbours, direction, shape):
    return jnp.broadcast_to(neighbours[:, direction : direction + 1], shape)


def pick(source, index):
    return jnp.take_along_axis(source, index, axis=0)


def roll(x, shift):
    return pltpu.roll(x, shift % LANES if isinstance(shift, int) else shift, 1)


def on_device(target, device, slots):
    return (target >= 0) & (target // slots == device)


def filter_kernel(pair, place_ref, mask_ref, taps_ref, factor_ref, nb_ref, x_ref, *rest):
    *other_refs, mixed_ref, first_ref, second_ref = rest
    slots, cells = mixed_ref.shape[1:]
    days = x_ref.shape[1]
    me, day = place_ref[0], place_ref[1]
    lane, sublane = iotas(slots)
    column = jnp.bitwise_and(lane, SIDE - 1)
    live = live_vector(mask_ref, sublane)
    taps = [taps_ref[lag] for lag in range(TIME_HALF + 1)]
    weights = [
        [
            live * (factor_ref[a, 0] * factor_ref[b, 0] + factor_ref[a, 1] * factor_ref[b, 1])
            for b in range(2)
        ]
        for a in range(2)
    ]
    nb = nb_ref[...]

    def end_slot(directions, devices):
        hit = None
        for direction, device in zip(directions, devices):
            one = on_device(entry(nb, direction, lane.shape), device, slots)
            hit = one if hit is None else hit | one
        return jnp.max(jnp.where(hit, sublane, 0), axis=0, keepdims=True)

    east_end = end_slot((EAST, NORTH_EAST, SOUTH_EAST), (me + 1, me + 1 - REACH, me + 1 + REACH))
    west_end = end_slot((WEST, NORTH_WEST, SOUTH_WEST), (me - 1, me - 1 - REACH, me - 1 + REACH))
    end_index = jnp.where(
        column >= SIDE // 2,
        jnp.broadcast_to(east_end, lane.shape),
        jnp.broadcast_to(west_end, lane.shape),
    )
    order = [day * (days - 1 - 2 * s) + s if pair else s for s in range(days)]
    group = column // SPACE_HALF
    groups = SIDE // SPACE_HALF
    is_row = [sublane == a * days + order[t] for a in range(2) for t in range(days)]

    def part(tile, step):
        filtered = []
        where = pl.ds(pl.multiple_of((tile * groups + step) * LANES, LANES), LANES)
        for comp in range(2):
            own = [x_ref[comp, order[s], :, where] for s in range(days)]
            totals = []
            for t in range(days):
                total = taps[0] * own[t]
                for s in range(days):
                    if s != t:
                        total = total + taps[abs(s - t)] * own[s]
                totals.append(total)
            later = [other_refs[-1][comp, order[s], :, where] for s in range(days)]
            for t in range(days):
                for s in range(t + 1):
                    totals[t] = totals[t] + taps[days + s - t] * later[s]
            if not pair:
                earlier = [other_refs[0][comp, s, :, where] for s in range(days)]
                for t in range(days):
                    for s in range(t, days):
                        totals[t] = totals[t] + taps[days + t - s] * earlier[s]
            filtered.append(totals)
        edge = jnp.zeros(lane.shape, jnp.float32)
        for a in range(2):
            for t in range(days):
                value = weights[a][0] * filtered[0][t] + weights[a][1] * filtered[1][t]
                mixed_ref[a * days + order[t], :, where] = value
                edge = jnp.where(is_row[a * days + t], pick(value, end_index), edge)
        return edge

    parity = jnp.bitwise_and(me, 1) == 0
    for tile in range(cells // (groups * LANES)):

        def body(step, held):
            east, west = held
            edge = part(tile, step)
            back = jnp.bitwise_and(LANES - SPACE_HALF * step, LANES - 1)
            east = jnp.where(group == groups - 1 - step, roll(edge, back), east)
            west = jnp.where(group == step, roll(edge, SPACE_HALF * step), west)
            return east, west

        zero = jnp.zeros(lane.shape, jnp.float32)
        east, west = lax.fori_loop(0, groups, body, (zero, zero))
        place = slice(tile * LANES, (tile + 1) * LANES)
        first_ref[:, place] = jnp.where(parity, east, west)
        second_ref[:, place] = jnp.where(parity, west, east)


def west_east(parity, first_ref, second_ref, tile):
    place = slice(tile * LANES, (tile + 1) * LANES)
    first, second = first_ref[:, place], second_ref[:, place]
    return jnp.where(parity, second, first), jnp.where(parity, first, second)


def unpacked(column, west, east, step):
    return jnp.where(
        column >= SIDE // 2, roll(west, SPACE_HALF * step), roll(east, -SPACE_HALF * step)
    )


def corner_kernel(place_ref, top_ref, bottom_ref, first_ref, second_ref, one_ref, two_ref):
    me = place_ref[0]
    lane, _ = iotas(first_ref.shape[0])
    column = jnp.bitwise_and(lane, SIDE - 1)
    parity = jnp.bitwise_and(me, 1) == 0
    upper = jnp.bitwise_and(me // REACH, 1) == 0
    count = top_ref.shape[0]
    groups = SIDE // SPACE_HALF
    last = first_ref.shape[1] // LANES - 1
    top, bottom = top_ref[...], bottom_ref[...]
    one_ref[:count] = jnp.where(upper, bottom, top)
    two_ref[:count] = jnp.where(upper, top, bottom)
    for half in range(STRIP // LANES):
        place = slice(half * LANES, (half + 1) * LANES)
        north = unpacked(column, *west_east(parity, first_ref, second_ref, 0), half)
        south = unpacked(
            column,
            *west_east(parity, first_ref, second_ref, last),
            groups - STRIP // LANES + half,
        )
        one_ref[count, :, place] = jnp.where(upper, south, north)
        two_ref[count, :, place] = jnp.where(upper, north, south)


def bands_kernel(taps_ref, bands_ref):
    shape = (2 * LANES, LANES)
    source = lax.broadcasted_iota(jnp.int32, shape, 0)
    target = lax.broadcasted_iota(jnp.int32, shape, 1)
    same = jnp.bitwise_and(source // SIDE, 1) == target // SIDE
    source_column = jnp.bitwise_and(source, SIDE - 1)
    outside = jnp.where(source_column >= SIDE // 2, source_column - SIDE, source_column + SIDE)
    position = jnp.where(source < LANES, source_column, outside)
    distance = jnp.abs(position - jnp.bitwise_and(target, SIDE - 1))
    bands = jnp.zeros(shape, jnp.float32)
    for lag in range(SPACE_HALF + 1):
        bands = jnp.where(same & (distance == lag), taps_ref[0, lag], bands)
    coarse, fine = two_parts(bands)
    bands_ref[: 2 * LANES, :LANES] = coarse
    bands_ref[: 2 * LANES, LANES:] = fine
    bands_ref[2 * LANES :, :LANES] = coarse
    bands_ref[2 * LANES :, LANES:] = jnp.zeros_like(fine)


def two_parts(x):
    coarse = x.astype(jnp.bfloat16)
    return coarse, (x - coarse.astype(jnp.float32)).astype(jnp.bfloat16)


def smooth_kernel(
    place_ref, mask_ref, taps_ref, nb_ref, bands_ref, mixed_ref, first_ref, second_ref, one_ref, two_ref,
    out_ref, side_ref,
):
    me = place_ref[0]
    count, slots, cells = mixed_ref.shape
    lane, sublane = iotas(slots)
    column = jnp.bitwise_and(lane, SIDE - 1)
    rightmost = column >= SIDE // 2
    low_half = lane < SIDE
    parity = jnp.bitwise_and(me, 1) == 0
    upper = jnp.bitwise_and(me // REACH, 1) == 0
    live = live_vector(mask_ref, sublane)
    down_taps = [taps_ref[1, lag] for lag in range(SPACE_HALF + 1)]
    nb = nb_ref[...]
    groups = SIDE // SPACE_HALF
    tiles = cells // LANES
    rows = STRIP // LANES

    def sides(west, east, device):
        target = jnp.where(rightmost, entry(nb, west, lane.shape), entry(nb, east, lane.shape))
        near = on_device(target, device, slots)
        return jnp.bitwise_and(target, slots - 1), near, (target >= 0) & ~near

    beside = sides(WEST, EAST, me)
    beside_north = sides(NORTH_WEST, NORTH_EAST, me - REACH)
    beside_south = sides(SOUTH_WEST, SOUTH_EAST, me + REACH)
    north_entry = entry(nb, NORTH, lane.shape)
    south_entry = entry(nb, SOUTH, lane.shape)

    for tile in range(tiles // groups):
        west, east = west_east(parity, first_ref, second_ref, tile)
        for step in range(groups):
            side_ref[tile * groups + step] = unpacked(column, west, east, step)

    def with_halo(centre, source, far, plan):
        index, near, remote = plan
        halo = jnp.where(near, pick(source, index), 0.0)
        return centre, jnp.where(remote, far, halo)

    def body(item, _):
        odd = []
        item_row = jnp.full(lane.shape, item, jnp.int32)

        def fetch(position):
            if rows <= position < rows + tiles:
                start = (position - rows) * LANES
                centre = mixed_ref[item, :, start : start + LANES]
                far = jnp.broadcast_to(
                    side_ref[position - rows, pl.ds(item, 1)], lane.shape
                )
                return with_halo(centre, centre, far, beside)
            north = position < rows
            start = (position if north else position - rows - tiles) * LANES
            place = slice(start, start + LANES)
            one, two = one_ref[item, :, place], two_ref[item, :, place]
            far_one, far_two = one_ref[count, :, place], two_ref[count, :, place]
            flag = jnp.logical_not(upper) if north else upper
            source = jnp.where(flag, one, two)
            far = pick(jnp.where(flag, far_one, far_two), item_row)
            target = north_entry if north else south_entry
            centre = jnp.where(
                target >= 0, pick(source, jnp.bitwise_and(target, slots - 1)), 0.0
            )
            return with_halo(centre, source, far, beside_north if north else beside_south)

        fetched = [fetch(position) for position in range(tiles + 2 * rows)]
        centre_parts = two_parts(jnp.concatenate([centre for centre, _ in fetched], axis=0))
        halo_parts = two_parts(jnp.concatenate([halo for _, halo in fetched], axis=0))
        across = jnp.dot(
            jnp.concatenate(
                [part for both in zip(centre_parts, halo_parts) for part in both], axis=1
            ),
            bands_ref[...],
            preferred_element_type=jnp.float32,
        )
        across = across[:, :LANES] + across[:, LANES:]
        lines = [across[slots * p : slots * (p + 1)] for p in range(tiles + 2 * rows)]
        for position in range(tiles + 2 * rows):
            if position:
                odd.append(roll(jnp.where(low_half, lines[position], lines[position - 1]), SIDE))
            if position >= 2 * rows:
                p = position - 2 * rows
                total = down_taps[0] * lines[p + 2]
                total = total + down_taps[1] * (odd[p + 1] + odd[p + 2])
                total = total + down_taps[2] * (lines[p + 1] + lines[p + 3])
                total = total + down_taps[3] * (odd[p] + odd[p + 3])
                total = total + down_taps[4] * (lines[p] + lines[p + 4])
                out_ref[item, :, p * LANES : (p + 1) * LANES] = live * total
        return 0

    lax.fori_loop(0, count, body, 0)


def exchange(first, second, pairs_first, pairs_second):
    return lax.ppermute(first, "blk", pairs_first), lax.ppermute(second, "blk", pairs_second)


def both_ways(pairs, count):
    partner = list(range(count))
    for a, b in pairs:
        partner[a], partner[b] = b, a
    return list(enumerate(partner))


def shards(input_field, active_mask, neighbours, time_taps, space_taps, coregion_factor):
    comps, days, slots, cells = input_field.shape
    count = comps * days
    blk = lax.axis_size("blk")
    day = lax.axis_size("day")
    place = jnp.stack([lax.axis_index("blk"), lax.axis_index("day")]).astype(jnp.int32)
    pair = day == 2
    if pair:
        others = [lax.ppermute(input_field, "day", [(0, 1), (1, 0)])]
    else:
        up = [(i, i + 1) for i in range(day - 1)]
        others = [
            lax.ppermute(input_field, "day", up),
            lax.ppermute(input_field, "day", [(b, a) for a, b in up]),
        ]
    packed = jax.ShapeDtypeStruct((slots, STRIP), jnp.float32)
    whole = pl.BlockSpec(memory_space=pltpu.VMEM)
    mixed, first, second = pl.pallas_call(
        functools.partial(filter_kernel, pair),
        out_shape=(jax.ShapeDtypeStruct((count, slots, cells), jnp.float32), packed, packed),
        in_specs=[SMEM] * 4 + [whole] * (2 + len(others)),
        out_specs=(whole,) * 3,
        compiler_params=PARAMS,
        name="time_filter",
    )(place, active_mask, time_taps, coregion_factor, neighbours, input_field, *others)

    columns = range(blk)
    even = both_ways([(i, i + 1) for i in columns if i % 2 == 0], blk)
    odd = [(i, i + 1) for i in columns if i % 2 == 1 and i % REACH != REACH - 1]
    odd = both_ways(odd, blk)
    first, second = exchange(first, second, even, odd)

    strip_spec = lambda at: pl.BlockSpec((count, slots, STRIP), lambda i: (0, 0, at))
    upright = jax.ShapeDtypeStruct((count + 1, slots, STRIP), jnp.float32)
    one, two = pl.pallas_call(
        corner_kernel,
        grid=(1,),
        out_shape=(upright, upright),
        in_specs=[SMEM, strip_spec(0), strip_spec(cells // STRIP - 1), whole, whole],
        out_specs=(whole, whole),
        compiler_params=PARAMS,
        name="corners",
    )(place, mixed, mixed, first, second)

    rows = blk // REACH
    upper = [(i, i + REACH) for i in columns if i // REACH % 2 == 0 and i // REACH + 1 < rows]
    lower = [(i, i + REACH) for i in columns if i // REACH % 2 == 1 and i // REACH + 1 < rows]
    one, two = exchange(one, two, both_ways(upper, blk), both_ways(lower, blk))

    bands = pl.pallas_call(
        bands_kernel,
        out_shape=jax.ShapeDtypeStruct((4 * LANES, 2 * LANES), jnp.bfloat16),
        in_specs=[SMEM],
        out_specs=whole,
        compiler_params=PARAMS,
        name="bands",
    )(space_taps)
    result = pl.pallas_call(
        smooth_kernel,
        out_shape=jax.ShapeDtypeStruct((count, slots, cells), jnp.float32),
        in_specs=[SMEM] * 3 + [whole] * 7,
        out_specs=whole,
        scratch_shapes=[pltpu.VMEM((cells // LANES, slots, LANES), jnp.float32)],
        compiler_params=PARAMS,
        name="spatial_filter",
    )(place, active_mask, space_taps, neighbours, bands, mixed, first, second, one, two)
    return result.reshape(input_field.shape)


def solution(mesh):
    in_specs = (P(None, "day", "blk", None), P("blk"), P("blk", None), P(), P(), P())
    out_specs = P(None, "day", "blk", None)
    return jax.shard_map(shards, mesh=mesh, in_specs=in_specs, out_specs=out_specs, check_vma=False)
```

```python
import functools

import jax
import jax.numpy as jnp
from jax import lax
from jax.experimental import pallas as pl
from jax.experimental.pallas import tpu as pltpu
from jax.sharding import PartitionSpec as P

SIDE = 64
SPACE_HALF = 4
TIME_HALF = 3
REACH = 4
LANES = 128
EAST, WEST, NORTH, SOUTH, NORTH_EAST, NORTH_WEST, SOUTH_EAST, SOUTH_WEST = range(8)
STRIP = SPACE_HALF * SIDE
PARAMS = pltpu.CompilerParams(vmem_limit_bytes=12 * 1024 * 1024)
SMEM = pl.BlockSpec(memory_space=pltpu.SMEM)


def iotas(slots):
    lane = lax.broadcasted_iota(jnp.int32, (slots, LANES), 1)
    sublane = lax.broadcasted_iota(jnp.int32, (slots, LANES), 0)
    return lane, sublane


def live_vector(mask_ref, sublane):
    live = jnp.zeros(sublane.shape, jnp.float32)
    for slot in range(sublane.shape[0]):
        live = jnp.where(sublane == slot, mask_ref[slot].astype(jnp.float32), live)
    return live


def entry(neighbours, direction, shape):
    return jnp.broadcast_to(neighbours[:, direction : direction + 1], shape)


def pick(source, index):
    return jnp.take_along_axis(source, index, axis=0)


def roll(x, shift):
    return pltpu.roll(x, shift % LANES if isinstance(shift, int) else shift, 1)


def on_device(target, device, slots):
    return (target >= 0) & (target // slots == device)


def put(ref, index, place, value):
    ref[index, :, place] = value


def filter_kernel(pair, place_ref, mask_ref, taps_ref, factor_ref, nb_ref, x_ref, *rest):
    *other_refs, mixed_ref, sent_ref = rest
    slots, cells = mixed_ref.shape[1:]
    days = x_ref.shape[1]
    me, day = place_ref[0], place_ref[1]
    lane, sublane = iotas(slots)
    column = jnp.bitwise_and(lane, SIDE - 1)
    live = live_vector(mask_ref, sublane)
    taps = [taps_ref[lag] for lag in range(TIME_HALF + 1)]
    weights = [
        [
            live * (factor_ref[a, 0] * factor_ref[b, 0] + factor_ref[a, 1] * factor_ref[b, 1])
            for b in range(2)
        ]
        for a in range(2)
    ]
    nb = nb_ref[...]

    def end_slot(directions, devices):
        hit = None
        for direction, device in zip(directions, devices):
            one = on_device(entry(nb, direction, lane.shape), device, slots)
            hit = one if hit is None else hit | one
        return jnp.max(jnp.where(hit, sublane, 0), axis=0, keepdims=True)

    east_end = end_slot((EAST, NORTH_EAST, SOUTH_EAST), (me + 1, me + 1 - REACH, me + 1 + REACH))
    west_end = end_slot((WEST, NORTH_WEST, SOUTH_WEST), (me - 1, me - 1 - REACH, me - 1 + REACH))
    end_index = jnp.where(
        column >= SIDE // 2,
        jnp.broadcast_to(east_end, lane.shape),
        jnp.broadcast_to(west_end, lane.shape),
    )
    order = [day * (days - 1 - 2 * s) + s if pair else s for s in range(days)]
    group = column // SPACE_HALF
    groups = SIDE // SPACE_HALF
    is_row = [sublane == a * days + order[t] for a in range(2) for t in range(days)]

    def part(tile, step):
        filtered = []
        where = pl.ds(pl.multiple_of((tile * groups + step) * LANES, LANES), LANES)
        for comp in range(2):
            own = [x_ref[comp, order[s], :, where] for s in range(days)]
            totals = []
            for t in range(days):
                total = taps[0] * own[t]
                for s in range(days):
                    if s != t:
                        total = total + taps[abs(s - t)] * own[s]
                totals.append(total)
            later = [other_refs[-1][comp, order[s], :, where] for s in range(days)]
            for t in range(days):
                for s in range(t + 1):
                    totals[t] = totals[t] + taps[days + s - t] * later[s]
            if not pair:
                earlier = [other_refs[0][comp, s, :, where] for s in range(days)]
                for t in range(days):
                    for s in range(t, days):
                        totals[t] = totals[t] + taps[days + t - s] * earlier[s]
            filtered.append(totals)
        edge = jnp.zeros(lane.shape, jnp.float32)
        for a in range(2):
            for t in range(days):
                value = weights[a][0] * filtered[0][t] + weights[a][1] * filtered[1][t]
                mixed_ref[a * days + order[t], :, where] = value
                edge = jnp.where(is_row[a * days + t], pick(value, end_index), edge)
        return edge

    at = jnp.bitwise_and(me, REACH - 1)
    sent_ref[...] = jnp.zeros(sent_ref.shape, jnp.float32)
    for tile in range(cells // (groups * LANES)):

        def body(step, held):
            east, west = held
            edge = part(tile, step)
            back = jnp.bitwise_and(LANES - SPACE_HALF * step, LANES - 1)
            east = jnp.where(group == groups - 1 - step, roll(edge, back), east)
            west = jnp.where(group == step, roll(edge, SPACE_HALF * step), west)
            return east, west

        zero = jnp.zeros(lane.shape, jnp.float32)
        east, west = lax.fori_loop(0, groups, body, (zero, zero))
        place = slice(tile * LANES, (tile + 1) * LANES)
        pl.when(at < REACH - 1)(functools.partial(put, sent_ref, at + 1, place, east))
        pl.when(at > 0)(functools.partial(put, sent_ref, at - 1, place, west))


def west_east(me, sent_ref, tile):
    place = slice(tile * LANES, (tile + 1) * LANES)
    at = jnp.bitwise_and(me, REACH - 1)
    west, east = jnp.maximum(at - 1, 0), jnp.minimum(at + 1, REACH - 1)
    return sent_ref[west, :, place], sent_ref[east, :, place]


def unpacked(column, west, east, step):
    return jnp.where(
        column >= SIDE // 2, roll(west, SPACE_HALF * step), roll(east, -SPACE_HALF * step)
    )


def corner_kernel(place_ref, top_ref, bottom_ref, beside_ref, sent_ref):
    me = place_ref[0]
    lane, _ = iotas(beside_ref.shape[1])
    column = jnp.bitwise_and(lane, SIDE - 1)
    row = me // REACH
    count = top_ref.shape[0]
    groups = SIDE // SPACE_HALF
    last = beside_ref.shape[2] // LANES - 1
    rows = STRIP // LANES

    def fill(target, strips_ref, tile, start):
        sent_ref[target, :count] = strips_ref[...]
        for half in range(rows):
            place = slice(half * LANES, (half + 1) * LANES)
            west, east = west_east(me, beside_ref, tile)
            sent_ref[target, count, :, place] = unpacked(column, west, east, start + half)

    pl.when(row > 0)(functools.partial(fill, row - 1, top_ref, 0, 0))
    pl.when(row < sent_ref.shape[0] - 1)(
        functools.partial(fill, row + 1, bottom_ref, last, groups - rows)
    )


def bands_kernel(taps_ref, bands_ref):
    shape = (2 * LANES, LANES)
    source = lax.broadcasted_iota(jnp.int32, shape, 0)
    target = lax.broadcasted_iota(jnp.int32, shape, 1)
    same = jnp.bitwise_and(source // SIDE, 1) == target // SIDE
    source_column = jnp.bitwise_and(source, SIDE - 1)
    outside = jnp.where(source_column >= SIDE // 2, source_column - SIDE, source_column + SIDE)
    position = jnp.where(source < LANES, source_column, outside)
    distance = jnp.abs(position - jnp.bitwise_and(target, SIDE - 1))
    bands = jnp.zeros(shape, jnp.float32)
    for lag in range(SPACE_HALF + 1):
        bands = jnp.where(same & (distance == lag), taps_ref[0, lag], bands)
    coarse, fine = two_parts(bands)
    bands_ref[: 2 * LANES, :LANES] = coarse
    bands_ref[: 2 * LANES, LANES:] = fine
    bands_ref[2 * LANES :, :LANES] = coarse
    bands_ref[2 * LANES :, LANES:] = jnp.zeros_like(fine)


def two_parts(x):
    coarse = x.astype(jnp.bfloat16)
    return coarse, (x - coarse.astype(jnp.float32)).astype(jnp.bfloat16)


def smooth_kernel(
    place_ref, mask_ref, taps_ref, nb_ref, bands_ref, mixed_ref, beside_ref, upright_ref,
    out_ref, side_ref,
):
    me = place_ref[0]
    count, slots, cells = mixed_ref.shape
    lane, sublane = iotas(slots)
    column = jnp.bitwise_and(lane, SIDE - 1)
    rightmost = column >= SIDE // 2
    low_half = lane < SIDE
    above = jnp.maximum(me // REACH - 1, 0)
    below = jnp.minimum(me // REACH + 1, upright_ref.shape[0] - 1)
    live = live_vector(mask_ref, sublane)
    down_taps = [taps_ref[1, lag] for lag in range(SPACE_HALF + 1)]
    nb = nb_ref[...]
    groups = SIDE // SPACE_HALF
    tiles = cells // LANES
    rows = STRIP // LANES

    def sides(west, east, device):
        target = jnp.where(rightmost, entry(nb, west, lane.shape), entry(nb, east, lane.shape))
        near = on_device(target, device, slots)
        return jnp.bitwise_and(target, slots - 1), near, (target >= 0) & ~near

    beside = sides(WEST, EAST, me)
    beside_north = sides(NORTH_WEST, NORTH_EAST, me - REACH)
    beside_south = sides(SOUTH_WEST, SOUTH_EAST, me + REACH)
    north_entry = entry(nb, NORTH, lane.shape)
    south_entry = entry(nb, SOUTH, lane.shape)

    for tile in range(tiles // groups):
        west, east = west_east(me, beside_ref, tile)
        for step in range(groups):
            side_ref[tile * groups + step] = unpacked(column, west, east, step)

    def with_halo(centre, source, far, plan):
        index, near, remote = plan
        halo = jnp.where(near, pick(source, index), 0.0)
        return centre, jnp.where(remote, far, halo)

    def body(item, _):
        odd = []
        item_row = jnp.full(lane.shape, item, jnp.int32)

        def fetch(position):
            if rows <= position < rows + tiles:
                start = (position - rows) * LANES
                centre = mixed_ref[item, :, start : start + LANES]
                far = jnp.broadcast_to(
                    side_ref[position - rows, pl.ds(item, 1)], lane.shape
                )
                return with_halo(centre, centre, far, beside)
            north = position < rows
            start = (position if north else position - rows - tiles) * LANES
            place = slice(start, start + LANES)
            upright = upright_ref.at[above if north else below]
            source = upright[item, :, place]
            far = pick(upright[count, :, place], item_row)
            target = north_entry if north else south_entry
            centre = jnp.where(
                target >= 0, pick(source, jnp.bitwise_and(target, slots - 1)), 0.0
            )
            return with_halo(centre, source, far, beside_north if north else beside_south)

        fetched = [fetch(position) for position in range(tiles + 2 * rows)]
        centre_parts = two_parts(jnp.concatenate([centre for centre, _ in fetched], axis=0))
        halo_parts = two_parts(jnp.concatenate([halo for _, halo in fetched], axis=0))
        across = jnp.dot(
            jnp.concatenate(
                [part for both in zip(centre_parts, halo_parts) for part in both], axis=1
            ),
            bands_ref[...],
            preferred_element_type=jnp.float32,
        )
        across = across[:, :LANES] + across[:, LANES:]
        lines = [across[slots * p : slots * (p + 1)] for p in range(tiles + 2 * rows)]
        for position in range(tiles + 2 * rows):
            if position:
                odd.append(roll(jnp.where(low_half, lines[position], lines[position - 1]), SIDE))
            if position >= 2 * rows:
                p = position - 2 * rows
                total = down_taps[0] * lines[p + 2]
                total = total + down_taps[1] * (odd[p + 1] + odd[p + 2])
                total = total + down_taps[2] * (lines[p + 1] + lines[p + 3])
                total = total + down_taps[3] * (odd[p] + odd[p + 3])
                total = total + down_taps[4] * (lines[p] + lines[p + 4])
                out_ref[item, :, p * LANES : (p + 1) * LANES] = live * total
        return 0

    lax.fori_loop(0, count, body, 0)


def shards(input_field, active_mask, neighbours, time_taps, space_taps, coregion_factor):
    comps, days, slots, cells = input_field.shape
    count = comps * days
    blk = lax.axis_size("blk")
    day = lax.axis_size("day")
    place = jnp.stack([lax.axis_index("blk"), lax.axis_index("day")]).astype(jnp.int32)
    pair = day == 2
    if pair:
        others = [lax.ppermute(input_field, "day", [(0, 1), (1, 0)])]
    else:
        up = [(i, i + 1) for i in range(day - 1)]
        others = [
            lax.ppermute(input_field, "day", up),
            lax.ppermute(input_field, "day", [(b, a) for a, b in up]),
        ]
    packed = jax.ShapeDtypeStruct((slots, STRIP), jnp.float32)
    whole = pl.BlockSpec(memory_space=pltpu.VMEM)
    mixed, beside = pl.pallas_call(
        functools.partial(filter_kernel, pair),
        out_shape=(
            jax.ShapeDtypeStruct((count, slots, cells), jnp.float32),
            jax.ShapeDtypeStruct((REACH, slots, STRIP), jnp.float32),
        ),
        in_specs=[SMEM] * 4 + [whole] * (2 + len(others)),
        out_specs=(whole,) * 2,
        compiler_params=PARAMS,
        name="time_filter",
    )(place, active_mask, time_taps, coregion_factor, neighbours, input_field, *others)

    rows = blk // REACH
    along = [[r * REACH + c for c in range(REACH)] for r in range(rows)]
    beside = lax.all_to_all(beside, "blk", 0, 0, axis_index_groups=along)

    strip_spec = lambda at: pl.BlockSpec((count, slots, STRIP), lambda i: (0, 0, at))
    upright = pl.pallas_call(
        corner_kernel,
        grid=(1,),
        out_shape=jax.ShapeDtypeStruct((rows, count + 1, slots, STRIP), jnp.float32),
        in_specs=[SMEM, strip_spec(0), strip_spec(cells // STRIP - 1), whole],
        out_specs=whole,
        compiler_params=PARAMS,
        name="corners",
    )(place, mixed, mixed, beside)

    down = [[r * REACH + c for r in range(rows)] for c in range(REACH)]
    upright = lax.all_to_all(upright, "blk", 0, 0, axis_index_groups=down)

    bands = pl.pallas_call(
        bands_kernel,
        out_shape=jax.ShapeDtypeStruct((4 * LANES, 2 * LANES), jnp.bfloat16),
        in_specs=[SMEM],
        out_specs=whole,
        compiler_params=PARAMS,
        name="bands",
    )(space_taps)
    result = pl.pallas_call(
        smooth_kernel,
        out_shape=jax.ShapeDtypeStruct((count, slots, cells), jnp.float32),
        in_specs=[SMEM] * 3 + [whole] * 5,
        out_specs=whole,
        scratch_shapes=[pltpu.VMEM((cells // LANES, slots, LANES), jnp.float32)],
        compiler_params=PARAMS,
        name="spatial_filter",
    )(place, active_mask, space_taps, neighbours, bands, mixed, beside, upright)
    return result.reshape(input_field.shape)


def solution(mesh):
    in_specs = (P(None, "day", "blk", None), P("blk"), P("blk", None), P(), P(), P())
    out_specs = P(None, "day", "blk", None)
    return jax.shard_map(shards, mesh=mesh, in_specs=in_specs, out_specs=out_specs, check_vma=False)
```

```python
import functools

import jax
import jax.numpy as jnp
from jax import lax
from jax.experimental import pallas as pl
from jax.experimental.pallas import tpu as pltpu
from jax.sharding import PartitionSpec as P

SIDE = 64
SPACE_HALF = 4
TIME_HALF = 3
REACH = 4
LANES = 128
EAST, WEST, NORTH, SOUTH, NORTH_EAST, NORTH_WEST, SOUTH_EAST, SOUTH_WEST = range(8)
PAIR_ROWS = SPACE_HALF * SIDE // LANES
GROUPS = SIDE // SPACE_HALF
PARAMS = pltpu.CompilerParams(vmem_limit_bytes=12 * 1024 * 1024)
SMEM = pl.BlockSpec(memory_space=pltpu.SMEM)
WHOLE = pl.BlockSpec(memory_space=pltpu.VMEM)


def array(*shape):
    return jax.ShapeDtypeStruct(shape, jnp.float32)


def iotas(slots):
    lane = lax.broadcasted_iota(jnp.int32, (slots, LANES), 1)
    sublane = lax.broadcasted_iota(jnp.int32, (slots, LANES), 0)
    return lane, sublane


def live_vector(mask_ref, sublane):
    live = jnp.zeros(sublane.shape, jnp.float32)
    for slot in range(sublane.shape[0]):
        live = jnp.where(sublane == slot, mask_ref[slot].astype(jnp.float32), live)
    return live


def entry(neighbours, direction, shape):
    return jnp.broadcast_to(neighbours[:, direction : direction + 1], shape)


def pick(source, index):
    return jnp.take_along_axis(source, index, axis=0)


def roll(x, shift):
    return pltpu.roll(x, shift % LANES if isinstance(shift, int) else shift, 1)


def wrapped(shift):
    return jnp.bitwise_and(shift, LANES - 1)


def on_device(target, device, slots):
    return (target >= 0) & (target // slots == device)


def taps_of(taps_ref):
    return [taps_ref[lag] for lag in range(TIME_HALF + 1)]


def order_of(pair, day, days):
    return [day * (days - 1 - 2 * s) + s if pair else s for s in range(days)]


def coupling_of(factor_ref):
    return [
        [
            factor_ref[a, 0] * factor_ref[b, 0] + factor_ref[a, 1] * factor_ref[b, 1]
            for b in range(2)
        ]
        for a in range(2)
    ]


def same_days(taps, values):
    totals = []
    for t in range(len(values)):
        total = taps[0] * values[t]
        for s in range(len(values)):
            if s != t:
                total = total + taps[abs(s - t)] * values[s]
        totals.append(total)
    return totals


def add_later(taps, totals, values):
    for t in range(len(totals)):
        for s in range(t + 1):
            totals[t] = totals[t] + taps[len(totals) + s - t] * values[s]


def add_earlier(taps, totals, values):
    for t in range(len(totals)):
        for s in range(t, len(totals)):
            totals[t] = totals[t] + taps[len(totals) + t - s] * values[s]


def heads_east(place_ref):
    return jnp.bitwise_and(place_ref[0] + place_ref[1], 1) == 0


def heads_south(place_ref):
    return jnp.bitwise_and(place_ref[0] // REACH + place_ref[1], 1) == 0


def end_slot(nb_ref, me, east):
    slots = nb_ref.shape[0]
    step, directions = (
        (1, (EAST, NORTH_EAST, SOUTH_EAST)) if east else (-1, (WEST, NORTH_WEST, SOUTH_WEST))
    )
    found = jnp.int32(0)
    for slot in range(slots):
        for direction, shift in zip(directions, (0, -REACH, REACH)):
            target = nb_ref[slot, direction]
            hit = (target >= 0) & (target // slots == me + step + shift)
            found = jnp.where(hit, slot, found)
    return found


def edge_plan(pair, place_ref, nb_ref):
    me = place_ref[0]
    east, west = end_slot(nb_ref, me, True), end_slot(nb_ref, me, False)
    if pair:
        to_east = heads_east(place_ref)
        return [(to_east, jnp.where(to_east, east, west))]
    return [(True, east), (False, west)]


def strip_starts(pair, place_ref, tiles):
    last = tiles - PAIR_ROWS
    return [jnp.where(heads_south(place_ref), last, 0)] if pair else [last, 0]


def own_kernel(pair, place_ref, mask_ref, taps_ref, nb_ref, x_ref, *out_refs):
    comps, days, tiles, slots, _ = x_ref.shape
    own_ref, *rest = out_refs
    edge_refs, strip_refs = rest[: len(rest) // 2], rest[len(rest) // 2 :]
    taps = taps_of(taps_ref)
    for edge_ref, (_, slot) in zip(edge_refs, edge_plan(pair, place_ref, nb_ref)):
        live = mask_ref[slot].astype(jnp.float32)
        for comp in range(comps):
            for t in range(days):
                edge_ref[comp * days + t] = live * x_ref[comp, t, :, slot, :]
    for strip_ref, start in zip(strip_refs, strip_starts(pair, place_ref, tiles)):
        for comp in range(comps):
            for t in range(days):
                strip_ref[comp * days + t] = x_ref[comp, t, pl.ds(start, PAIR_ROWS)]

    def body(tile, _):
        for comp in range(comps):
            values = [x_ref[comp, t, tile] for t in range(days)]
            for t, total in enumerate(same_days(taps, values)):
                own_ref[comp * days + t, tile] = total
        return 0

    lax.fori_loop(0, tiles, body, 0, unroll=4)


def send_kernel(pair, place_ref, mask_ref, taps_ref, factor_ref, nb_ref, *refs):
    sides = 1 if pair else 2
    edge_refs, strip_refs = refs[:sides], refs[sides : 2 * sides]
    other_refs = refs[2 * sides : len(refs) - 2 * sides]
    packed_refs = refs[len(refs) - 2 * sides : len(refs) - sides]
    sent_refs = refs[len(refs) - sides :]
    comps, days, tiles, slots, _ = other_refs[0].shape
    lane, sublane = iotas(slots)
    group = jnp.bitwise_and(lax.broadcasted_iota(jnp.int32, (tiles, LANES), 1), SIDE - 1)
    group = group // SPACE_HALF
    live_slots = live_vector(mask_ref, sublane)
    taps = taps_of(taps_ref)
    coupling = coupling_of(factor_ref)
    order = order_of(pair, place_ref[1], days)

    def all_days(raw_ref, read_other):
        results = [None] * (comps * days * (2 if pair else 1))
        mine, theirs = [], []
        for comp in range(comps):
            values = [raw_ref[comp * days + order[s]] for s in range(days)]
            later = [read_other(other_refs[-1], comp, order[s]) for s in range(days)]
            totals = same_days(taps, values)
            add_later(taps, totals, later)
            if pair:
                others = same_days(taps, later)
                add_earlier(taps, others, values)
                theirs.append(others)
            else:
                add_earlier(
                    taps, totals, [read_other(other_refs[0], comp, s) for s in range(days)]
                )
            mine.append(totals)
        for base, filtered in enumerate([mine, theirs] if pair else [mine]):
            for a in range(comps):
                for t in range(days):
                    value = coupling[a][0] * filtered[0][t] + coupling[a][1] * filtered[1][t]
                    yield base * comps * days + a * days + order[t], value

    for edge_ref, packed_ref, (to_east, slot) in zip(
        edge_refs, packed_refs, edge_plan(pair, place_ref, nb_ref)
    ):
        live = mask_ref[slot].astype(jnp.float32)
        packed = jnp.zeros((tiles, LANES), jnp.float32)
        for at, value in all_days(edge_ref, lambda ref, c, s: live * ref[c, s, :, slot, :]):
            shift = wrapped(jnp.where(to_east, LANES - SPACE_HALF * at, SPACE_HALF * at))
            spot = jnp.where(to_east, GROUPS - 1 - at, at)
            packed = jnp.where(group == spot, roll(value, shift), packed)
        packed_ref[...] = packed
    for strip_ref, sent_ref, start in zip(
        strip_refs, sent_refs, strip_starts(pair, place_ref, tiles)
    ):
        for at, value in all_days(strip_ref, lambda ref, c, s: ref[c, s, pl.ds(start, PAIR_ROWS)]):
            sent_ref[at] = live_slots * value


def mix_kernel(pair, place_ref, mask_ref, taps_ref, factor_ref, own_ref, *rest):
    *other_refs, mixed_ref = rest
    _, tiles, slots, _ = mixed_ref.shape
    comps, days = other_refs[0].shape[:2]
    _, sublane = iotas(slots)
    live = live_vector(mask_ref, sublane)
    taps = taps_of(taps_ref)
    weights = [[live * value for value in row] for row in coupling_of(factor_ref)]
    order = order_of(pair, place_ref[1], days)

    def body(tile, _):
        filtered = []
        for comp in range(comps):
            totals = [own_ref[comp * days + order[t], tile] for t in range(days)]
            add_later(taps, totals, [other_refs[-1][comp, order[s], tile] for s in range(days)])
            if not pair:
                add_earlier(taps, totals, [other_refs[0][comp, s, tile] for s in range(days)])
            filtered.append(totals)
        for a in range(comps):
            for t in range(days):
                mixed_ref[a * days + order[t], tile] = (
                    weights[a][0] * filtered[0][t] + weights[a][1] * filtered[1][t]
                )
        return 0

    lax.fori_loop(0, tiles, body, 0, unroll=4)


def west_east(pair, place_ref, first, second):
    if not pair:
        return first, second
    to_east = heads_east(place_ref)
    return jnp.where(to_east, second, first), jnp.where(to_east, first, second)


def unpacked(pair, place_ref, count, item, west, east):
    column = jnp.bitwise_and(lax.broadcasted_iota(jnp.int32, west.shape, 1), SIDE - 1)
    far_west = far_east = item
    if pair:
        to_east = heads_east(place_ref)
        far_west = item + jnp.where(to_east, count, 0)
        far_east = item + jnp.where(to_east, 0, count)
    return jnp.where(
        column >= SIDE // 2,
        roll(west, wrapped(SPACE_HALF * far_west)),
        roll(east, wrapped(LANES - SPACE_HALF * far_east)),
    )


def corner_kernel(pair, place_ref, first_ref, second_ref, *refs):
    out_refs = refs[len(refs) // 2 :]
    slots = out_refs[0].shape[2]
    west, east = west_east(pair, place_ref, first_ref[...], second_ref[...])
    top = [west[:slots], east[:slots]]
    bottom = [west[-slots:], east[-slots:]]
    for side, out_ref in enumerate(out_refs):
        for k in range(2):
            if pair:
                out_ref[0, k] = jnp.where(heads_south(place_ref), bottom[k], top[k])
            else:
                out_ref[0, k] = (bottom, top)[side][k]


def two_parts(x):
    coarse = x.astype(jnp.bfloat16)
    return coarse, (x - coarse.astype(jnp.float32)).astype(jnp.bfloat16)


def bands_kernel(taps_ref, bands_ref):
    shape = (2 * LANES, LANES)
    source = lax.broadcasted_iota(jnp.int32, shape, 0)
    target = lax.broadcasted_iota(jnp.int32, shape, 1)
    same = jnp.bitwise_and(source // SIDE, 1) == target // SIDE
    source_column = jnp.bitwise_and(source, SIDE - 1)
    outside = jnp.where(source_column >= SIDE // 2, source_column - SIDE, source_column + SIDE)
    position = jnp.where(source < LANES, source_column, outside)
    distance = jnp.abs(position - jnp.bitwise_and(target, SIDE - 1))
    bands = jnp.zeros(shape, jnp.float32)
    for lag in range(SPACE_HALF + 1):
        bands = jnp.where(same & (distance == lag), taps_ref[0, lag], bands)
    coarse, fine = two_parts(bands)
    bands_ref[: 2 * LANES, :LANES] = coarse
    bands_ref[: 2 * LANES, LANES:] = fine
    bands_ref[2 * LANES :, :LANES] = coarse
    bands_ref[2 * LANES :, LANES:] = jnp.zeros_like(fine)


def across(bands, tiles):
    slots = tiles[0][0].shape[0]
    centre_parts = two_parts(jnp.concatenate([centre for centre, _ in tiles], axis=0))
    halo_parts = two_parts(jnp.concatenate([halo for _, halo in tiles], axis=0))
    product = jnp.dot(
        jnp.concatenate([part for both in zip(centre_parts, halo_parts) for part in both], axis=1),
        bands,
        preferred_element_type=jnp.float32,
    )
    product = product[:, :LANES] + product[:, LANES:]
    return [product[slots * p : slots * (p + 1)] for p in range(len(tiles))]


def sides_of(nb, west, east, device, shape):
    slots = shape[0]
    column = jnp.bitwise_and(lax.broadcasted_iota(jnp.int32, shape, 1), SIDE - 1)
    target = jnp.where(column >= SIDE // 2, entry(nb, west, shape), entry(nb, east, shape))
    near = on_device(target, device, slots)
    return jnp.bitwise_and(target, slots - 1), near, (target >= 0) & ~near


def halo_of(source, far, plan):
    index, near, remote = plan
    halo = jnp.where(near, pick(source, index), 0.0)
    return jnp.where(remote, jnp.broadcast_to(far, halo.shape), halo)


def odd_rows(before, after):
    low = lax.broadcasted_iota(jnp.int32, before.shape, 1) < SIDE
    return roll(jnp.where(low, after, before), SIDE)


def inner_kernel(
    pair, place_ref, mask_ref, taps_ref, nb_ref, bands_ref, mixed_ref, first_ref, second_ref,
    out_ref, outer_ref, far_ref,
):
    count, tiles, slots, _ = mixed_ref.shape
    lane, sublane = iotas(slots)
    live = live_vector(mask_ref, sublane)
    taps = [taps_ref[1, lag] for lag in range(SPACE_HALF + 1)]
    plan = sides_of(nb_ref[...], WEST, EAST, place_ref[0], lane.shape)
    west, east = west_east(pair, place_ref, first_ref[...], second_ref[...])
    share = out_ref.shape[0]

    def body(step, _):
        item = pl.program_id(0) * share + step
        far_ref[...] = unpacked(pair, place_ref, count, item, west, east)
        fetched = []
        for tile in range(tiles):
            centre = mixed_ref[item, tile]
            fetched.append((centre, halo_of(centre, far_ref[tile : tile + 1], plan)))
        zero = jnp.zeros(lane.shape, jnp.float32)
        rows = [zero] * PAIR_ROWS + across(bands_ref[...], fetched) + [zero] * PAIR_ROWS
        odd = [odd_rows(rows[p], rows[p + 1]) for p in range(len(rows) - 1)]
        for p in range(tiles):
            total = taps[0] * rows[p + 2]
            total = total + taps[1] * (odd[p + 1] + odd[p + 2])
            total = total + taps[2] * (rows[p + 1] + rows[p + 3])
            total = total + taps[3] * (odd[p] + odd[p + 3])
            total = total + taps[4] * (rows[p] + rows[p + 4])
            total = live * total
            out_ref[step, p] = total
            if p < PAIR_ROWS:
                outer_ref[item, p] = total
            elif p >= tiles - PAIR_ROWS:
                outer_ref[item, p - tiles + 2 * PAIR_ROWS] = total
        return 0

    lax.fori_loop(0, share, body, 0)


def outer_kernel(
    pair, place_ref, mask_ref, taps_ref, nb_ref, bands_ref, outer_ref, first_ref, second_ref,
    _, out_ref,
):
    count, _, slots, _ = outer_ref.shape
    lane, sublane = iotas(slots)
    live = live_vector(mask_ref, sublane)
    taps = [taps_ref[1, lag] for lag in range(SPACE_HALF + 1)]
    nb = nb_ref[...]
    me = place_ref[0]

    def one_side(north):
        if pair:
            use_second = heads_south(place_ref) if north else ~heads_south(place_ref)
        else:
            use_second = not north

        def read(index, part):
            if not pair:
                return (first_ref if north else second_ref)[index, part]
            at = index if index < count else 2 * count
            return jnp.where(use_second, second_ref[index, part], first_ref[at, part])

        target = entry(nb, NORTH if north else SOUTH, lane.shape)
        plan = sides_of(
            nb,
            NORTH_WEST if north else SOUTH_WEST,
            NORTH_EAST if north else SOUTH_EAST,
            me - REACH if north else me + REACH,
            lane.shape,
        )
        corner = [read(count, 0), read(count, 1)]
        fetched = []
        for item in range(count):
            far = unpacked(pair, place_ref, count, jnp.int32(item), *corner)
            for part in range(PAIR_ROWS):
                source = read(item, part)
                centre = jnp.where(
                    target >= 0, pick(source, jnp.bitwise_and(target, slots - 1)), 0.0
                )
                row = slots - PAIR_ROWS + part if north else part
                fetched.append((centre, halo_of(source, far[row : row + 1], plan)))
        rows = across(bands_ref[...], fetched)
        zero = jnp.zeros(lane.shape, jnp.float32)
        for item in range(count):
            one, two = rows[PAIR_ROWS * item : PAIR_ROWS * (item + 1)]
            if north:
                edge = odd_rows(two, zero)
                near = taps[1] * edge + taps[2] * two + taps[3] * odd_rows(one, two)
                near = near + taps[4] * one
                off = taps[3] * edge + taps[4] * two
                out_ref[item, 0] = outer_ref[item, 0] + live * near
                out_ref[item, 1] = outer_ref[item, 1] + live * off
            else:
                edge = odd_rows(zero, one)
                near = taps[1] * edge + taps[2] * one + taps[3] * odd_rows(one, two)
                near = near + taps[4] * two
                off = taps[3] * edge + taps[4] * one
                out_ref[item, 0] = outer_ref[item, 2] + live * off
                out_ref[item, 1] = outer_ref[item, 3] + live * near

    pl.when(pl.program_id(0) == 0)(lambda: one_side(True))
    pl.when(pl.program_id(0) == 1)(lambda: one_side(False))


def partners(pairs, count):
    partner = list(range(count))
    for a, b in pairs:
        partner[a], partner[b] = b, a
    return partner


def split_swap(x, first, second):
    pairs = [(2 * a, 2 * b) for a, b in enumerate(first)]
    pairs += [(2 * a + 1, 2 * b + 1) for a, b in enumerate(second)]
    return lax.ppermute(x, ("blk", "day"), pairs)


def shards(input_field, active_mask, neighbours, time_taps, space_taps, coregion_factor):
    comps, days, slots, cells = input_field.shape
    count = comps * days
    tiles = cells // LANES
    blk = lax.axis_size("blk")
    day = lax.axis_size("day")
    pair = day == 2
    sides = 1 if pair else 2
    place = jnp.stack([lax.axis_index("blk"), lax.axis_index("day")]).astype(jnp.int32)
    columns = range(blk)
    chip_swap = [(0, 1), (1, 0)]

    def in_tiles(x):
        return x.reshape(comps, days, slots, tiles, LANES).transpose(0, 1, 3, 2, 4)

    if pair:
        others = [lax.ppermute(input_field, "day", chip_swap)]
    else:
        up = [(i, i + 1) for i in range(day - 1)]
        others = [
            lax.ppermute(input_field, "day", up),
            lax.ppermute(input_field, "day", [(b, a) for a, b in up]),
        ]
    others = [in_tiles(x) for x in others]
    field = array(count, tiles, slots, LANES)

    own, *raw = pl.pallas_call(
        functools.partial(own_kernel, pair),
        out_shape=(field,)
        + (array(count, tiles, LANES),) * sides
        + (array(count, PAIR_ROWS, slots, LANES),) * sides,
        in_specs=[SMEM] * 4 + [WHOLE],
        out_specs=(WHOLE,) * (1 + 2 * sides),
        compiler_params=PARAMS,
        name="own_days",
    )(place, active_mask, time_taps, neighbours, in_tiles(input_field))

    sent_count = count * (2 if pair else 1) + 1
    sent_shape = array(sent_count, PAIR_ROWS, slots, LANES)
    packed_and_sent = pl.pallas_call(
        functools.partial(send_kernel, pair),
        out_shape=(array(tiles, LANES),) * sides + (sent_shape,) * sides,
        in_specs=[SMEM] * 5 + [WHOLE] * (len(raw) + len(others)),
        out_specs=(WHOLE,) * (2 * sides),
        compiler_params=PARAMS,
        name="edges_and_strips",
    )(place, active_mask, time_taps, coregion_factor, neighbours, *raw, *others)
    packed, sent = packed_and_sent[:sides], packed_and_sent[sides:]

    if pair:
        even = partners([(i, i + 1) for i in columns if i % 2 == 0], blk)
        odd = [(i, i + 1) for i in columns if i % 2 == 1 and i % REACH != REACH - 1]
        first = split_swap(packed[0], even, partners(odd, blk))
        second = lax.ppermute(first, "day", chip_swap)
    else:
        east = [(i, i + 1) for i in columns if i % REACH != REACH - 1]
        first = lax.ppermute(packed[0], "blk", east)
        second = lax.ppermute(packed[1], "blk", [(b, a) for a, b in east])

    mixed = pl.pallas_call(
        functools.partial(mix_kernel, pair),
        out_shape=field,
        in_specs=[SMEM] * 4 + [WHOLE] * (1 + len(others)),
        out_specs=WHOLE,
        compiler_params=PARAMS,
        name="mix",
    )(place, active_mask, time_taps, coregion_factor, own, *others)

    bands = pl.pallas_call(
        bands_kernel,
        out_shape=jax.ShapeDtypeStruct((4 * LANES, 2 * LANES), jnp.bfloat16),
        in_specs=[SMEM],
        out_specs=WHOLE,
        compiler_params=PARAMS,
        name="bands",
    )(space_taps)

    sent = pl.pallas_call(
        functools.partial(corner_kernel, pair),
        grid=(1,),
        out_shape=(sent_shape,) * sides,
        in_specs=[SMEM, WHOLE, WHOLE] + [pl.BlockSpec(memory_space=pl.ANY)] * sides,
        out_specs=(
            pl.BlockSpec((1, PAIR_ROWS, slots, LANES), lambda i: (sent_count - 1, 0, 0, 0)),
        )
        * sides,
        input_output_aliases={3 + side: side for side in range(sides)},
        compiler_params=PARAMS,
        name="corners",
    )(place, first, second, *sent)

    if pair:
        south = [(i, i + REACH) for i in columns if i + REACH < blk]
        even = partners([(a, b) for a, b in south if a // REACH % 2 == 0], blk)
        odd = partners([(a, b) for a, b in south if a // REACH % 2 == 1], blk)
        one = split_swap(sent[0], even, odd)
        two = lax.ppermute(one[count:], "day", chip_swap)
    else:
        south = [(i, i + REACH) for i in range(blk - REACH)]
        one = lax.ppermute(sent[0], "blk", south)
        two = lax.ppermute(sent[1], "blk", [(b, a) for a, b in south])

    steps = 2
    inner, outer = pl.pallas_call(
        functools.partial(inner_kernel, pair),
        grid=(steps,),
        out_shape=(field, array(count, 2 * PAIR_ROWS, slots, LANES)),
        in_specs=[SMEM] * 3 + [WHOLE] * 5,
        out_specs=(
            pl.BlockSpec((count // steps, tiles, slots, LANES), lambda i: (i, 0, 0, 0)),
            pl.BlockSpec((count, 2 * PAIR_ROWS, slots, LANES), lambda i: (0, 0, 0, 0)),
        ),
        scratch_shapes=[pltpu.VMEM((tiles, LANES), jnp.float32)],
        compiler_params=PARAMS,
        name="inner_rows",
    )(place, active_mask, space_taps, neighbours, bands, mixed, first, second)

    last = tiles // PAIR_ROWS - 1
    result = pl.pallas_call(
        functools.partial(outer_kernel, pair),
        grid=(2,),
        out_shape=field,
        in_specs=[SMEM] * 3 + [WHOLE] * 5 + [pl.BlockSpec(memory_space=pl.ANY)],
        out_specs=pl.BlockSpec((count, PAIR_ROWS, slots, LANES), lambda i: (0, i * last, 0, 0)),
        input_output_aliases={8: 0},
        compiler_params=PARAMS,
        name="outer_rows",
    )(place, active_mask, space_taps, neighbours, bands, outer, one, two, inner)
    result = result.reshape(comps, days, tiles, slots, LANES).transpose(0, 1, 3, 2, 4)
    return result.reshape(input_field.shape)


def solution(mesh):
    in_specs = (P(None, "day", "blk", None), P("blk"), P("blk", None), P(), P(), P())
    out_specs = P(None, "day", "blk", None)
    return jax.shard_map(shards, mesh=mesh, in_specs=in_specs, out_specs=out_specs, check_vma=False)
```

```python
import functools

import jax
import jax.numpy as jnp
from jax import lax
from jax.experimental import pallas as pl
from jax.experimental.pallas import tpu as pltpu
from jax.sharding import PartitionSpec as P

SIDE = 64
SPACE_HALF = 4
TIME_HALF = 3
REACH = 4
LANES = 128
EAST, WEST, NORTH, SOUTH, NORTH_EAST, NORTH_WEST, SOUTH_EAST, SOUTH_WEST = range(8)
PAIR_ROWS = SPACE_HALF * SIDE // LANES
GROUPS = SIDE // SPACE_HALF
PARAMS = pltpu.CompilerParams(vmem_limit_bytes=12 * 1024 * 1024)
SMEM = pl.BlockSpec(memory_space=pltpu.SMEM)
WHOLE = pl.BlockSpec(memory_space=pltpu.VMEM)


def array(*shape):
    return jax.ShapeDtypeStruct(shape, jnp.float32)


def iotas(slots):
    lane = lax.broadcasted_iota(jnp.int32, (slots, LANES), 1)
    sublane = lax.broadcasted_iota(jnp.int32, (slots, LANES), 0)
    return lane, sublane


def live_vector(mask_ref, sublane):
    live = jnp.zeros(sublane.shape, jnp.float32)
    for slot in range(sublane.shape[0]):
        live = jnp.where(sublane == slot, mask_ref[slot].astype(jnp.float32), live)
    return live


def entry(neighbours, direction, shape):
    return jnp.broadcast_to(neighbours[:, direction : direction + 1], shape)


def pick(source, index):
    return jnp.take_along_axis(source, index, axis=0)


def roll(x, shift):
    return pltpu.roll(x, shift % LANES if isinstance(shift, int) else shift, 1)


def wrapped(shift):
    return jnp.bitwise_and(shift, LANES - 1)


def on_device(target, device, slots):
    return (target >= 0) & (target // slots == device)


def taps_of(taps_ref):
    return [taps_ref[lag] for lag in range(TIME_HALF + 1)]


def order_of(pair, day, days):
    return [day * (days - 1 - 2 * s) + s if pair else s for s in range(days)]


def coupling_of(factor_ref):
    return [
        [
            factor_ref[a, 0] * factor_ref[b, 0] + factor_ref[a, 1] * factor_ref[b, 1]
            for b in range(2)
        ]
        for a in range(2)
    ]


def same_days(taps, values):
    totals = []
    for t in range(len(values)):
        total = taps[0] * values[t]
        for s in range(len(values)):
            if s != t:
                total = total + taps[abs(s - t)] * values[s]
        totals.append(total)
    return totals


def add_later(taps, totals, values):
    for t in range(len(totals)):
        for s in range(t + 1):
            totals[t] = totals[t] + taps[len(totals) + s - t] * values[s]


def add_earlier(taps, totals, values):
    for t in range(len(totals)):
        for s in range(t, len(totals)):
            totals[t] = totals[t] + taps[len(totals) + t - s] * values[s]


def east_first(place_ref):
    return jnp.bitwise_and(place_ref[0], 1) == 0


def south_first(place_ref):
    return jnp.bitwise_and(place_ref[0] // REACH, 1) == 0


def end_slot(nb_ref, me, east):
    slots = nb_ref.shape[0]
    step, directions = (
        (1, (EAST, NORTH_EAST, SOUTH_EAST)) if east else (-1, (WEST, NORTH_WEST, SOUTH_WEST))
    )
    found = jnp.int32(0)
    for slot in range(slots):
        for direction, shift in zip(directions, (0, -REACH, REACH)):
            target = nb_ref[slot, direction]
            hit = (target >= 0) & (target // slots == me + step + shift)
            found = jnp.where(hit, slot, found)
    return found


def edge_plan(place_ref, nb_ref):
    me = place_ref[0]
    east, west = end_slot(nb_ref, me, True), end_slot(nb_ref, me, False)
    first = east_first(place_ref)
    return [(first, jnp.where(first, east, west)), (~first, jnp.where(first, west, east))]


def strip_starts(place_ref, tiles):
    last = tiles - PAIR_ROWS
    first = south_first(place_ref)
    return [jnp.where(first, last, 0), jnp.where(first, 0, last)]


def own_kernel(place_ref, mask_ref, taps_ref, _, nb_ref, x_ref, *out_refs):
    comps, days, tiles, slots, _ = x_ref.shape
    own_ref, *rest = out_refs
    edge_refs, strip_refs = rest[: len(rest) // 2], rest[len(rest) // 2 :]
    taps = taps_of(taps_ref)
    for edge_ref, (_, slot) in zip(edge_refs, edge_plan(place_ref, nb_ref)):
        live = mask_ref[slot].astype(jnp.float32)
        for comp in range(comps):
            for t in range(days):
                edge_ref[comp * days + t] = live * x_ref[comp, t, :, slot, :]
    for strip_ref, start in zip(strip_refs, strip_starts(place_ref, tiles)):
        for comp in range(comps):
            for t in range(days):
                strip_ref[comp * days + t] = x_ref[comp, t, pl.ds(start, PAIR_ROWS)]

    def body(tile, _):
        for comp in range(comps):
            values = [x_ref[comp, t, tile] for t in range(days)]
            for t, total in enumerate(same_days(taps, values)):
                own_ref[comp * days + t, tile] = total
        return 0

    lax.fori_loop(0, tiles, body, 0, unroll=4)


def send_kernel(pair, place_ref, mask_ref, taps_ref, factor_ref, nb_ref, *refs):
    sides = 2
    edge_refs, strip_refs = refs[:sides], refs[sides : 2 * sides]
    other_refs = refs[2 * sides : len(refs) - 2 * sides]
    packed_refs = refs[len(refs) - 2 * sides : len(refs) - sides]
    sent_refs = refs[len(refs) - sides :]
    comps, days, tiles, slots, _ = other_refs[0].shape
    lane, sublane = iotas(slots)
    group = jnp.bitwise_and(lax.broadcasted_iota(jnp.int32, (tiles, LANES), 1), SIDE - 1)
    group = group // SPACE_HALF
    live_slots = live_vector(mask_ref, sublane)
    taps = taps_of(taps_ref)
    coupling = coupling_of(factor_ref)
    order = order_of(pair, place_ref[1], days)

    def all_days(raw_ref, read_other):
        filtered = []
        for comp in range(comps):
            values = [raw_ref[comp * days + order[s]] for s in range(days)]
            later = [read_other(other_refs[-1], comp, order[s]) for s in range(days)]
            totals = same_days(taps, values)
            add_later(taps, totals, later)
            if not pair:
                add_earlier(
                    taps, totals, [read_other(other_refs[0], comp, s) for s in range(days)]
                )
            filtered.append(totals)
        for a in range(comps):
            for t in range(days):
                value = coupling[a][0] * filtered[0][t] + coupling[a][1] * filtered[1][t]
                yield a * days + order[t], value

    for edge_ref, packed_ref, (to_east, slot) in zip(
        edge_refs, packed_refs, edge_plan(place_ref, nb_ref)
    ):
        live = mask_ref[slot].astype(jnp.float32)
        packed = jnp.zeros((tiles, LANES), jnp.float32)
        for at, value in all_days(edge_ref, lambda ref, c, s: live * ref[c, s, :, slot, :]):
            shift = wrapped(jnp.where(to_east, LANES - SPACE_HALF * at, SPACE_HALF * at))
            spot = jnp.where(to_east, GROUPS - 1 - at, at)
            packed = jnp.where(group == spot, roll(value, shift), packed)
        packed_ref[...] = packed
    for strip_ref, sent_ref, start in zip(
        strip_refs, sent_refs, strip_starts(place_ref, tiles)
    ):
        for at, value in all_days(strip_ref, lambda ref, c, s: ref[c, s, pl.ds(start, PAIR_ROWS)]):
            sent_ref[at] = live_slots * value


def mix_kernel(pair, place_ref, mask_ref, taps_ref, factor_ref, own_ref, *rest):
    *other_refs, mixed_ref = rest
    _, tiles, slots, _ = mixed_ref.shape
    comps, days = other_refs[0].shape[:2]
    _, sublane = iotas(slots)
    live = live_vector(mask_ref, sublane)
    taps = taps_of(taps_ref)
    weights = [[live * value for value in row] for row in coupling_of(factor_ref)]
    order = order_of(pair, place_ref[1], days)

    def body(tile, _):
        filtered = []
        for comp in range(comps):
            totals = [own_ref[comp * days + order[t], tile] for t in range(days)]
            add_later(taps, totals, [other_refs[-1][comp, order[s], tile] for s in range(days)])
            if not pair:
                add_earlier(taps, totals, [other_refs[0][comp, s, tile] for s in range(days)])
            filtered.append(totals)
        for a in range(comps):
            for t in range(days):
                mixed_ref[a * days + order[t], tile] = (
                    weights[a][0] * filtered[0][t] + weights[a][1] * filtered[1][t]
                )
        return 0

    lax.fori_loop(0, tiles, body, 0, unroll=4)


def west_east(place_ref, first, second):
    flag = east_first(place_ref)
    return jnp.where(flag, second, first), jnp.where(flag, first, second)


def unpacked(item, west, east):
    column = jnp.bitwise_and(lax.broadcasted_iota(jnp.int32, west.shape, 1), SIDE - 1)
    return jnp.where(
        column >= SIDE // 2,
        roll(west, wrapped(SPACE_HALF * item)),
        roll(east, wrapped(LANES - SPACE_HALF * item)),
    )


def corner_kernel(place_ref, first_ref, second_ref, *refs):
    one_ref, two_ref = refs[-2:]
    slots = one_ref.shape[2]
    south = south_first(place_ref)
    for k, side in enumerate(west_east(place_ref, first_ref[...], second_ref[...])):
        top, bottom = side[:slots], side[-slots:]
        one_ref[0, k] = jnp.where(south, bottom, top)
        two_ref[0, k] = jnp.where(south, top, bottom)


def two_parts(x):
    coarse = x.astype(jnp.bfloat16)
    return coarse, (x - coarse.astype(jnp.float32)).astype(jnp.bfloat16)


def bands_kernel(taps_ref, bands_ref):
    shape = (2 * LANES, LANES)
    source = lax.broadcasted_iota(jnp.int32, shape, 0)
    target = lax.broadcasted_iota(jnp.int32, shape, 1)
    same = jnp.bitwise_and(source // SIDE, 1) == target // SIDE
    source_column = jnp.bitwise_and(source, SIDE - 1)
    outside = jnp.where(source_column >= SIDE // 2, source_column - SIDE, source_column + SIDE)
    position = jnp.where(source < LANES, source_column, outside)
    distance = jnp.abs(position - jnp.bitwise_and(target, SIDE - 1))
    bands = jnp.zeros(shape, jnp.float32)
    for lag in range(SPACE_HALF + 1):
        bands = jnp.where(same & (distance == lag), taps_ref[0, lag], bands)
    coarse, fine = two_parts(bands)
    bands_ref[: 2 * LANES, :LANES] = coarse
    bands_ref[: 2 * LANES, LANES:] = fine
    bands_ref[2 * LANES :, :LANES] = coarse
    bands_ref[2 * LANES :, LANES:] = jnp.zeros_like(fine)


def across(bands, tiles):
    slots = tiles[0][0].shape[0]
    centre_parts = two_parts(jnp.concatenate([centre for centre, _ in tiles], axis=0))
    halo_parts = two_parts(jnp.concatenate([halo for _, halo in tiles], axis=0))
    product = jnp.dot(
        jnp.concatenate([part for both in zip(centre_parts, halo_parts) for part in both], axis=1),
        bands,
        preferred_element_type=jnp.float32,
    )
    product = product[:, :LANES] + product[:, LANES:]
    return [product[slots * p : slots * (p + 1)] for p in range(len(tiles))]


def sides_of(nb, west, east, device, shape):
    slots = shape[0]
    column = jnp.bitwise_and(lax.broadcasted_iota(jnp.int32, shape, 1), SIDE - 1)
    target = jnp.where(column >= SIDE // 2, entry(nb, west, shape), entry(nb, east, shape))
    near = on_device(target, device, slots)
    return jnp.bitwise_and(target, slots - 1), near, (target >= 0) & ~near


def halo_of(source, far, plan):
    index, near, remote = plan
    halo = jnp.where(near, pick(source, index), 0.0)
    return jnp.where(remote, jnp.broadcast_to(far, halo.shape), halo)


def odd_rows(before, after):
    low = lax.broadcasted_iota(jnp.int32, before.shape, 1) < SIDE
    return roll(jnp.where(low, after, before), SIDE)


def inner_kernel(
    place_ref, mask_ref, taps_ref, nb_ref, bands_ref, mixed_ref, first_ref, second_ref,
    out_ref, outer_ref, far_ref,
):
    count, tiles, slots, _ = mixed_ref.shape
    lane, sublane = iotas(slots)
    live = live_vector(mask_ref, sublane)
    taps = [taps_ref[1, lag] for lag in range(SPACE_HALF + 1)]
    plan = sides_of(nb_ref[...], WEST, EAST, place_ref[0], lane.shape)
    west, east = west_east(place_ref, first_ref[...], second_ref[...])
    share = out_ref.shape[0]

    def body(step, _):
        item = pl.program_id(0) * share + step
        far_ref[...] = unpacked(item, west, east)
        fetched = []
        for tile in range(tiles):
            centre = mixed_ref[item, tile]
            fetched.append((centre, halo_of(centre, far_ref[tile : tile + 1], plan)))
        zero = jnp.zeros(lane.shape, jnp.float32)
        rows = [zero] * PAIR_ROWS + across(bands_ref[...], fetched) + [zero] * PAIR_ROWS
        odd = [odd_rows(rows[p], rows[p + 1]) for p in range(len(rows) - 1)]
        for p in range(tiles):
            total = taps[0] * rows[p + 2]
            total = total + taps[1] * (odd[p + 1] + odd[p + 2])
            total = total + taps[2] * (rows[p + 1] + rows[p + 3])
            total = total + taps[3] * (odd[p] + odd[p + 3])
            total = total + taps[4] * (rows[p] + rows[p + 4])
            total = live * total
            out_ref[step, p] = total
            if p < PAIR_ROWS:
                outer_ref[item, p] = total
            elif p >= tiles - PAIR_ROWS:
                outer_ref[item, p - tiles + 2 * PAIR_ROWS] = total
        return 0

    lax.fori_loop(0, share, body, 0)


def outer_kernel(
    place_ref, mask_ref, taps_ref, nb_ref, bands_ref, outer_ref, first_ref, second_ref,
    _, out_ref,
):
    count, _, slots, _ = outer_ref.shape
    lane, sublane = iotas(slots)
    live = live_vector(mask_ref, sublane)
    taps = [taps_ref[1, lag] for lag in range(SPACE_HALF + 1)]
    nb = nb_ref[...]
    me = place_ref[0]

    def one_side(north):
        use_first = ~south_first(place_ref) if north else south_first(place_ref)

        def read(index, part):
            return jnp.where(use_first, first_ref[index, part], second_ref[index, part])

        target = entry(nb, NORTH if north else SOUTH, lane.shape)
        plan = sides_of(
            nb,
            NORTH_WEST if north else SOUTH_WEST,
            NORTH_EAST if north else SOUTH_EAST,
            me - REACH if north else me + REACH,
            lane.shape,
        )
        corner = [read(count, 0), read(count, 1)]
        fetched = []
        for item in range(count):
            far = unpacked(jnp.int32(item), *corner)
            for part in range(PAIR_ROWS):
                source = read(item, part)
                centre = jnp.where(
                    target >= 0, pick(source, jnp.bitwise_and(target, slots - 1)), 0.0
                )
                row = slots - PAIR_ROWS + part if north else part
                fetched.append((centre, halo_of(source, far[row : row + 1], plan)))
        rows = across(bands_ref[...], fetched)
        zero = jnp.zeros(lane.shape, jnp.float32)
        for item in range(count):
            one, two = rows[PAIR_ROWS * item : PAIR_ROWS * (item + 1)]
            if north:
                edge = odd_rows(two, zero)
                near = taps[1] * edge + taps[2] * two + taps[3] * odd_rows(one, two)
                near = near + taps[4] * one
                off = taps[3] * edge + taps[4] * two
                out_ref[item, 0] = outer_ref[item, 0] + live * near
                out_ref[item, 1] = outer_ref[item, 1] + live * off
            else:
                edge = odd_rows(zero, one)
                near = taps[1] * edge + taps[2] * one + taps[3] * odd_rows(one, two)
                near = near + taps[4] * two
                off = taps[3] * edge + taps[4] * one
                out_ref[item, 0] = outer_ref[item, 2] + live * off
                out_ref[item, 1] = outer_ref[item, 3] + live * near

    pl.when(pl.program_id(0) == 0)(lambda: one_side(True))
    pl.when(pl.program_id(0) == 1)(lambda: one_side(False))


def swap_both(first, second, index, length):
    blk = lax.axis_size("blk")
    results = []
    for x, shift in ((first, 0), (second, 1)):
        partner = {}
        for at in range(shift, length + shift, 2):
            low, high = at % length, (at + 1) % length
            partner[low], partner[high] = high, low
        place = [index(i) for i in range(blk)]
        pairs = [(i, i + (partner[at] - at) * step) for i, (at, step) in enumerate(place)]
        results.append(lax.ppermute(x, "blk", pairs))
    return results


def shards(input_field, active_mask, neighbours, time_taps, space_taps, coregion_factor):
    comps, days, slots, cells = input_field.shape
    count = comps * days
    tiles = cells // LANES
    blk = lax.axis_size("blk")
    day = lax.axis_size("day")
    pair = day == 2
    sides = 2
    place = jnp.stack([lax.axis_index("blk"), lax.axis_index("day")]).astype(jnp.int32)

    def in_tiles(x):
        return x.reshape(comps, days, slots, tiles, LANES).transpose(0, 1, 3, 2, 4)

    if pair:
        others = [lax.ppermute(input_field, "day", [(0, 1), (1, 0)])]
    else:
        up = [(i, i + 1) for i in range(day - 1)]
        others = [
            lax.ppermute(input_field, "day", up),
            lax.ppermute(input_field, "day", [(b, a) for a, b in up]),
        ]
    others = [in_tiles(x) for x in others]
    field = array(count, tiles, slots, LANES)

    own, *raw = pl.pallas_call(
        own_kernel,
        out_shape=(field,)
        + (array(count, tiles, LANES),) * sides
        + (array(count, PAIR_ROWS, slots, LANES),) * sides,
        in_specs=[SMEM] * 5 + [WHOLE],
        out_specs=(WHOLE,) * (1 + 2 * sides),
        compiler_params=PARAMS,
        name="own_days",
    )(place, active_mask, time_taps, coregion_factor, neighbours, in_tiles(input_field))

    sent_count = count + 1
    sent_shape = array(sent_count, PAIR_ROWS, slots, LANES)
    packed_and_sent = pl.pallas_call(
        functools.partial(send_kernel, pair),
        out_shape=(array(tiles, LANES),) * sides + (sent_shape,) * sides,
        in_specs=[SMEM] * 5 + [WHOLE] * (len(raw) + len(others)),
        out_specs=(WHOLE,) * (2 * sides),
        compiler_params=PARAMS,
        name="edges_and_strips",
    )(place, active_mask, time_taps, coregion_factor, neighbours, *raw, *others)
    packed, sent = packed_and_sent[:sides], packed_and_sent[sides:]

    first, second = swap_both(*packed, lambda i: (i % REACH, 1), REACH)

    mixed = pl.pallas_call(
        functools.partial(mix_kernel, pair),
        out_shape=field,
        in_specs=[SMEM] * 4 + [WHOLE] * (1 + len(others)),
        out_specs=WHOLE,
        compiler_params=PARAMS,
        cost_estimate=pl.CostEstimate(
            flops=20 * field.size, bytes_accessed=12 * field.size, transcendentals=0
        ),
        name="mix",
    )(place, active_mask, time_taps, coregion_factor, own, *others)

    bands = pl.pallas_call(
        bands_kernel,
        out_shape=jax.ShapeDtypeStruct((4 * LANES, 2 * LANES), jnp.bfloat16),
        in_specs=[SMEM],
        out_specs=WHOLE,
        compiler_params=PARAMS,
        name="bands",
    )(space_taps)

    sent = pl.pallas_call(
        corner_kernel,
        grid=(1,),
        out_shape=(sent_shape,) * sides,
        in_specs=[SMEM, WHOLE, WHOLE] + [pl.BlockSpec(memory_space=pl.ANY)] * (sides + 2),
        out_specs=(
            pl.BlockSpec((1, PAIR_ROWS, slots, LANES), lambda i: (sent_count - 1, 0, 0, 0)),
        )
        * sides,
        input_output_aliases={5 + side: side for side in range(sides)},
        compiler_params=PARAMS,
        name="corners",
    )(place, first, second, mixed, bands, *sent)

    one, two = swap_both(*sent, lambda i: (i // REACH, REACH), blk // REACH)

    steps = 6
    inner, outer = pl.pallas_call(
        inner_kernel,
        grid=(steps,),
        out_shape=(field, array(count, 2 * PAIR_ROWS, slots, LANES)),
        in_specs=[SMEM] * 3 + [WHOLE] * 5,
        out_specs=(
            pl.BlockSpec((count // steps, tiles, slots, LANES), lambda i: (i, 0, 0, 0)),
            pl.BlockSpec((count, 2 * PAIR_ROWS, slots, LANES), lambda i: (0, 0, 0, 0)),
        ),
        scratch_shapes=[pltpu.VMEM((tiles, LANES), jnp.float32)],
        compiler_params=PARAMS,
        cost_estimate=pl.CostEstimate(
            flops=4 * field.size * LANES, bytes_accessed=8 * field.size, transcendentals=0
        ),
        name="inner_rows",
    )(place, active_mask, space_taps, neighbours, bands, mixed, first, second)

    last = tiles // PAIR_ROWS - 1
    result = pl.pallas_call(
        outer_kernel,
        grid=(2,),
        out_shape=field,
        in_specs=[SMEM] * 3 + [WHOLE] * 5 + [pl.BlockSpec(memory_space=pl.ANY)],
        out_specs=pl.BlockSpec((count, PAIR_ROWS, slots, LANES), lambda i: (0, i * last, 0, 0)),
        input_output_aliases={8: 0},
        compiler_params=PARAMS,
        name="outer_rows",
    )(place, active_mask, space_taps, neighbours, bands, outer, one, two, inner)
    result = result.reshape(comps, days, tiles, slots, LANES).transpose(0, 1, 3, 2, 4)
    return result.reshape(input_field.shape)


def solution(mesh):
    in_specs = (P(None, "day", "blk", None), P("blk"), P("blk", None), P(), P(), P())
    out_specs = P(None, "day", "blk", None)
    return jax.shard_map(shards, mesh=mesh, in_specs=in_specs, out_specs=out_specs, check_vma=False)
```

```python
import functools

import jax
import jax.numpy as jnp
from jax import lax
from jax.experimental import pallas as pl
from jax.experimental.pallas import tpu as pltpu
from jax.sharding import PartitionSpec as P

SIDE = 64
SPACE_HALF = 4
TIME_HALF = 3
REACH = 4
LANES = 128
EAST, WEST, NORTH, SOUTH, NORTH_EAST, NORTH_WEST, SOUTH_EAST, SOUTH_WEST = range(8)
PAIR_ROWS = SPACE_HALF * SIDE // LANES
GROUPS = SIDE // SPACE_HALF
PARAMS = pltpu.CompilerParams(vmem_limit_bytes=12 * 1024 * 1024)
SMEM = pl.BlockSpec(memory_space=pltpu.SMEM)
WHOLE = pl.BlockSpec(memory_space=pltpu.VMEM)
IN_HBM = pl.BlockSpec(memory_space=pltpu.HBM)
DMA = pltpu.SemaphoreType.DMA


def array(*shape):
    return jax.ShapeDtypeStruct(shape, jnp.float32)


def iotas(slots):
    lane = lax.broadcasted_iota(jnp.int32, (slots, LANES), 1)
    sublane = lax.broadcasted_iota(jnp.int32, (slots, LANES), 0)
    return lane, sublane


def live_vector(mask_ref, sublane):
    live = jnp.zeros(sublane.shape, jnp.float32)
    for slot in range(sublane.shape[0]):
        live = jnp.where(sublane == slot, mask_ref[slot].astype(jnp.float32), live)
    return live


def entry(neighbours, direction, shape):
    return jnp.broadcast_to(neighbours[:, direction : direction + 1], shape)


def pick(source, index):
    return jnp.take_along_axis(source, index, axis=0)


def roll(x, shift):
    return pltpu.roll(x, shift % LANES if isinstance(shift, int) else shift, 1)


def wrapped(shift):
    return jnp.bitwise_and(shift, LANES - 1)


def device_of(target, slots):
    return lax.shift_right_arithmetic(target, jnp.int32(slots.bit_length() - 1))


def on_device(target, device, slots):
    return (target >= 0) & (device_of(target, slots) == device)


def taps_of(taps_ref):
    return [taps_ref[lag] for lag in range(TIME_HALF + 1)]


def order_of(pair, day, days):
    return [day * (days - 1 - 2 * s) + s if pair else s for s in range(days)]


def coupling_of(factor_ref):
    return [
        [
            factor_ref[a, 0] * factor_ref[b, 0] + factor_ref[a, 1] * factor_ref[b, 1]
            for b in range(2)
        ]
        for a in range(2)
    ]


def same_days(taps, values):
    totals = []
    for t in range(len(values)):
        total = taps[0] * values[t]
        for s in range(len(values)):
            if s != t:
                total = total + taps[abs(s - t)] * values[s]
        totals.append(total)
    return totals


def add_later(taps, totals, values):
    for t in range(len(totals)):
        for s in range(t + 1):
            totals[t] = totals[t] + taps[len(totals) + s - t] * values[s]


def add_earlier(taps, totals, values):
    for t in range(len(totals)):
        for s in range(t, len(totals)):
            totals[t] = totals[t] + taps[len(totals) + t - s] * values[s]


def east_first(place_ref):
    return jnp.bitwise_and(place_ref[0], 1) == 0


def south_first(place_ref):
    return jnp.bitwise_and(place_ref[0], REACH) == 0


def end_slot(nb_ref, me, east):
    slots = nb_ref.shape[0]
    step, directions = (
        (1, (EAST, NORTH_EAST, SOUTH_EAST)) if east else (-1, (WEST, NORTH_WEST, SOUTH_WEST))
    )
    found = jnp.int32(0)
    for slot in range(slots):
        for direction, shift in zip(directions, (0, -REACH, REACH)):
            target = nb_ref[slot, direction]
            hit = (target >= 0) & (device_of(target, slots) == me + step + shift)
            found = jnp.where(hit, slot, found)
    return found


def edge_plan(place_ref, ends_ref):
    first = east_first(place_ref)
    return [(first, ends_ref[0]), (~first, ends_ref[1])]


def strip_starts(place_ref, tiles):
    last = tiles - PAIR_ROWS
    first = south_first(place_ref)
    return [jnp.where(first, last, 0), jnp.where(first, 0, last)]


def own_kernel(place_ref, mask_ref, taps_ref, _, nb_ref, x_hbm, *refs):
    own_ref, ends_ref, *rest, x_ref, arrived = refs
    comps, days, tiles, slots, _ = x_ref.shape
    copies = [
        [
            pltpu.make_async_copy(x_hbm.at[comp, t], x_ref.at[comp, t], arrived.at[comp, t])
            for t in range(days)
        ]
        for comp in range(comps)
    ]
    for row in copies:
        for copy in row:
            copy.start()
    edge_refs, strip_refs = rest[: len(rest) // 2], rest[len(rest) // 2 :]
    taps = taps_of(taps_ref)
    me = place_ref[0]
    east, west = end_slot(nb_ref, me, True), end_slot(nb_ref, me, False)
    first = east_first(place_ref)
    ends = [jnp.where(first, east, west), jnp.where(first, west, east)]
    for k, slot in enumerate(ends):
        ends_ref[k] = slot
    for comp in range(comps):
        for copy in copies[comp]:
            copy.wait()
        for edge_ref, slot in zip(edge_refs, ends):
            live = mask_ref[slot].astype(jnp.float32)
            for t in range(days):
                edge_ref[comp * days + t] = live * x_ref[comp, t, :, slot, :]
        for strip_ref, start in zip(strip_refs, strip_starts(place_ref, tiles)):
            for t in range(days):
                strip_ref[comp * days + t] = x_ref[comp, t, pl.ds(start, PAIR_ROWS)]

        def body(tile, _, comp=comp):
            values = [x_ref[comp, t, tile] for t in range(days)]
            for t, total in enumerate(same_days(taps, values)):
                own_ref[comp * days + t, tile] = total
            return 0

        lax.fori_loop(0, tiles, body, 0, unroll=8)


def send_kernel(pair, place_ref, mask_ref, taps_ref, factor_ref, ends_ref, *refs):
    sides = 2
    edge_refs, strip_refs = refs[:sides], refs[sides : 2 * sides]
    other_refs = refs[2 * sides : len(refs) - 2 * sides]
    packed_refs = refs[len(refs) - 2 * sides : len(refs) - sides]
    sent_refs = refs[len(refs) - sides :]
    comps, days, tiles, slots, _ = other_refs[0].shape
    lane, sublane = iotas(slots)
    group = jnp.bitwise_and(lax.broadcasted_iota(jnp.int32, (tiles, LANES), 1), SIDE - 1)
    group = group // SPACE_HALF
    live_slots = live_vector(mask_ref, sublane)
    taps = taps_of(taps_ref)
    coupling = coupling_of(factor_ref)
    order = order_of(pair, place_ref[1], days)

    def all_days(raw_ref, read_other):
        filtered = []
        for comp in range(comps):
            values = [raw_ref[comp * days + order[s]] for s in range(days)]
            later = [read_other(other_refs[-1], comp, order[s]) for s in range(days)]
            totals = same_days(taps, values)
            add_later(taps, totals, later)
            if not pair:
                add_earlier(
                    taps, totals, [read_other(other_refs[0], comp, s) for s in range(days)]
                )
            filtered.append(totals)
        for a in range(comps):
            for t in range(days):
                value = coupling[a][0] * filtered[0][t] + coupling[a][1] * filtered[1][t]
                yield a * days + order[t], value

    for edge_ref, packed_ref, (to_east, slot) in zip(
        edge_refs, packed_refs, edge_plan(place_ref, ends_ref)
    ):
        live = mask_ref[slot].astype(jnp.float32)
        packed = jnp.zeros((tiles, LANES), jnp.float32)
        for at, value in all_days(edge_ref, lambda ref, c, s: live * ref[c, s, :, slot, :]):
            shift = wrapped(jnp.where(to_east, LANES - SPACE_HALF * at, SPACE_HALF * at))
            spot = jnp.where(to_east, GROUPS - 1 - at, at)
            packed = jnp.where(group == spot, roll(value, shift), packed)
        packed_ref[...] = packed
    for strip_ref, sent_ref, start in zip(
        strip_refs, sent_refs, strip_starts(place_ref, tiles)
    ):
        for at, value in all_days(strip_ref, lambda ref, c, s: ref[c, s, pl.ds(start, PAIR_ROWS)]):
            sent_ref[at] = live_slots * value


def mix_kernel(pair, place_ref, mask_ref, taps_ref, factor_ref, own_ref, *rest):
    *other_refs, mixed_ref = rest
    _, tiles, slots, _ = mixed_ref.shape
    comps, days = other_refs[0].shape[:2]
    _, sublane = iotas(slots)
    live = live_vector(mask_ref, sublane)
    taps = taps_of(taps_ref)
    weights = [[live * value for value in row] for row in coupling_of(factor_ref)]
    order = order_of(pair, place_ref[1], days)

    def body(tile, _):
        filtered = []
        for comp in range(comps):
            totals = [own_ref[comp * days + order[t], tile] for t in range(days)]
            add_later(taps, totals, [other_refs[-1][comp, order[s], tile] for s in range(days)])
            if not pair:
                add_earlier(taps, totals, [other_refs[0][comp, s, tile] for s in range(days)])
            filtered.append(totals)
        for a in range(comps):
            for t in range(days):
                mixed_ref[a * days + order[t], tile] = (
                    weights[a][0] * filtered[0][t] + weights[a][1] * filtered[1][t]
                )
        return 0

    lax.fori_loop(0, tiles, body, 0, unroll=4)


def west_east(place_ref, first, second):
    flag = east_first(place_ref)
    return jnp.where(flag, second, first), jnp.where(flag, first, second)


def unpacked(item, west, east):
    column = jnp.bitwise_and(lax.broadcasted_iota(jnp.int32, west.shape, 1), SIDE - 1)
    return jnp.where(
        column >= SIDE // 2,
        roll(west, wrapped(SPACE_HALF * item)),
        roll(east, wrapped(LANES - SPACE_HALF * item)),
    )


def corner_kernel(place_ref, first_ref, second_ref, *refs):
    one_ref, two_ref = refs[-2:]
    slots = one_ref.shape[2]
    south = south_first(place_ref)
    for k, side in enumerate(west_east(place_ref, first_ref[...], second_ref[...])):
        top, bottom = side[:slots], side[-slots:]
        one_ref[0, k] = jnp.where(south, bottom, top)
        two_ref[0, k] = jnp.where(south, top, bottom)


def two_parts(x):
    coarse = x.astype(jnp.bfloat16)
    return coarse, (x - coarse.astype(jnp.float32)).astype(jnp.bfloat16)


def bands_kernel(taps_ref, bands_ref):
    shape = (2 * LANES, LANES)
    source = lax.broadcasted_iota(jnp.int32, shape, 0)
    target = lax.broadcasted_iota(jnp.int32, shape, 1)
    same = jnp.bitwise_and(source // SIDE, 1) == target // SIDE
    source_column = jnp.bitwise_and(source, SIDE - 1)
    outside = jnp.where(source_column >= SIDE // 2, source_column - SIDE, source_column + SIDE)
    position = jnp.where(source < LANES, source_column, outside)
    distance = jnp.abs(position - jnp.bitwise_and(target, SIDE - 1))
    bands = jnp.zeros(shape, jnp.float32)
    for lag in range(SPACE_HALF + 1):
        bands = jnp.where(same & (distance == lag), taps_ref[0, lag], bands)
    coarse, fine = two_parts(bands)
    bands_ref[: 2 * LANES, :LANES] = coarse
    bands_ref[: 2 * LANES, LANES:] = fine
    bands_ref[2 * LANES :, :LANES] = coarse
    bands_ref[2 * LANES :, LANES:] = jnp.zeros_like(fine)


def across(bands, tiles):
    slots = tiles[0][0].shape[0]
    centre_parts = two_parts(jnp.concatenate([centre for centre, _ in tiles], axis=0))
    halo_parts = two_parts(jnp.concatenate([halo for _, halo in tiles], axis=0))
    product = jnp.dot(
        jnp.concatenate([part for both in zip(centre_parts, halo_parts) for part in both], axis=1),
        bands,
        preferred_element_type=jnp.float32,
    )
    product = product[:, :LANES] + product[:, LANES:]
    return [product[slots * p : slots * (p + 1)] for p in range(len(tiles))]


def sides_of(nb, west, east, device, shape):
    slots = shape[0]
    column = jnp.bitwise_and(lax.broadcasted_iota(jnp.int32, shape, 1), SIDE - 1)
    target = jnp.where(column >= SIDE // 2, entry(nb, west, shape), entry(nb, east, shape))
    near = on_device(target, device, slots)
    return jnp.bitwise_and(target, slots - 1), near, (target >= 0) & ~near


def halo_of(source, far, plan):
    index, near, remote = plan
    halo = jnp.where(near, pick(source, index), 0.0)
    return jnp.where(remote, jnp.broadcast_to(far, halo.shape), halo)


def odd_rows(before, after):
    low = lax.broadcasted_iota(jnp.int32, before.shape, 1) < SIDE
    return roll(jnp.where(low, after, before), SIDE)


def inner_kernel(
    place_ref, mask_ref, taps_ref, nb_ref, bands_ref, mixed_ref, first_ref, second_ref,
    out_hbm, outer_ref, out_ref, far_ref, stored,
):
    count, tiles, slots, _ = mixed_ref.shape
    lane, sublane = iotas(slots)
    live = live_vector(mask_ref, sublane)
    taps = [taps_ref[1, lag] for lag in range(SPACE_HALF + 1)]
    plan = sides_of(nb_ref[...], WEST, EAST, place_ref[0], lane.shape)
    west, east = west_east(place_ref, first_ref[...], second_ref[...])
    together = far_ref.shape[0]

    def store(step):
        part = pl.ds(step * together, together)
        return pltpu.make_async_copy(out_ref.at[part], out_hbm.at[part], stored.at[step])

    def body(step, _):
        fetched = []
        for k in range(together):
            item = step * together + k
            far_ref[k] = unpacked(item, west, east)
            for tile in range(tiles):
                centre = mixed_ref[item, tile]
                fetched.append((centre, halo_of(centre, far_ref[k, tile : tile + 1], plan)))
        lines = across(bands_ref[...], fetched)
        zero = jnp.zeros(lane.shape, jnp.float32)
        for k in range(together):
            item = step * together + k
            rows = [zero] * PAIR_ROWS + lines[k * tiles : (k + 1) * tiles] + [zero] * PAIR_ROWS
            odd = [odd_rows(rows[p], rows[p + 1]) for p in range(len(rows) - 1)]
            for p in range(tiles):
                total = taps[0] * rows[p + 2]
                total = total + taps[1] * (odd[p + 1] + odd[p + 2])
                total = total + taps[2] * (rows[p + 1] + rows[p + 3])
                total = total + taps[3] * (odd[p] + odd[p + 3])
                total = total + taps[4] * (rows[p] + rows[p + 4])
                total = live * total
                out_ref[item, p] = total
                if p < PAIR_ROWS:
                    outer_ref[item, p] = total
                elif p >= tiles - PAIR_ROWS:
                    outer_ref[item, p - tiles + 2 * PAIR_ROWS] = total
        store(step).start()
        return 0

    lax.fori_loop(0, count // together, body, 0)
    for step in range(count // together):
        store(step).wait()


def outer_kernel(
    place_ref, mask_ref, taps_ref, nb_ref, bands_ref, outer_ref, first_ref, second_ref,
    _, out_hbm, out_ref, stored,
):
    count, _, slots, _ = outer_ref.shape
    tiles = out_hbm.shape[1]
    lane, sublane = iotas(slots)
    live = live_vector(mask_ref, sublane)
    taps = [taps_ref[1, lag] for lag in range(SPACE_HALF + 1)]
    nb = nb_ref[...]
    me = place_ref[0]
    fetched = []
    for north in (True, False):
        use_first = ~south_first(place_ref) if north else south_first(place_ref)

        def read(index, part, use_first=use_first):
            return jnp.where(use_first, first_ref[index, part], second_ref[index, part])

        target = entry(nb, NORTH if north else SOUTH, lane.shape)
        plan = sides_of(
            nb,
            NORTH_WEST if north else SOUTH_WEST,
            NORTH_EAST if north else SOUTH_EAST,
            me - REACH if north else me + REACH,
            lane.shape,
        )
        corner = [read(count, 0), read(count, 1)]
        for item in range(count):
            far = unpacked(jnp.int32(item), *corner)
            for part in range(PAIR_ROWS):
                source = read(item, part)
                centre = jnp.where(
                    target >= 0, pick(source, jnp.bitwise_and(target, slots - 1)), 0.0
                )
                row = slots - PAIR_ROWS + part if north else part
                fetched.append((centre, halo_of(source, far[row : row + 1], plan)))
    rows = across(bands_ref[...], fetched)
    zero = jnp.zeros(lane.shape, jnp.float32)
    copies = []
    for side in range(2):
        for item in range(count):
            at = (side * count + item) * PAIR_ROWS
            one, two = rows[at : at + PAIR_ROWS]
            close, far = (one, two) if side else (two, one)
            edge = odd_rows(zero, one) if side else odd_rows(two, zero)
            near = taps[1] * edge + taps[2] * close + taps[3] * odd_rows(one, two)
            near = near + taps[4] * far
            off = taps[3] * edge + taps[4] * close
            for part, value in enumerate((off, near) if side else (near, off)):
                out_ref[side, item, part] = (
                    outer_ref[item, side * PAIR_ROWS + part] + live * value
                )
        place = pl.ds(side * (tiles - PAIR_ROWS), PAIR_ROWS)
        copy = pltpu.make_async_copy(out_ref.at[side], out_hbm.at[:, place], stored.at[side])
        copy.start()
        copies.append(copy)
    for copy in copies:
        copy.wait()


def swap_both(first, second, index, length):
    blk = lax.axis_size("blk")
    results = []
    for x, shift in ((second, 1), (first, 0)):
        partner = {}
        for at in range(shift, length + shift, 2):
            low, high = at % length, (at + 1) % length
            partner[low], partner[high] = high, low
        place = [index(i) for i in range(blk)]
        pairs = [(i, i + (partner[at] - at) * step) for i, (at, step) in enumerate(place)]
        results.append(lax.ppermute(x, "blk", pairs))
    return results[::-1]


def shards(input_field, active_mask, neighbours, time_taps, space_taps, coregion_factor):
    comps, days, slots, cells = input_field.shape
    count = comps * days
    tiles = cells // LANES
    blk = lax.axis_size("blk")
    day = lax.axis_size("day")
    pair = day == 2
    sides = 2
    place = jnp.stack([lax.axis_index("blk"), lax.axis_index("day")]).astype(jnp.int32)

    def in_tiles(x):
        return x.reshape(comps, days, slots, tiles, LANES).transpose(0, 1, 3, 2, 4)

    if pair:
        others = [lax.ppermute(input_field, "day", [(0, 1), (1, 0)])]
    else:
        up = [(i, i + 1) for i in range(day - 1)]
        others = [
            lax.ppermute(input_field, "day", up),
            lax.ppermute(input_field, "day", [(b, a) for a, b in up]),
        ]
    others = [in_tiles(x) for x in others]
    field = array(count, tiles, slots, LANES)

    own, ends, *raw = pl.pallas_call(
        own_kernel,
        out_shape=(field, jax.ShapeDtypeStruct((2,), jnp.int32))
        + (array(count, tiles, LANES),) * sides
        + (array(count, PAIR_ROWS, slots, LANES),) * sides,
        in_specs=[SMEM] * 5 + [IN_HBM],
        out_specs=(WHOLE, SMEM) + (WHOLE,) * (2 * sides),
        scratch_shapes=[
            pltpu.VMEM((comps, days, tiles, slots, LANES), jnp.float32),
            DMA((comps, days)),
        ],
        compiler_params=PARAMS,
        name="own_days",
    )(place, active_mask, time_taps, coregion_factor, neighbours, in_tiles(input_field))

    sent_count = count + 1
    sent_shape = array(sent_count, PAIR_ROWS, slots, LANES)
    packed_and_sent = pl.pallas_call(
        functools.partial(send_kernel, pair),
        out_shape=(array(tiles, LANES),) * sides + (sent_shape,) * sides,
        in_specs=[SMEM] * 5 + [WHOLE] * (len(raw) + len(others)),
        out_specs=(WHOLE,) * (2 * sides),
        compiler_params=PARAMS,
        name="edges_and_strips",
    )(place, active_mask, time_taps, coregion_factor, ends, *raw, *others)
    packed, sent = packed_and_sent[:sides], packed_and_sent[sides:]

    first, second = swap_both(*packed, lambda i: (i % REACH, 1), REACH)

    mixed = pl.pallas_call(
        functools.partial(mix_kernel, pair),
        out_shape=field,
        in_specs=[SMEM] * 4 + [WHOLE] * (1 + len(others)),
        out_specs=WHOLE,
        compiler_params=PARAMS,
        cost_estimate=pl.CostEstimate(
            flops=20 * field.size, bytes_accessed=12 * field.size, transcendentals=0
        ),
        name="mix",
    )(place, active_mask, time_taps, coregion_factor, own, *others)

    bands = pl.pallas_call(
        bands_kernel,
        out_shape=jax.ShapeDtypeStruct((4 * LANES, 2 * LANES), jnp.bfloat16),
        in_specs=[SMEM],
        out_specs=WHOLE,
        compiler_params=PARAMS,
        name="bands",
    )(space_taps)

    sent = pl.pallas_call(
        corner_kernel,
        grid=(1,),
        out_shape=(sent_shape,) * sides,
        in_specs=[SMEM, WHOLE, WHOLE] + [pl.BlockSpec(memory_space=pl.ANY)] * (sides + 2),
        out_specs=(
            pl.BlockSpec((1, PAIR_ROWS, slots, LANES), lambda i: (sent_count - 1, 0, 0, 0)),
        )
        * sides,
        input_output_aliases={5 + side: side for side in range(sides)},
        compiler_params=PARAMS,
        name="corners",
    )(place, first, second, mixed, bands, *sent)

    one, two = swap_both(*sent, lambda i: (i // REACH, REACH), blk // REACH)

    together = 2
    inner, outer = pl.pallas_call(
        inner_kernel,
        out_shape=(field, array(count, 2 * PAIR_ROWS, slots, LANES)),
        in_specs=[SMEM] * 3 + [WHOLE] * 5,
        out_specs=(IN_HBM, WHOLE),
        scratch_shapes=[
            pltpu.VMEM(field.shape, jnp.float32),
            pltpu.VMEM((together, tiles, LANES), jnp.float32),
            DMA((count // together,)),
        ],
        compiler_params=PARAMS,
        cost_estimate=pl.CostEstimate(
            flops=4 * field.size * LANES, bytes_accessed=8 * field.size, transcendentals=0
        ),
        name="inner_rows",
    )(place, active_mask, space_taps, neighbours, bands, mixed, first, second)

    result = pl.pallas_call(
        outer_kernel,
        out_shape=field,
        in_specs=[SMEM] * 3 + [WHOLE] * 5 + [IN_HBM],
        out_specs=IN_HBM,
        scratch_shapes=[
            pltpu.VMEM((2, count, PAIR_ROWS, slots, LANES), jnp.float32),
            DMA((2,)),
        ],
        input_output_aliases={8: 0},
        compiler_params=PARAMS,
        name="outer_rows",
    )(place, active_mask, space_taps, neighbours, bands, outer, one, two, inner)
    result = result.reshape(comps, days, tiles, slots, LANES).transpose(0, 1, 3, 2, 4)
    return result.reshape(input_field.shape)


def solution(mesh):
    in_specs = (P(None, "day", "blk", None), P("blk"), P("blk", None), P(), P(), P())
    out_specs = P(None, "day", "blk", None)
    return jax.shard_map(shards, mesh=mesh, in_specs=in_specs, out_specs=out_specs, check_vma=False)
```

```python
import functools

import jax
import jax.numpy as jnp
from jax import lax
from jax.experimental import pallas as pl
from jax.experimental.pallas import tpu as pltpu
from jax.sharding import PartitionSpec as P

SIDE = 64
SPACE_HALF = 4
TIME_HALF = 3
REACH = 4
LANES = 128
EAST, WEST, NORTH, SOUTH, NORTH_EAST, NORTH_WEST, SOUTH_EAST, SOUTH_WEST = range(8)
PAIR_ROWS = SPACE_HALF * SIDE // LANES
GROUPS = SIDE // SPACE_HALF
PARAMS = pltpu.CompilerParams(vmem_limit_bytes=12 * 1024 * 1024)
SMEM = pl.BlockSpec(memory_space=pltpu.SMEM)
WHOLE = pl.BlockSpec(memory_space=pltpu.VMEM)
IN_HBM = pl.BlockSpec(memory_space=pltpu.HBM)
DMA = pltpu.SemaphoreType.DMA


def array(*shape):
    return jax.ShapeDtypeStruct(shape, jnp.float32)


def iotas(slots):
    lane = lax.broadcasted_iota(jnp.int32, (slots, LANES), 1)
    sublane = lax.broadcasted_iota(jnp.int32, (slots, LANES), 0)
    return lane, sublane


def live_vector(mask_ref, sublane):
    live = jnp.zeros(sublane.shape, jnp.float32)
    for slot in range(sublane.shape[0]):
        live = jnp.where(sublane == slot, mask_ref[slot].astype(jnp.float32), live)
    return live


def entry(neighbours, direction, shape):
    return jnp.broadcast_to(neighbours[:, direction : direction + 1], shape)


def pick(source, index):
    return jnp.take_along_axis(source, index, axis=0)


def roll(x, shift):
    return pltpu.roll(x, shift % LANES if isinstance(shift, int) else shift, 1)


def wrapped(shift):
    return jnp.bitwise_and(shift, LANES - 1)


def device_of(target, slots):
    return lax.shift_right_arithmetic(target, jnp.int32(slots.bit_length() - 1))


def on_device(target, device, slots):
    return (target >= 0) & (device_of(target, slots) == device)


def taps_of(taps_ref):
    return [taps_ref[lag] for lag in range(TIME_HALF + 1)]


def order_of(pair, day, days):
    return [day * (days - 1 - 2 * s) + s if pair else s for s in range(days)]


def coupling_of(factor_ref):
    return [
        [
            factor_ref[a, 0] * factor_ref[b, 0] + factor_ref[a, 1] * factor_ref[b, 1]
            for b in range(2)
        ]
        for a in range(2)
    ]


def same_days(taps, values):
    totals = []
    for t in range(len(values)):
        total = taps[0] * values[t]
        for s in range(len(values)):
            if s != t:
                total = total + taps[abs(s - t)] * values[s]
        totals.append(total)
    return totals


def add_later(taps, totals, values):
    for t in range(len(totals)):
        for s in range(t + 1):
            totals[t] = totals[t] + taps[len(totals) + s - t] * values[s]


def add_earlier(taps, totals, values):
    for t in range(len(totals)):
        for s in range(t, len(totals)):
            totals[t] = totals[t] + taps[len(totals) + t - s] * values[s]


def east_first(place_ref):
    return jnp.bitwise_and(place_ref[0], 1) == 0


def south_first(place_ref):
    return jnp.bitwise_and(place_ref[0], REACH) == 0


def end_slot(nb_ref, me, east):
    slots = nb_ref.shape[0]
    step, directions = (
        (1, (EAST, NORTH_EAST, SOUTH_EAST)) if east else (-1, (WEST, NORTH_WEST, SOUTH_WEST))
    )
    found = jnp.int32(0)
    for slot in range(slots):
        for direction, shift in zip(directions, (0, -REACH, REACH)):
            target = nb_ref[slot, direction]
            hit = (target >= 0) & (device_of(target, slots) == me + step + shift)
            found = jnp.where(hit, slot, found)
    return found


def edge_plan(place_ref, ends_ref):
    first = east_first(place_ref)
    return [(first, ends_ref[0]), (~first, ends_ref[1])]


def strip_starts(place_ref, tiles):
    last = tiles - PAIR_ROWS
    first = south_first(place_ref)
    return [jnp.where(first, last, 0), jnp.where(first, 0, last)]


def own_kernel(place_ref, mask_ref, taps_ref, _, nb_ref, x_ref, own_ref, ends_ref, *rest):
    comps, days, tiles, slots, _ = x_ref.shape
    edge_refs, strip_refs = rest[: len(rest) // 2], rest[len(rest) // 2 :]
    taps = taps_of(taps_ref)
    me = place_ref[0]
    east, west = end_slot(nb_ref, me, True), end_slot(nb_ref, me, False)
    first = east_first(place_ref)
    ends = [jnp.where(first, east, west), jnp.where(first, west, east)]
    for k, slot in enumerate(ends):
        ends_ref[k] = slot
    for edge_ref, slot in zip(edge_refs, ends):
        live = mask_ref[slot].astype(jnp.float32)
        for comp in range(comps):
            for t in range(days):
                edge_ref[comp * days + t] = live * x_ref[comp, t, :, slot, :]
    for strip_ref, start in zip(strip_refs, strip_starts(place_ref, tiles)):
        for comp in range(comps):
            for t in range(days):
                strip_ref[comp * days + t] = x_ref[comp, t, pl.ds(start, PAIR_ROWS)]

    def body(tile, _):
        for comp in range(comps):
            values = [x_ref[comp, t, tile] for t in range(days)]
            for t, total in enumerate(same_days(taps, values)):
                own_ref[comp * days + t, tile] = total
        return 0

    lax.fori_loop(0, tiles, body, 0, unroll=8)


def send_kernel(pair, place_ref, mask_ref, taps_ref, factor_ref, ends_ref, *refs):
    sides = 2
    edge_refs, strip_refs = refs[:sides], refs[sides : 2 * sides]
    other_refs = refs[2 * sides : len(refs) - 2 * sides]
    packed_refs = refs[len(refs) - 2 * sides : len(refs) - sides]
    sent_refs = refs[len(refs) - sides :]
    comps, days, tiles, slots, _ = other_refs[0].shape
    lane, sublane = iotas(slots)
    group = jnp.bitwise_and(lax.broadcasted_iota(jnp.int32, (tiles, LANES), 1), SIDE - 1)
    group = group // SPACE_HALF
    live_slots = live_vector(mask_ref, sublane)
    taps = taps_of(taps_ref)
    coupling = coupling_of(factor_ref)
    order = order_of(pair, place_ref[1], days)

    def all_days(raw_ref, read_other):
        filtered = []
        for comp in range(comps):
            values = [raw_ref[comp * days + order[s]] for s in range(days)]
            later = [read_other(other_refs[-1], comp, order[s]) for s in range(days)]
            totals = same_days(taps, values)
            add_later(taps, totals, later)
            if not pair:
                add_earlier(
                    taps, totals, [read_other(other_refs[0], comp, s) for s in range(days)]
                )
            filtered.append(totals)
        for a in range(comps):
            for t in range(days):
                value = coupling[a][0] * filtered[0][t] + coupling[a][1] * filtered[1][t]
                yield a * days + order[t], value

    for edge_ref, packed_ref, (to_east, slot) in zip(
        edge_refs, packed_refs, edge_plan(place_ref, ends_ref)
    ):
        live = mask_ref[slot].astype(jnp.float32)
        packed = jnp.zeros((tiles, LANES), jnp.float32)
        for at, value in all_days(edge_ref, lambda ref, c, s: live * ref[c, s, :, slot, :]):
            shift = wrapped(jnp.where(to_east, LANES - SPACE_HALF * at, SPACE_HALF * at))
            spot = jnp.where(to_east, GROUPS - 1 - at, at)
            packed = jnp.where(group == spot, roll(value, shift), packed)
        packed_ref[...] = packed
    for strip_ref, sent_ref, start in zip(
        strip_refs, sent_refs, strip_starts(place_ref, tiles)
    ):
        for at, value in all_days(strip_ref, lambda ref, c, s: ref[c, s, pl.ds(start, PAIR_ROWS)]):
            sent_ref[at] = live_slots * value


def mix_kernel(pair, place_ref, mask_ref, taps_ref, factor_ref, own_ref, *rest):
    *other_refs, mixed_ref = rest
    _, tiles, slots, _ = mixed_ref.shape
    comps, days = other_refs[0].shape[:2]
    _, sublane = iotas(slots)
    live = live_vector(mask_ref, sublane)
    taps = taps_of(taps_ref)
    weights = [[live * value for value in row] for row in coupling_of(factor_ref)]
    order = order_of(pair, place_ref[1], days)

    def body(tile, _):
        filtered = []
        for comp in range(comps):
            totals = [own_ref[comp * days + order[t], tile] for t in range(days)]
            add_later(taps, totals, [other_refs[-1][comp, order[s], tile] for s in range(days)])
            if not pair:
                add_earlier(taps, totals, [other_refs[0][comp, s, tile] for s in range(days)])
            filtered.append(totals)
        for a in range(comps):
            for t in range(days):
                mixed_ref[a * days + order[t], tile] = (
                    weights[a][0] * filtered[0][t] + weights[a][1] * filtered[1][t]
                )
        return 0

    lax.fori_loop(0, tiles, body, 0, unroll=4)


def west_east(place_ref, first, second):
    flag = east_first(place_ref)
    return jnp.where(flag, second, first), jnp.where(flag, first, second)


def unpacked(item, west, east):
    column = jnp.bitwise_and(lax.broadcasted_iota(jnp.int32, west.shape, 1), SIDE - 1)
    return jnp.where(
        column >= SIDE // 2,
        roll(west, wrapped(SPACE_HALF * item)),
        roll(east, wrapped(LANES - SPACE_HALF * item)),
    )


def corner_kernel(place_ref, second_ref, first_ref, *refs):
    one_ref, two_ref = refs[-2:]
    slots = one_ref.shape[2]
    south = south_first(place_ref)
    for k, side in enumerate(west_east(place_ref, first_ref[...], second_ref[...])):
        top, bottom = side[:slots], side[-slots:]
        one_ref[0, k] = jnp.where(south, bottom, top)
        two_ref[0, k] = jnp.where(south, top, bottom)


def two_parts(x):
    coarse = x.astype(jnp.bfloat16)
    return coarse, (x - coarse.astype(jnp.float32)).astype(jnp.bfloat16)


def bands_kernel(taps_ref, bands_ref):
    shape = (2 * LANES, LANES)
    source = lax.broadcasted_iota(jnp.int32, shape, 0)
    target = lax.broadcasted_iota(jnp.int32, shape, 1)
    same = jnp.bitwise_and(source // SIDE, 1) == target // SIDE
    source_column = jnp.bitwise_and(source, SIDE - 1)
    outside = jnp.where(source_column >= SIDE // 2, source_column - SIDE, source_column + SIDE)
    position = jnp.where(source < LANES, source_column, outside)
    distance = jnp.abs(position - jnp.bitwise_and(target, SIDE - 1))
    bands = jnp.zeros(shape, jnp.float32)
    for lag in range(SPACE_HALF + 1):
        bands = jnp.where(same & (distance == lag), taps_ref[0, lag], bands)
    coarse, fine = two_parts(bands)
    bands_ref[: 2 * LANES, :LANES] = coarse
    bands_ref[: 2 * LANES, LANES:] = fine
    bands_ref[2 * LANES :, :LANES] = coarse
    bands_ref[2 * LANES :, LANES:] = jnp.zeros_like(fine)


def across(bands, tiles):
    slots = tiles[0][0].shape[0]
    centre_parts = two_parts(jnp.concatenate([centre for centre, _ in tiles], axis=0))
    halo_parts = two_parts(jnp.concatenate([halo for _, halo in tiles], axis=0))
    product = jnp.dot(
        jnp.concatenate([part for both in zip(centre_parts, halo_parts) for part in both], axis=1),
        bands,
        preferred_element_type=jnp.float32,
    )
    product = product[:, :LANES] + product[:, LANES:]
    return [product[slots * p : slots * (p + 1)] for p in range(len(tiles))]


def sides_of(nb, west, east, device, shape):
    slots = shape[0]
    column = jnp.bitwise_and(lax.broadcasted_iota(jnp.int32, shape, 1), SIDE - 1)
    target = jnp.where(column >= SIDE // 2, entry(nb, west, shape), entry(nb, east, shape))
    near = on_device(target, device, slots)
    return jnp.bitwise_and(target, slots - 1), near, (target >= 0) & ~near


def halo_of(source, far, plan):
    index, near, remote = plan
    halo = jnp.where(near, pick(source, index), 0.0)
    return jnp.where(remote, jnp.broadcast_to(far, halo.shape), halo)


def odd_rows(before, after):
    low = lax.broadcasted_iota(jnp.int32, before.shape, 1) < SIDE
    return roll(jnp.where(low, after, before), SIDE)


def inner_kernel(
    place_ref, mask_ref, taps_ref, nb_ref, bands_ref, mixed_ref, second_ref, first_ref,
    out_hbm, outer_ref, out_ref, far_ref, stored,
):
    count, tiles, slots, _ = mixed_ref.shape
    lane, sublane = iotas(slots)
    live = live_vector(mask_ref, sublane)
    taps = [taps_ref[1, lag] for lag in range(SPACE_HALF + 1)]
    plan = sides_of(nb_ref[...], WEST, EAST, place_ref[0], lane.shape)
    west, east = west_east(place_ref, first_ref[...], second_ref[...])
    together = far_ref.shape[0]

    def store(step):
        part = pl.ds(step * together, together)
        return pltpu.make_async_copy(out_ref.at[part], out_hbm.at[part], stored.at[step])

    def body(step, _):
        fetched = []
        for k in range(together):
            item = step * together + k
            far_ref[k] = unpacked(item, west, east)
            for tile in range(tiles):
                centre = mixed_ref[item, tile]
                fetched.append((centre, halo_of(centre, far_ref[k, tile : tile + 1], plan)))
        lines = across(bands_ref[...], fetched)
        zero = jnp.zeros(lane.shape, jnp.float32)
        for k in range(together):
            item = step * together + k
            rows = [zero] * PAIR_ROWS + lines[k * tiles : (k + 1) * tiles] + [zero] * PAIR_ROWS
            odd = [odd_rows(rows[p], rows[p + 1]) for p in range(len(rows) - 1)]
            for p in range(tiles):
                total = taps[0] * rows[p + 2]
                total = total + taps[1] * (odd[p + 1] + odd[p + 2])
                total = total + taps[2] * (rows[p + 1] + rows[p + 3])
                total = total + taps[3] * (odd[p] + odd[p + 3])
                total = total + taps[4] * (rows[p] + rows[p + 4])
                total = live * total
                out_ref[item, p] = total
                if p < PAIR_ROWS:
                    outer_ref[item, p] = total
                elif p >= tiles - PAIR_ROWS:
                    outer_ref[item, p - tiles + 2 * PAIR_ROWS] = total
        store(step).start()
        return 0

    lax.fori_loop(0, count // together, body, 0)
    for step in range(count // together):
        store(step).wait()


def outer_kernel(
    place_ref, mask_ref, taps_ref, nb_ref, bands_ref, outer_ref, second_ref, first_ref,
    _, out_hbm, out_ref, stored,
):
    count, _, slots, _ = outer_ref.shape
    tiles = out_hbm.shape[1]
    lane, sublane = iotas(slots)
    live = live_vector(mask_ref, sublane)
    taps = [taps_ref[1, lag] for lag in range(SPACE_HALF + 1)]
    nb = nb_ref[...]
    me = place_ref[0]
    fetched = []
    for north in (True, False):
        use_first = ~south_first(place_ref) if north else south_first(place_ref)

        def read(index, part, use_first=use_first):
            return jnp.where(use_first, first_ref[index, part], second_ref[index, part])

        target = entry(nb, NORTH if north else SOUTH, lane.shape)
        plan = sides_of(
            nb,
            NORTH_WEST if north else SOUTH_WEST,
            NORTH_EAST if north else SOUTH_EAST,
            me - REACH if north else me + REACH,
            lane.shape,
        )
        corner = [read(count, 0), read(count, 1)]
        for item in range(count):
            far = unpacked(jnp.int32(item), *corner)
            for part in range(PAIR_ROWS):
                source = read(item, part)
                centre = jnp.where(
                    target >= 0, pick(source, jnp.bitwise_and(target, slots - 1)), 0.0
                )
                row = slots - PAIR_ROWS + part if north else part
                fetched.append((centre, halo_of(source, far[row : row + 1], plan)))
    rows = across(bands_ref[...], fetched)
    zero = jnp.zeros(lane.shape, jnp.float32)
    copies = []
    for side in range(2):
        for item in range(count):
            at = (side * count + item) * PAIR_ROWS
            one, two = rows[at : at + PAIR_ROWS]
            close, far = (one, two) if side else (two, one)
            edge = odd_rows(zero, one) if side else odd_rows(two, zero)
            near = taps[1] * edge + taps[2] * close + taps[3] * odd_rows(one, two)
            near = near + taps[4] * far
            off = taps[3] * edge + taps[4] * close
            for part, value in enumerate((off, near) if side else (near, off)):
                out_ref[side, item, part] = (
                    outer_ref[item, side * PAIR_ROWS + part] + live * value
                )
        place = pl.ds(side * (tiles - PAIR_ROWS), PAIR_ROWS)
        copy = pltpu.make_async_copy(out_ref.at[side], out_hbm.at[:, place], stored.at[side])
        copy.start()
        copies.append(copy)
    for copy in copies:
        copy.wait()


def swap_both(first, second, index, length):
    blk = lax.axis_size("blk")
    results = []
    for x, shift in ((second, 1), (first, 0)):
        partner = {}
        for at in range(shift, length + shift, 2):
            low, high = at % length, (at + 1) % length
            partner[low], partner[high] = high, low
        place = [index(i) for i in range(blk)]
        pairs = [(i, i + (partner[at] - at) * step) for i, (at, step) in enumerate(place)]
        results.append(lax.ppermute(x, "blk", pairs))
    return results[::-1]


def shards(input_field, active_mask, neighbours, time_taps, space_taps, coregion_factor):
    comps, days, slots, cells = input_field.shape
    count = comps * days
    tiles = cells // LANES
    blk = lax.axis_size("blk")
    day = lax.axis_size("day")
    pair = day == 2
    sides = 2
    place = jnp.stack([lax.axis_index("blk"), lax.axis_index("day")]).astype(jnp.int32)

    def in_tiles(x):
        return x.reshape(comps, days, slots, tiles, LANES).transpose(0, 1, 3, 2, 4)

    if pair:
        others = [lax.ppermute(input_field, "day", [(0, 1), (1, 0)])]
    else:
        up = [(i, i + 1) for i in range(day - 1)]
        others = [
            lax.ppermute(input_field, "day", up),
            lax.ppermute(input_field, "day", [(b, a) for a, b in up]),
        ]
    others = [in_tiles(x) for x in others]
    field = array(count, tiles, slots, LANES)

    own, ends, *raw = pl.pallas_call(
        own_kernel,
        out_shape=(field, jax.ShapeDtypeStruct((2,), jnp.int32))
        + (array(count, tiles, LANES),) * sides
        + (array(count, PAIR_ROWS, slots, LANES),) * sides,
        in_specs=[SMEM] * 5 + [WHOLE],
        out_specs=(WHOLE, SMEM) + (WHOLE,) * (2 * sides),
        compiler_params=PARAMS,
        name="own_days",
    )(place, active_mask, time_taps, coregion_factor, neighbours, in_tiles(input_field))

    sent_count = count + 1
    sent_shape = array(sent_count, PAIR_ROWS, slots, LANES)
    packed_and_sent = pl.pallas_call(
        functools.partial(send_kernel, pair),
        out_shape=(array(tiles, LANES),) * sides + (sent_shape,) * sides,
        in_specs=[SMEM] * 5 + [WHOLE] * (len(raw) + len(others)),
        out_specs=(WHOLE,) * (2 * sides),
        compiler_params=PARAMS,
        name="edges_and_strips",
    )(place, active_mask, time_taps, coregion_factor, ends, *raw, *others)
    packed, sent = packed_and_sent[:sides], packed_and_sent[sides:]

    first, second = swap_both(*packed, lambda i: (i % REACH, 1), REACH)

    mixed = pl.pallas_call(
        functools.partial(mix_kernel, pair),
        out_shape=field,
        in_specs=[SMEM] * 4 + [WHOLE] * (1 + len(others)),
        out_specs=WHOLE,
        compiler_params=PARAMS,
        cost_estimate=pl.CostEstimate(
            flops=20 * field.size, bytes_accessed=12 * field.size, transcendentals=0
        ),
        name="mix",
    )(place, active_mask, time_taps, coregion_factor, own, *others)

    bands = pl.pallas_call(
        bands_kernel,
        out_shape=jax.ShapeDtypeStruct((4 * LANES, 2 * LANES), jnp.bfloat16),
        in_specs=[SMEM],
        out_specs=WHOLE,
        compiler_params=PARAMS,
        name="bands",
    )(space_taps)

    sent = pl.pallas_call(
        corner_kernel,
        grid=(1,),
        out_shape=(sent_shape,) * sides,
        in_specs=[SMEM, WHOLE, WHOLE] + [pl.BlockSpec(memory_space=pl.ANY)] * (sides + 2),
        out_specs=(
            pl.BlockSpec((1, PAIR_ROWS, slots, LANES), lambda i: (sent_count - 1, 0, 0, 0)),
        )
        * sides,
        input_output_aliases={5 + side: side for side in range(sides)},
        compiler_params=PARAMS,
        name="corners",
    )(place, second, first, mixed, bands, *sent)

    one, two = swap_both(*sent, lambda i: (i // REACH, REACH), blk // REACH)

    together = 2
    inner, outer = pl.pallas_call(
        inner_kernel,
        out_shape=(field, array(count, 2 * PAIR_ROWS, slots, LANES)),
        in_specs=[SMEM] * 3 + [WHOLE] * 5,
        out_specs=(IN_HBM, WHOLE),
        scratch_shapes=[
            pltpu.VMEM(field.shape, jnp.float32),
            pltpu.VMEM((together, tiles, LANES), jnp.float32),
            DMA((count // together,)),
        ],
        compiler_params=PARAMS,
        cost_estimate=pl.CostEstimate(
            flops=4 * field.size * LANES, bytes_accessed=8 * field.size, transcendentals=0
        ),
        name="inner_rows",
    )(place, active_mask, space_taps, neighbours, bands, mixed, second, first)

    result = pl.pallas_call(
        outer_kernel,
        out_shape=field,
        in_specs=[SMEM] * 3 + [WHOLE] * 5 + [IN_HBM],
        out_specs=IN_HBM,
        scratch_shapes=[
            pltpu.VMEM((2, count, PAIR_ROWS, slots, LANES), jnp.float32),
            DMA((2,)),
        ],
        input_output_aliases={8: 0},
        compiler_params=PARAMS,
        name="outer_rows",
    )(place, active_mask, space_taps, neighbours, bands, outer, two, one, inner)
    result = result.reshape(comps, days, tiles, slots, LANES).transpose(0, 1, 3, 2, 4)
    return result.reshape(input_field.shape)


def solution(mesh):
    in_specs = (P(None, "day", "blk", None), P("blk"), P("blk", None), P(), P(), P())
    out_specs = P(None, "day", "blk", None)
    return jax.shard_map(shards, mesh=mesh, in_specs=in_specs, out_specs=out_specs, check_vma=False)
```

```python
import functools

import jax
import jax.numpy as jnp
from jax import lax
from jax.experimental import pallas as pl
from jax.experimental.pallas import tpu as pltpu
from jax.sharding import PartitionSpec as P

SIDE = 64
SPACE_HALF = 4
TIME_HALF = 3
REACH = 4
LANES = 128
EAST, WEST, NORTH, SOUTH, NORTH_EAST, NORTH_WEST, SOUTH_EAST, SOUTH_WEST = range(8)
PAIR_ROWS = SPACE_HALF * SIDE // LANES
GROUPS = SIDE // SPACE_HALF
PARAMS = pltpu.CompilerParams(vmem_limit_bytes=12 * 1024 * 1024)
SMEM = pl.BlockSpec(memory_space=pltpu.SMEM)
WHOLE = pl.BlockSpec(memory_space=pltpu.VMEM)
IN_HBM = pl.BlockSpec(memory_space=pltpu.HBM)
DMA = pltpu.SemaphoreType.DMA


def array(*shape):
    return jax.ShapeDtypeStruct(shape, jnp.float32)


def iotas(slots):
    lane = lax.broadcasted_iota(jnp.int32, (slots, LANES), 1)
    sublane = lax.broadcasted_iota(jnp.int32, (slots, LANES), 0)
    return lane, sublane


def live_vector(mask_ref, sublane):
    live = jnp.zeros(sublane.shape, jnp.float32)
    for slot in range(sublane.shape[0]):
        live = jnp.where(sublane == slot, mask_ref[slot].astype(jnp.float32), live)
    return live


def entry(neighbours, direction, shape):
    return jnp.broadcast_to(neighbours[:, direction : direction + 1], shape)


def pick(source, index):
    return jnp.take_along_axis(source, index, axis=0)


def roll(x, shift):
    return pltpu.roll(x, shift % LANES if isinstance(shift, int) else shift, 1)


def wrapped(shift):
    return jnp.bitwise_and(shift, LANES - 1)


def device_of(target, slots):
    return lax.shift_right_arithmetic(target, jnp.int32(slots.bit_length() - 1))


def on_device(target, device, slots):
    return (target >= 0) & (device_of(target, slots) == device)


def taps_of(taps_ref):
    return [taps_ref[lag] for lag in range(TIME_HALF + 1)]


def order_of(pair, day, days):
    return [day * (days - 1 - 2 * s) + s if pair else s for s in range(days)]


def coupling_of(factor_ref):
    return [
        [
            factor_ref[a, 0] * factor_ref[b, 0] + factor_ref[a, 1] * factor_ref[b, 1]
            for b in range(2)
        ]
        for a in range(2)
    ]


def same_days(taps, values):
    totals = []
    for t in range(len(values)):
        total = taps[0] * values[t]
        for s in range(len(values)):
            if s != t:
                total = total + taps[abs(s - t)] * values[s]
        totals.append(total)
    return totals


def add_later(taps, totals, values):
    for t in range(len(totals)):
        for s in range(t + 1):
            totals[t] = totals[t] + taps[len(totals) + s - t] * values[s]


def add_earlier(taps, totals, values):
    for t in range(len(totals)):
        for s in range(t, len(totals)):
            totals[t] = totals[t] + taps[len(totals) + t - s] * values[s]


def east_first(place_ref):
    return jnp.bitwise_and(place_ref[0], 1) == 0


def south_first(place_ref):
    return jnp.bitwise_and(place_ref[0], REACH) == 0


def end_slot(nb_ref, me, east):
    slots = nb_ref.shape[0]
    step, directions = (
        (1, (EAST, NORTH_EAST, SOUTH_EAST)) if east else (-1, (WEST, NORTH_WEST, SOUTH_WEST))
    )
    found = jnp.int32(0)
    for slot in range(slots):
        for direction, shift in zip(directions, (0, -REACH, REACH)):
            target = nb_ref[slot, direction]
            hit = (target >= 0) & (device_of(target, slots) == me + step + shift)
            found = jnp.where(hit, slot, found)
    return found


def edge_plan(place_ref, ends_ref):
    first = east_first(place_ref)
    return [(first, ends_ref[0]), (~first, ends_ref[1])]


def strip_starts(place_ref, tiles):
    last = tiles - PAIR_ROWS
    first = south_first(place_ref)
    return [jnp.where(first, last, 0), jnp.where(first, 0, last)]


def own_kernel(place_ref, mask_ref, taps_ref, _, nb_ref, x_ref, own_ref, ends_ref, *rest):
    comps, days, tiles, slots, _ = x_ref.shape
    edge_refs, strip_refs = rest[: len(rest) // 2], rest[len(rest) // 2 :]
    taps = taps_of(taps_ref)
    me = place_ref[0]
    east, west = end_slot(nb_ref, me, True), end_slot(nb_ref, me, False)
    first = east_first(place_ref)
    ends = [jnp.where(first, east, west), jnp.where(first, west, east)]
    for k, slot in enumerate(ends):
        ends_ref[k] = slot
    for edge_ref, slot in zip(edge_refs, ends):
        live = mask_ref[slot].astype(jnp.float32)
        for comp in range(comps):
            for t in range(days):
                edge_ref[comp * days + t] = live * x_ref[comp, t, :, slot, :]
    for strip_ref, start in zip(strip_refs, strip_starts(place_ref, tiles)):
        for comp in range(comps):
            for t in range(days):
                strip_ref[comp * days + t] = x_ref[comp, t, pl.ds(start, PAIR_ROWS)]

    def body(tile, _):
        for comp in range(comps):
            values = [x_ref[comp, t, tile] for t in range(days)]
            for t, total in enumerate(same_days(taps, values)):
                own_ref[comp * days + t, tile] = total
        return 0

    lax.fori_loop(0, tiles, body, 0, unroll=8)


def send_kernel(pair, place_ref, mask_ref, taps_ref, factor_ref, ends_ref, *refs):
    sides = 2
    edge_refs, strip_refs = refs[:sides], refs[sides : 2 * sides]
    other_refs = refs[2 * sides : len(refs) - 2 * sides]
    packed_refs = refs[len(refs) - 2 * sides : len(refs) - sides]
    sent_refs = refs[len(refs) - sides :]
    comps, days, tiles, slots, _ = other_refs[0].shape
    lane, sublane = iotas(slots)
    group = jnp.bitwise_and(lax.broadcasted_iota(jnp.int32, (tiles, LANES), 1), SIDE - 1)
    group = group // SPACE_HALF
    live_slots = live_vector(mask_ref, sublane)
    taps = taps_of(taps_ref)
    coupling = coupling_of(factor_ref)
    order = order_of(pair, place_ref[1], days)

    def all_days(raw_ref, read_other):
        filtered = []
        for comp in range(comps):
            values = [raw_ref[comp * days + order[s]] for s in range(days)]
            later = [read_other(other_refs[-1], comp, order[s]) for s in range(days)]
            totals = same_days(taps, values)
            add_later(taps, totals, later)
            if not pair:
                add_earlier(
                    taps, totals, [read_other(other_refs[0], comp, s) for s in range(days)]
                )
            filtered.append(totals)
        for a in range(comps):
            for t in range(days):
                value = coupling[a][0] * filtered[0][t] + coupling[a][1] * filtered[1][t]
                yield a * days + order[t], value

    for edge_ref, packed_ref, (to_east, slot) in zip(
        edge_refs, packed_refs, edge_plan(place_ref, ends_ref)
    ):
        live = mask_ref[slot].astype(jnp.float32)
        packed = jnp.zeros((tiles, LANES), jnp.float32)
        for at, value in all_days(edge_ref, lambda ref, c, s: live * ref[c, s, :, slot, :]):
            shift = wrapped(jnp.where(to_east, LANES - SPACE_HALF * at, SPACE_HALF * at))
            spot = jnp.where(to_east, GROUPS - 1 - at, at)
            packed = jnp.where(group == spot, roll(value, shift), packed)
        packed_ref[...] = packed
    for strip_ref, sent_ref, start in zip(
        strip_refs, sent_refs, strip_starts(place_ref, tiles)
    ):
        for at, value in all_days(strip_ref, lambda ref, c, s: ref[c, s, pl.ds(start, PAIR_ROWS)]):
            sent_ref[at] = live_slots * value


def mix_kernel(pair, place_ref, mask_ref, taps_ref, factor_ref, own_ref, *rest):
    *other_refs, mixed_ref = rest
    _, tiles, slots, _ = mixed_ref.shape
    comps, days = other_refs[0].shape[:2]
    _, sublane = iotas(slots)
    live = live_vector(mask_ref, sublane)
    taps = taps_of(taps_ref)
    weights = [[live * value for value in row] for row in coupling_of(factor_ref)]
    order = order_of(pair, place_ref[1], days)

    def body(tile, _):
        filtered = []
        for comp in range(comps):
            totals = [own_ref[comp * days + order[t], tile] for t in range(days)]
            add_later(taps, totals, [other_refs[-1][comp, order[s], tile] for s in range(days)])
            if not pair:
                add_earlier(taps, totals, [other_refs[0][comp, s, tile] for s in range(days)])
            filtered.append(totals)
        for a in range(comps):
            for t in range(days):
                mixed_ref[a * days + order[t], tile] = (
                    weights[a][0] * filtered[0][t] + weights[a][1] * filtered[1][t]
                )
        return 0

    lax.fori_loop(0, tiles, body, 0, unroll=4)


def west_east(place_ref, first, second):
    flag = east_first(place_ref)
    return jnp.where(flag, second, first), jnp.where(flag, first, second)


def unpacked(item, west, east):
    column = jnp.bitwise_and(lax.broadcasted_iota(jnp.int32, west.shape, 1), SIDE - 1)
    return jnp.where(
        column >= SIDE // 2,
        roll(west, wrapped(SPACE_HALF * item)),
        roll(east, wrapped(LANES - SPACE_HALF * item)),
    )


def corner_kernel(place_ref, first_ref, second_ref, *refs):
    one_ref, two_ref = refs[-2:]
    slots = one_ref.shape[2]
    south = south_first(place_ref)
    for k, side in enumerate(west_east(place_ref, first_ref[...], second_ref[...])):
        top, bottom = side[:slots], side[-slots:]
        one_ref[0, k] = jnp.where(south, bottom, top)
        two_ref[0, k] = jnp.where(south, top, bottom)


def two_parts(x):
    coarse = x.astype(jnp.bfloat16)
    return coarse, (x - coarse.astype(jnp.float32)).astype(jnp.bfloat16)


def bands_kernel(taps_ref, bands_ref):
    shape = (2 * LANES, LANES)
    source = lax.broadcasted_iota(jnp.int32, shape, 0)
    target = lax.broadcasted_iota(jnp.int32, shape, 1)
    same = jnp.bitwise_and(source // SIDE, 1) == target // SIDE
    source_column = jnp.bitwise_and(source, SIDE - 1)
    outside = jnp.where(source_column >= SIDE // 2, source_column - SIDE, source_column + SIDE)
    position = jnp.where(source < LANES, source_column, outside)
    distance = jnp.abs(position - jnp.bitwise_and(target, SIDE - 1))
    bands = jnp.zeros(shape, jnp.float32)
    for lag in range(SPACE_HALF + 1):
        bands = jnp.where(same & (distance == lag), taps_ref[0, lag], bands)
    coarse, fine = two_parts(bands)
    bands_ref[: 2 * LANES, :LANES] = coarse
    bands_ref[: 2 * LANES, LANES:] = fine
    bands_ref[2 * LANES :, :LANES] = coarse
    bands_ref[2 * LANES :, LANES:] = jnp.zeros_like(fine)


def across(bands, tiles):
    slots = tiles[0][0].shape[0]
    centre_parts = two_parts(jnp.concatenate([centre for centre, _ in tiles], axis=0))
    halo_parts = two_parts(jnp.concatenate([halo for _, halo in tiles], axis=0))
    product = jnp.dot(
        jnp.concatenate([part for both in zip(centre_parts, halo_parts) for part in both], axis=1),
        bands,
        preferred_element_type=jnp.float32,
    )
    product = product[:, :LANES] + product[:, LANES:]
    return [product[slots * p : slots * (p + 1)] for p in range(len(tiles))]


def sides_of(nb, west, east, device, shape):
    slots = shape[0]
    column = jnp.bitwise_and(lax.broadcasted_iota(jnp.int32, shape, 1), SIDE - 1)
    target = jnp.where(column >= SIDE // 2, entry(nb, west, shape), entry(nb, east, shape))
    near = on_device(target, device, slots)
    return jnp.bitwise_and(target, slots - 1), near, (target >= 0) & ~near


def halo_of(source, far, plan):
    index, near, remote = plan
    halo = jnp.where(near, pick(source, index), 0.0)
    return jnp.where(remote, jnp.broadcast_to(far, halo.shape), halo)


def odd_rows(before, after):
    low = lax.broadcasted_iota(jnp.int32, before.shape, 1) < SIDE
    return roll(jnp.where(low, after, before), SIDE)


def inner_kernel(
    place_ref, mask_ref, taps_ref, nb_ref, bands_ref, mixed_ref, first_ref, second_ref,
    out_hbm, outer_ref, out_ref, far_ref, stored,
):
    count, tiles, slots, _ = mixed_ref.shape
    lane, sublane = iotas(slots)
    live = live_vector(mask_ref, sublane)
    taps = [taps_ref[1, lag] for lag in range(SPACE_HALF + 1)]
    plan = sides_of(nb_ref[...], WEST, EAST, place_ref[0], lane.shape)
    west, east = west_east(place_ref, first_ref[...], second_ref[...])
    together = far_ref.shape[0]

    def store(step):
        part = pl.ds(step * together, together)
        return pltpu.make_async_copy(out_ref.at[part], out_hbm.at[part], stored.at[step])

    def body(step, _):
        fetched = []
        for k in range(together):
            item = step * together + k
            far_ref[k] = unpacked(item, west, east)
            for tile in range(tiles):
                centre = mixed_ref[item, tile]
                fetched.append((centre, halo_of(centre, far_ref[k, tile : tile + 1], plan)))
        lines = across(bands_ref[...], fetched)
        zero = jnp.zeros(lane.shape, jnp.float32)
        for k in range(together):
            item = step * together + k
            rows = [zero] * PAIR_ROWS + lines[k * tiles : (k + 1) * tiles] + [zero] * PAIR_ROWS
            odd = [odd_rows(rows[p], rows[p + 1]) for p in range(len(rows) - 1)]
            for p in range(tiles):
                total = taps[0] * rows[p + 2]
                total = total + taps[1] * (odd[p + 1] + odd[p + 2])
                total = total + taps[2] * (rows[p + 1] + rows[p + 3])
                total = total + taps[3] * (odd[p] + odd[p + 3])
                total = total + taps[4] * (rows[p] + rows[p + 4])
                total = live * total
                out_ref[item, p] = total
                if p < PAIR_ROWS:
                    outer_ref[item, p] = total
                elif p >= tiles - PAIR_ROWS:
                    outer_ref[item, p - tiles + 2 * PAIR_ROWS] = total
        store(step).start()
        return 0

    lax.fori_loop(0, count // together, body, 0)
    for step in range(count // together):
        store(step).wait()


def outer_kernel(
    place_ref, mask_ref, taps_ref, nb_ref, bands_ref, outer_ref, first_ref, second_ref,
    _, out_hbm, out_ref, stored,
):
    count, _, slots, _ = outer_ref.shape
    tiles = out_hbm.shape[1]
    lane, sublane = iotas(slots)
    live = live_vector(mask_ref, sublane)
    taps = [taps_ref[1, lag] for lag in range(SPACE_HALF + 1)]
    nb = nb_ref[...]
    me = place_ref[0]
    fetched = []
    for north in (True, False):
        use_first = ~south_first(place_ref) if north else south_first(place_ref)

        def read(index, part, use_first=use_first):
            return jnp.where(use_first, first_ref[index, part], second_ref[index, part])

        target = entry(nb, NORTH if north else SOUTH, lane.shape)
        plan = sides_of(
            nb,
            NORTH_WEST if north else SOUTH_WEST,
            NORTH_EAST if north else SOUTH_EAST,
            me - REACH if north else me + REACH,
            lane.shape,
        )
        corner = [read(count, 0), read(count, 1)]
        for item in range(count):
            far = unpacked(jnp.int32(item), *corner)
            for part in range(PAIR_ROWS):
                source = read(item, part)
                centre = jnp.where(
                    target >= 0, pick(source, jnp.bitwise_and(target, slots - 1)), 0.0
                )
                row = slots - PAIR_ROWS + part if north else part
                fetched.append((centre, halo_of(source, far[row : row + 1], plan)))
    rows = across(bands_ref[...], fetched)
    zero = jnp.zeros(lane.shape, jnp.float32)
    copies = []
    for side in range(2):
        for item in range(count):
            at = (side * count + item) * PAIR_ROWS
            one, two = rows[at : at + PAIR_ROWS]
            close, far = (one, two) if side else (two, one)
            edge = odd_rows(zero, one) if side else odd_rows(two, zero)
            near = taps[1] * edge + taps[2] * close + taps[3] * odd_rows(one, two)
            near = near + taps[4] * far
            off = taps[3] * edge + taps[4] * close
            for part, value in enumerate((off, near) if side else (near, off)):
                out_ref[side, item, part] = (
                    outer_ref[item, side * PAIR_ROWS + part] + live * value
                )
        place = pl.ds(side * (tiles - PAIR_ROWS), PAIR_ROWS)
        copy = pltpu.make_async_copy(out_ref.at[side], out_hbm.at[:, place], stored.at[side])
        copy.start()
        copies.append(copy)
    for copy in copies:
        copy.wait()


def swap_both(first, second, index, length):
    blk, day = lax.axis_size("blk"), lax.axis_size("day")
    results = []
    for x, shift in ((first, 0), (second, 1)):
        partner = {}
        for at in range(shift, length + shift, 2):
            low, high = at % length, (at + 1) % length
            partner[low], partner[high] = high, low
        pairs = []
        for i in range(blk):
            at, step = index(i)
            across_chip = day == 2 and abs(partner[at] - at) > 1
            other = i if across_chip else i + (partner[at] - at) * step
            for core in range(day):
                pairs.append((i * day + core, other * day + (1 - core if across_chip else core)))
        results.append(lax.ppermute(x, ("blk", "day"), pairs))
    return results


def shards(input_field, active_mask, neighbours, time_taps, space_taps, coregion_factor):
    comps, days, slots, cells = input_field.shape
    count = comps * days
    tiles = cells // LANES
    blk = lax.axis_size("blk")
    day = lax.axis_size("day")
    pair = day == 2
    sides = 2
    place = jnp.stack([lax.axis_index("blk"), lax.axis_index("day")]).astype(jnp.int32)

    def in_tiles(x):
        return x.reshape(comps, days, slots, tiles, LANES).transpose(0, 1, 3, 2, 4)

    if pair:
        others = [lax.ppermute(input_field, "day", [(0, 1), (1, 0)])]
    else:
        up = [(i, i + 1) for i in range(day - 1)]
        others = [
            lax.ppermute(input_field, "day", up),
            lax.ppermute(input_field, "day", [(b, a) for a, b in up]),
        ]
    others = [in_tiles(x) for x in others]
    field = array(count, tiles, slots, LANES)

    own, ends, *raw = pl.pallas_call(
        own_kernel,
        out_shape=(field, jax.ShapeDtypeStruct((2,), jnp.int32))
        + (array(count, tiles, LANES),) * sides
        + (array(count, PAIR_ROWS, slots, LANES),) * sides,
        in_specs=[SMEM] * 5 + [WHOLE],
        out_specs=(WHOLE, SMEM) + (WHOLE,) * (2 * sides),
        compiler_params=PARAMS,
        name="own_days",
    )(place, active_mask, time_taps, coregion_factor, neighbours, in_tiles(input_field))

    sent_count = count + 1
    sent_shape = array(sent_count, PAIR_ROWS, slots, LANES)
    packed_and_sent = pl.pallas_call(
        functools.partial(send_kernel, pair),
        out_shape=(array(tiles, LANES),) * sides + (sent_shape,) * sides,
        in_specs=[SMEM] * 5 + [WHOLE] * (len(raw) + len(others)),
        out_specs=(WHOLE,) * (2 * sides),
        compiler_params=PARAMS,
        name="edges_and_strips",
    )(place, active_mask, time_taps, coregion_factor, ends, *raw, *others)
    packed, sent = packed_and_sent[:sides], packed_and_sent[sides:]

    first, second = swap_both(*packed, lambda i: (i % REACH, 1), REACH)

    mixed = pl.pallas_call(
        functools.partial(mix_kernel, pair),
        out_shape=field,
        in_specs=[SMEM] * 4 + [WHOLE] * (1 + len(others)),
        out_specs=WHOLE,
        compiler_params=PARAMS,
        cost_estimate=pl.CostEstimate(
            flops=20 * field.size, bytes_accessed=12 * field.size, transcendentals=0
        ),
        name="mix",
    )(place, active_mask, time_taps, coregion_factor, own, *others)

    bands = pl.pallas_call(
        bands_kernel,
        out_shape=jax.ShapeDtypeStruct((4 * LANES, 2 * LANES), jnp.bfloat16),
        in_specs=[SMEM],
        out_specs=WHOLE,
        compiler_params=PARAMS,
        name="bands",
    )(space_taps)

    sent = pl.pallas_call(
        corner_kernel,
        grid=(1,),
        out_shape=(sent_shape,) * sides,
        in_specs=[SMEM, WHOLE, WHOLE] + [pl.BlockSpec(memory_space=pl.ANY)] * (sides + 2),
        out_specs=(
            pl.BlockSpec((1, PAIR_ROWS, slots, LANES), lambda i: (sent_count - 1, 0, 0, 0)),
        )
        * sides,
        input_output_aliases={5 + side: side for side in range(sides)},
        compiler_params=PARAMS,
        name="corners",
    )(place, first, second, mixed, bands, *sent)

    one, two = swap_both(*sent, lambda i: (i // REACH, REACH), blk // REACH)

    together = 2
    inner, outer = pl.pallas_call(
        inner_kernel,
        out_shape=(field, array(count, 2 * PAIR_ROWS, slots, LANES)),
        in_specs=[SMEM] * 3 + [WHOLE] * 5,
        out_specs=(IN_HBM, WHOLE),
        scratch_shapes=[
            pltpu.VMEM(field.shape, jnp.float32),
            pltpu.VMEM((together, tiles, LANES), jnp.float32),
            DMA((count // together,)),
        ],
        compiler_params=PARAMS,
        cost_estimate=pl.CostEstimate(
            flops=4 * field.size * LANES, bytes_accessed=8 * field.size, transcendentals=0
        ),
        name="inner_rows",
    )(place, active_mask, space_taps, neighbours, bands, mixed, first, second)

    result = pl.pallas_call(
        outer_kernel,
        out_shape=field,
        in_specs=[SMEM] * 3 + [WHOLE] * 5 + [IN_HBM],
        out_specs=IN_HBM,
        scratch_shapes=[
            pltpu.VMEM((2, count, PAIR_ROWS, slots, LANES), jnp.float32),
            DMA((2,)),
        ],
        input_output_aliases={8: 0},
        compiler_params=PARAMS,
        name="outer_rows",
    )(place, active_mask, space_taps, neighbours, bands, outer, one, two, inner)
    result = result.reshape(comps, days, tiles, slots, LANES).transpose(0, 1, 3, 2, 4)
    return result.reshape(input_field.shape)


def solution(mesh):
    in_specs = (P(None, "day", "blk", None), P("blk"), P("blk", None), P(), P(), P())
    out_specs = P(None, "day", "blk", None)
    return jax.shard_map(shards, mesh=mesh, in_specs=in_specs, out_specs=out_specs, check_vma=False)
```

```python
import functools

import jax
import jax.numpy as jnp
from jax import lax
from jax.experimental import pallas as pl
from jax.experimental.pallas import tpu as pltpu
from jax.sharding import PartitionSpec as P

SIDE = 64
SPACE_HALF = 4
TIME_HALF = 3
REACH = 4
LANES = 128
EAST, WEST, NORTH, SOUTH, NORTH_EAST, NORTH_WEST, SOUTH_EAST, SOUTH_WEST = range(8)
PAIR_ROWS = SPACE_HALF * SIDE // LANES
GROUPS = SIDE // SPACE_HALF
PARAMS = pltpu.CompilerParams(vmem_limit_bytes=12 * 1024 * 1024)
SMEM = pl.BlockSpec(memory_space=pltpu.SMEM)
WHOLE = pl.BlockSpec(memory_space=pltpu.VMEM)
IN_HBM = pl.BlockSpec(memory_space=pltpu.HBM)
DMA = pltpu.SemaphoreType.DMA


def array(*shape):
    return jax.ShapeDtypeStruct(shape, jnp.float32)


def iotas(slots):
    lane = lax.broadcasted_iota(jnp.int32, (slots, LANES), 1)
    sublane = lax.broadcasted_iota(jnp.int32, (slots, LANES), 0)
    return lane, sublane


def live_vector(mask_ref, sublane):
    live = jnp.zeros(sublane.shape, jnp.float32)
    for slot in range(sublane.shape[0]):
        live = jnp.where(sublane == slot, mask_ref[slot].astype(jnp.float32), live)
    return live


def entry(neighbours, direction, shape):
    return jnp.broadcast_to(neighbours[:, direction : direction + 1], shape)


def pick(source, index):
    return jnp.take_along_axis(source, index, axis=0)


def roll(x, shift):
    return pltpu.roll(x, shift % LANES if isinstance(shift, int) else shift, 1)


def wrapped(shift):
    return jnp.bitwise_and(shift, LANES - 1)


def device_of(target, slots):
    return lax.shift_right_arithmetic(target, jnp.int32(slots.bit_length() - 1))


def on_device(target, device, slots):
    return (target >= 0) & (device_of(target, slots) == device)


def taps_of(taps_ref):
    return [taps_ref[lag] for lag in range(TIME_HALF + 1)]


def order_of(pair, day, days):
    return [day * (days - 1 - 2 * s) + s if pair else s for s in range(days)]


def coupling_of(factor_ref):
    return [
        [
            factor_ref[a, 0] * factor_ref[b, 0] + factor_ref[a, 1] * factor_ref[b, 1]
            for b in range(2)
        ]
        for a in range(2)
    ]


def same_days(taps, values):
    totals = []
    for t in range(len(values)):
        total = taps[0] * values[t]
        for s in range(len(values)):
            if s != t:
                total = total + taps[abs(s - t)] * values[s]
        totals.append(total)
    return totals


def add_later(taps, totals, values):
    for t in range(len(totals)):
        for s in range(t + 1):
            totals[t] = totals[t] + taps[len(totals) + s - t] * values[s]


def add_earlier(taps, totals, values):
    for t in range(len(totals)):
        for s in range(t, len(totals)):
            totals[t] = totals[t] + taps[len(totals) + t - s] * values[s]


def east_first(place_ref):
    return jnp.bitwise_and(place_ref[0], 1) == 0


def south_first(place_ref):
    return jnp.bitwise_and(place_ref[0], REACH) == 0


def end_slot(nb_ref, me, east):
    slots = nb_ref.shape[0]
    step, directions = (
        (1, (EAST, NORTH_EAST, SOUTH_EAST)) if east else (-1, (WEST, NORTH_WEST, SOUTH_WEST))
    )
    found = jnp.int32(0)
    for slot in range(slots):
        for direction, shift in zip(directions, (0, -REACH, REACH)):
            target = nb_ref[slot, direction]
            hit = (target >= 0) & (device_of(target, slots) == me + step + shift)
            found = jnp.where(hit, slot, found)
    return found


def edge_plan(place_ref, ends_ref):
    first = east_first(place_ref)
    return [(first, ends_ref[0]), (~first, ends_ref[1])]


def strip_starts(place_ref, tiles):
    last = tiles - PAIR_ROWS
    first = south_first(place_ref)
    return [jnp.where(first, last, 0), jnp.where(first, 0, last)]


def own_kernel(place_ref, mask_ref, taps_ref, _, nb_ref, x_ref, own_ref, ends_ref, *edge_refs):
    comps, days, tiles, slots, _ = x_ref.shape
    taps = taps_of(taps_ref)
    me = place_ref[0]
    east, west = end_slot(nb_ref, me, True), end_slot(nb_ref, me, False)
    first = east_first(place_ref)
    ends = [jnp.where(first, east, west), jnp.where(first, west, east)]
    for k, slot in enumerate(ends):
        ends_ref[k] = slot
    for edge_ref, slot in zip(edge_refs, ends):
        live = mask_ref[slot].astype(jnp.float32)
        for comp in range(comps):
            for t in range(days):
                edge_ref[comp * days + t] = live * x_ref[comp, t, :, slot, :]
    def body(tile, _):
        for comp in range(comps):
            values = [x_ref[comp, t, tile] for t in range(days)]
            for t, total in enumerate(same_days(taps, values)):
                own_ref[comp * days + t, tile] = total
        return 0

    lax.fori_loop(0, tiles, body, 0, unroll=4)


def all_days(pair, place_ref, taps_ref, factor_ref, raw_ref, other_refs, read_other):
    comps, days = other_refs[0].shape[:2]
    taps = taps_of(taps_ref)
    coupling = coupling_of(factor_ref)
    order = order_of(pair, place_ref[1], days)
    filtered = []
    for comp in range(comps):
        totals = same_days(taps, [raw_ref[comp * days + order[s]] for s in range(days)])
        later = [read_other(other_refs[-1], comp, order[s]) for s in range(days)]
        add_later(taps, totals, later)
        if not pair:
            earlier = [read_other(other_refs[0], comp, s) for s in range(days)]
            add_earlier(taps, totals, earlier)
        filtered.append(totals)
    for a in range(comps):
        for t in range(days):
            value = coupling[a][0] * filtered[0][t] + coupling[a][1] * filtered[1][t]
            yield a * days + order[t], value


def edge_kernel(pair, place_ref, mask_ref, taps_ref, factor_ref, ends_ref, *refs):
    raw_refs, other_refs, packed_refs = refs[:2], refs[2:-2], refs[-2:]
    tiles = other_refs[0].shape[2]
    column = jnp.bitwise_and(lax.broadcasted_iota(jnp.int32, (tiles, LANES), 1), SIDE - 1)
    group = lax.shift_right_logical(column, jnp.int32(SPACE_HALF.bit_length() - 1))
    for raw_ref, packed_ref, (to_east, slot) in zip(
        raw_refs, packed_refs, edge_plan(place_ref, ends_ref)
    ):
        live = mask_ref[slot].astype(jnp.float32)
        packed = jnp.zeros((tiles, LANES), jnp.float32)
        for at, value in all_days(
            pair, place_ref, taps_ref, factor_ref, raw_ref, other_refs,
            lambda ref, c, s: live * ref[c, s, :, slot, :],
        ):
            shift = wrapped(jnp.where(to_east, LANES - SPACE_HALF * at, SPACE_HALF * at))
            spot = jnp.where(to_east, GROUPS - 1 - at, at)
            packed = jnp.where(group == spot, roll(value, shift), packed)
        packed_ref[...] = packed


def mix_kernel(pair, place_ref, mask_ref, taps_ref, factor_ref, own_ref, *rest):
    *other_refs, mixed_ref, first_ref, second_ref = rest
    _, tiles, slots, _ = mixed_ref.shape
    comps, days = other_refs[0].shape[:2]
    _, sublane = iotas(slots)
    live = live_vector(mask_ref, sublane)
    taps = taps_of(taps_ref)
    weights = [[live * value for value in row] for row in coupling_of(factor_ref)]
    order = order_of(pair, place_ref[1], days)

    def body(tile, _):
        filtered = []
        for comp in range(comps):
            totals = [own_ref[comp * days + order[t], tile] for t in range(days)]
            add_later(taps, totals, [other_refs[-1][comp, order[s], tile] for s in range(days)])
            if not pair:
                add_earlier(taps, totals, [other_refs[0][comp, s, tile] for s in range(days)])
            filtered.append(totals)
        for a in range(comps):
            for t in range(days):
                mixed_ref[a * days + order[t], tile] = (
                    weights[a][0] * filtered[0][t] + weights[a][1] * filtered[1][t]
                )
        return 0

    lax.fori_loop(0, tiles, body, 0, unroll=4)
    for sent_ref, start in zip((first_ref, second_ref), strip_starts(place_ref, tiles)):
        for item in range(comps * days):
            sent_ref[item] = mixed_ref[item, pl.ds(start, PAIR_ROWS)]


def west_east(place_ref, first, second):
    flag = east_first(place_ref)
    return jnp.where(flag, second, first), jnp.where(flag, first, second)


def unpacked(item, west, east):
    column = jnp.bitwise_and(lax.broadcasted_iota(jnp.int32, west.shape, 1), SIDE - 1)
    return jnp.where(
        column >= SIDE // 2,
        roll(west, wrapped(SPACE_HALF * item)),
        roll(east, wrapped(LANES - SPACE_HALF * item)),
    )


def corner_kernel(place_ref, second_ref, first_ref, *refs):
    one_ref, two_ref = refs[-2:]
    slots = one_ref.shape[2]
    south = south_first(place_ref)
    for k, side in enumerate(west_east(place_ref, first_ref[...], second_ref[...])):
        top, bottom = side[:slots], side[-slots:]
        one_ref[0, k] = jnp.where(south, bottom, top)
        two_ref[0, k] = jnp.where(south, top, bottom)


def two_parts(x):
    coarse = x.astype(jnp.bfloat16)
    return coarse, (x - coarse.astype(jnp.float32)).astype(jnp.bfloat16)


def bands_kernel(taps_ref, bands_ref):
    shape = (2 * LANES, LANES)
    source = lax.broadcasted_iota(jnp.int32, shape, 0)
    target = lax.broadcasted_iota(jnp.int32, shape, 1)
    same = jnp.bitwise_and(source // SIDE, 1) == target // SIDE
    source_column = jnp.bitwise_and(source, SIDE - 1)
    outside = jnp.where(source_column >= SIDE // 2, source_column - SIDE, source_column + SIDE)
    position = jnp.where(source < LANES, source_column, outside)
    distance = jnp.abs(position - jnp.bitwise_and(target, SIDE - 1))
    bands = jnp.zeros(shape, jnp.float32)
    for lag in range(SPACE_HALF + 1):
        bands = jnp.where(same & (distance == lag), taps_ref[0, lag], bands)
    coarse, fine = two_parts(bands)
    bands_ref[: 2 * LANES, :LANES] = coarse
    bands_ref[: 2 * LANES, LANES:] = fine
    bands_ref[2 * LANES :, :LANES] = coarse
    bands_ref[2 * LANES :, LANES:] = jnp.zeros_like(fine)


def across(bands, tiles):
    slots = tiles[0][0].shape[0]
    centre_parts = two_parts(jnp.concatenate([centre for centre, _ in tiles], axis=0))
    halo_parts = two_parts(jnp.concatenate([halo for _, halo in tiles], axis=0))
    product = jnp.dot(
        jnp.concatenate([part for both in zip(centre_parts, halo_parts) for part in both], axis=1),
        bands,
        preferred_element_type=jnp.float32,
    )
    product = product[:, :LANES] + product[:, LANES:]
    return [product[slots * p : slots * (p + 1)] for p in range(len(tiles))]


def sides_of(nb, west, east, device, shape):
    slots = shape[0]
    column = jnp.bitwise_and(lax.broadcasted_iota(jnp.int32, shape, 1), SIDE - 1)
    target = jnp.where(column >= SIDE // 2, entry(nb, west, shape), entry(nb, east, shape))
    near = on_device(target, device, slots)
    return jnp.bitwise_and(target, slots - 1), near, (target >= 0) & ~near


def halo_of(source, far, plan):
    index, near, remote = plan
    halo = jnp.where(near, pick(source, index), 0.0)
    return jnp.where(remote, jnp.broadcast_to(far, halo.shape), halo)


def odd_rows(before, after):
    low = lax.broadcasted_iota(jnp.int32, before.shape, 1) < SIDE
    return roll(jnp.where(low, after, before), SIDE)


def inner_kernel(
    place_ref, mask_ref, taps_ref, nb_ref, bands_ref, mixed_ref, second_ref, first_ref,
    out_hbm, outer_ref, out_ref, far_ref, stored,
):
    count, tiles, slots, _ = mixed_ref.shape
    lane, sublane = iotas(slots)
    live = live_vector(mask_ref, sublane)
    taps = [taps_ref[1, lag] for lag in range(SPACE_HALF + 1)]
    plan = sides_of(nb_ref[...], WEST, EAST, place_ref[0], lane.shape)
    west, east = west_east(place_ref, first_ref[...], second_ref[...])
    together = far_ref.shape[0]

    def store(step):
        part = pl.ds(step * together, together)
        return pltpu.make_async_copy(out_ref.at[part], out_hbm.at[part], stored.at[step])

    def body(step, _):
        fetched = []
        for k in range(together):
            item = step * together + k
            far_ref[k] = unpacked(item, west, east)
            for tile in range(tiles):
                centre = mixed_ref[item, tile]
                fetched.append((centre, halo_of(centre, far_ref[k, tile : tile + 1], plan)))
        lines = across(bands_ref[...], fetched)
        zero = jnp.zeros(lane.shape, jnp.float32)
        for k in range(together):
            item = step * together + k
            rows = [zero] * PAIR_ROWS + lines[k * tiles : (k + 1) * tiles] + [zero] * PAIR_ROWS
            odd = [odd_rows(rows[p], rows[p + 1]) for p in range(len(rows) - 1)]
            for p in range(tiles):
                total = taps[0] * rows[p + 2]
                total = total + taps[1] * (odd[p + 1] + odd[p + 2])
                total = total + taps[2] * (rows[p + 1] + rows[p + 3])
                total = total + taps[3] * (odd[p] + odd[p + 3])
                total = total + taps[4] * (rows[p] + rows[p + 4])
                total = live * total
                out_ref[item, p] = total
                if p < PAIR_ROWS:
                    outer_ref[item, p] = total
                elif p >= tiles - PAIR_ROWS:
                    outer_ref[item, p - tiles + 2 * PAIR_ROWS] = total
        store(step).start()
        return 0

    lax.fori_loop(0, count // together, body, 0)
    for step in range(count // together):
        store(step).wait()


def outer_kernel(
    place_ref, mask_ref, taps_ref, nb_ref, bands_ref, outer_ref, second_ref, first_ref,
    _, out_hbm, out_ref, stored,
):
    count, _, slots, _ = outer_ref.shape
    tiles = out_hbm.shape[1]
    lane, sublane = iotas(slots)
    live = live_vector(mask_ref, sublane)
    taps = [taps_ref[1, lag] for lag in range(SPACE_HALF + 1)]
    nb = nb_ref[...]
    me = place_ref[0]
    fetched = []
    for north in (True, False):
        use_first = ~south_first(place_ref) if north else south_first(place_ref)

        def read(index, part, use_first=use_first):
            return jnp.where(use_first, first_ref[index, part], second_ref[index, part])

        target = entry(nb, NORTH if north else SOUTH, lane.shape)
        plan = sides_of(
            nb,
            NORTH_WEST if north else SOUTH_WEST,
            NORTH_EAST if north else SOUTH_EAST,
            me - REACH if north else me + REACH,
            lane.shape,
        )
        corner = [read(count, 0), read(count, 1)]
        for item in range(count):
            far = unpacked(jnp.int32(item), *corner)
            for part in range(PAIR_ROWS):
                source = read(item, part)
                centre = jnp.where(
                    target >= 0, pick(source, jnp.bitwise_and(target, slots - 1)), 0.0
                )
                row = slots - PAIR_ROWS + part if north else part
                fetched.append((centre, halo_of(source, far[row : row + 1], plan)))
    rows = across(bands_ref[...], fetched)
    zero = jnp.zeros(lane.shape, jnp.float32)
    copies = []
    for side in range(2):
        for item in range(count):
            at = (side * count + item) * PAIR_ROWS
            one, two = rows[at : at + PAIR_ROWS]
            close, far = (one, two) if side else (two, one)
            edge = odd_rows(zero, one) if side else odd_rows(two, zero)
            near = taps[1] * edge + taps[2] * close + taps[3] * odd_rows(one, two)
            near = near + taps[4] * far
            off = taps[3] * edge + taps[4] * close
            for part, value in enumerate((off, near) if side else (near, off)):
                out_ref[side, item, part] = (
                    outer_ref[item, side * PAIR_ROWS + part] + live * value
                )
        place = pl.ds(side * (tiles - PAIR_ROWS), PAIR_ROWS)
        copy = pltpu.make_async_copy(out_ref.at[side], out_hbm.at[:, place], stored.at[side])
        copy.start()
        copies.append(copy)
    for copy in copies:
        copy.wait()


def swap_both(first, second, index, length):
    blk, day = lax.axis_size("blk"), lax.axis_size("day")
    results = []
    for x, shift in ((first, 0), (second, 1)):
        partner = {}
        for at in range(shift, length + shift, 2):
            low, high = at % length, (at + 1) % length
            partner[low], partner[high] = high, low
        pairs = []
        for i in range(blk):
            at, step = index(i)
            across_chip = day == 2 and abs(partner[at] - at) > 1
            other = i if across_chip else i + (partner[at] - at) * step
            for core in range(day):
                pairs.append((i * day + core, other * day + (1 - core if across_chip else core)))
        results.append(lax.ppermute(x, ("blk", "day"), pairs))
    return results


def shards(input_field, active_mask, neighbours, time_taps, space_taps, coregion_factor):
    comps, days, slots, cells = input_field.shape
    count = comps * days
    tiles = cells // LANES
    blk = lax.axis_size("blk")
    day = lax.axis_size("day")
    pair = day == 2
    sides = 2
    place = jnp.stack([lax.axis_index("blk"), lax.axis_index("day")]).astype(jnp.int32)

    def in_tiles(x):
        return x.reshape(comps, days, slots, tiles, LANES).transpose(0, 1, 3, 2, 4)

    if pair:
        others = [lax.ppermute(input_field, "day", [(0, 1), (1, 0)])]
    else:
        up = [(i, i + 1) for i in range(day - 1)]
        others = [
            lax.ppermute(input_field, "day", up),
            lax.ppermute(input_field, "day", [(b, a) for a, b in up]),
        ]
    others = [in_tiles(x) for x in others]
    field = array(count, tiles, slots, LANES)

    own, ends, *raw = pl.pallas_call(
        own_kernel,
        out_shape=(field, jax.ShapeDtypeStruct((2,), jnp.int32))
        + (array(count, tiles, LANES),) * 2,
        in_specs=[SMEM] * 5 + [WHOLE],
        out_specs=(WHOLE, SMEM, WHOLE, WHOLE),
        compiler_params=PARAMS,
        name="own_days",
    )(place, active_mask, time_taps, coregion_factor, neighbours, in_tiles(input_field))

    sent_count = count + 1
    sent_shape = array(sent_count, PAIR_ROWS, slots, LANES)
    packed = pl.pallas_call(
        functools.partial(edge_kernel, pair),
        out_shape=(array(tiles, LANES),) * 2,
        in_specs=[SMEM] * 5 + [WHOLE] * (2 + len(others)),
        out_specs=(WHOLE,) * 2,
        compiler_params=PARAMS,
        name="edges",
    )(place, active_mask, time_taps, coregion_factor, ends, *raw, *others)
    first, second = swap_both(*packed, lambda i: (i % REACH, 1), REACH)

    mixed, *sent = pl.pallas_call(
        functools.partial(mix_kernel, pair),
        out_shape=(field, sent_shape, sent_shape),
        in_specs=[SMEM] * 4 + [WHOLE] * (1 + len(others)),
        out_specs=(WHOLE,) * 3,
        compiler_params=PARAMS,
        cost_estimate=pl.CostEstimate(
            flops=20 * field.size, bytes_accessed=12 * field.size, transcendentals=0
        ),
        name="mix",
    )(place, active_mask, time_taps, coregion_factor, own, *others)

    bands = pl.pallas_call(
        bands_kernel,
        out_shape=jax.ShapeDtypeStruct((4 * LANES, 2 * LANES), jnp.bfloat16),
        in_specs=[SMEM],
        out_specs=WHOLE,
        compiler_params=PARAMS,
        name="bands",
    )(space_taps)

    sent = pl.pallas_call(
        corner_kernel,
        grid=(1,),
        out_shape=(sent_shape,) * sides,
        in_specs=[SMEM, WHOLE, WHOLE] + [pl.BlockSpec(memory_space=pl.ANY)] * (sides + 2),
        out_specs=(
            pl.BlockSpec((1, PAIR_ROWS, slots, LANES), lambda i: (sent_count - 1, 0, 0, 0)),
        )
        * sides,
        input_output_aliases={5 + side: side for side in range(sides)},
        compiler_params=PARAMS,
        name="corners",
    )(place, second, first, mixed, bands, *sent)

    one, two = swap_both(*sent, lambda i: (i // REACH, REACH), blk // REACH)

    together = 2
    inner, outer = pl.pallas_call(
        inner_kernel,
        out_shape=(field, array(count, 2 * PAIR_ROWS, slots, LANES)),
        in_specs=[SMEM] * 3 + [WHOLE] * 5,
        out_specs=(IN_HBM, WHOLE),
        scratch_shapes=[
            pltpu.VMEM(field.shape, jnp.float32),
            pltpu.VMEM((together, tiles, LANES), jnp.float32),
            DMA((count // together,)),
        ],
        compiler_params=PARAMS,
        cost_estimate=pl.CostEstimate(
            flops=4 * field.size * LANES, bytes_accessed=8 * field.size, transcendentals=0
        ),
        name="inner_rows",
    )(place, active_mask, space_taps, neighbours, bands, mixed, second, first)

    result = pl.pallas_call(
        outer_kernel,
        out_shape=field,
        in_specs=[SMEM] * 3 + [WHOLE] * 5 + [IN_HBM],
        out_specs=IN_HBM,
        scratch_shapes=[
            pltpu.VMEM((2, count, PAIR_ROWS, slots, LANES), jnp.float32),
            DMA((2,)),
        ],
        input_output_aliases={8: 0},
        compiler_params=PARAMS,
        name="outer_rows",
    )(place, active_mask, space_taps, neighbours, bands, outer, two, one, inner)
    result = result.reshape(comps, days, tiles, slots, LANES).transpose(0, 1, 3, 2, 4)
    return result.reshape(input_field.shape)


def solution(mesh):
    in_specs = (P(None, "day", "blk", None), P("blk"), P("blk", None), P(), P(), P())
    out_specs = P(None, "day", "blk", None)
    return jax.shard_map(shards, mesh=mesh, in_specs=in_specs, out_specs=out_specs, check_vma=False)
```

```python
import functools

import jax
import jax.numpy as jnp
from jax import lax
from jax.experimental import pallas as pl
from jax.experimental.pallas import tpu as pltpu
from jax.sharding import PartitionSpec as P

SIDE = 64
SPACE_HALF = 4
TIME_HALF = 3
REACH = 4
LANES = 128
EAST, WEST, NORTH, SOUTH, NORTH_EAST, NORTH_WEST, SOUTH_EAST, SOUTH_WEST = range(8)
PAIR_ROWS = SPACE_HALF * SIDE // LANES
GROUPS = SIDE // SPACE_HALF
PARAMS = pltpu.CompilerParams(vmem_limit_bytes=12 * 1024 * 1024)
SMEM = pl.BlockSpec(memory_space=pltpu.SMEM)
WHOLE = pl.BlockSpec(memory_space=pltpu.VMEM)
IN_HBM = pl.BlockSpec(memory_space=pltpu.HBM)
DMA = pltpu.SemaphoreType.DMA


def array(*shape):
    return jax.ShapeDtypeStruct(shape, jnp.float32)


def iotas(slots):
    lane = lax.broadcasted_iota(jnp.int32, (slots, LANES), 1)
    sublane = lax.broadcasted_iota(jnp.int32, (slots, LANES), 0)
    return lane, sublane


def live_vector(mask_ref, sublane):
    live = jnp.zeros(sublane.shape, jnp.float32)
    for slot in range(sublane.shape[0]):
        live = jnp.where(sublane == slot, mask_ref[slot].astype(jnp.float32), live)
    return live


def entry(neighbours, direction, shape):
    return jnp.broadcast_to(neighbours[:, direction : direction + 1], shape)


def pick(source, index):
    return jnp.take_along_axis(source, index, axis=0)


def roll(x, shift):
    return pltpu.roll(x, shift % LANES if isinstance(shift, int) else shift, 1)


def wrapped(shift):
    return jnp.bitwise_and(shift, LANES - 1)


def device_of(target, slots):
    return lax.shift_right_arithmetic(target, jnp.int32(slots.bit_length() - 1))


def on_device(target, device, slots):
    return (target >= 0) & (device_of(target, slots) == device)


def taps_of(taps_ref):
    return [taps_ref[lag] for lag in range(TIME_HALF + 1)]


def order_of(pair, day, days):
    return [day * (days - 1 - 2 * s) + s if pair else s for s in range(days)]


def coupling_of(factor_ref):
    return [
        [
            factor_ref[a, 0] * factor_ref[b, 0] + factor_ref[a, 1] * factor_ref[b, 1]
            for b in range(2)
        ]
        for a in range(2)
    ]


def same_days(taps, values):
    totals = []
    for t in range(len(values)):
        total = taps[0] * values[t]
        for s in range(len(values)):
            if s != t:
                total = total + taps[abs(s - t)] * values[s]
        totals.append(total)
    return totals


def add_later(taps, totals, values):
    for t in range(len(totals)):
        for s in range(t + 1):
            totals[t] = totals[t] + taps[len(totals) + s - t] * values[s]


def add_earlier(taps, totals, values):
    for t in range(len(totals)):
        for s in range(t, len(totals)):
            totals[t] = totals[t] + taps[len(totals) + t - s] * values[s]


def east_first(place_ref):
    return jnp.bitwise_and(place_ref[0], 1) == 0


def south_first(place_ref):
    return jnp.bitwise_and(place_ref[0], REACH) == 0


def end_slot(nb_ref, me, east):
    slots = nb_ref.shape[0]
    step, directions = (
        (1, (EAST, NORTH_EAST, SOUTH_EAST)) if east else (-1, (WEST, NORTH_WEST, SOUTH_WEST))
    )
    found = jnp.int32(0)
    for slot in range(slots):
        for direction, shift in zip(directions, (0, -REACH, REACH)):
            target = nb_ref[slot, direction]
            hit = (target >= 0) & (device_of(target, slots) == me + step + shift)
            found = jnp.where(hit, slot, found)
    return found


def edge_plan(place_ref, nb_ref):
    me = place_ref[0]
    east, west = end_slot(nb_ref, me, True), end_slot(nb_ref, me, False)
    first = east_first(place_ref)
    return [(first, jnp.where(first, east, west)), (~first, jnp.where(first, west, east))]


def strip_starts(place_ref, tiles):
    last = tiles - PAIR_ROWS
    first = south_first(place_ref)
    return [jnp.where(first, last, 0), jnp.where(first, 0, last)]


def own_kernel(place_ref, mask_ref, taps_ref, _, nb_ref, x_ref, own_ref, *edge_refs):
    comps, days, tiles, slots, _ = x_ref.shape
    taps = taps_of(taps_ref)
    for edge_ref, (_, slot) in zip(edge_refs, edge_plan(place_ref, nb_ref)):
        live = mask_ref[slot].astype(jnp.float32)
        for comp in range(comps):
            for t in range(days):
                edge_ref[comp * days + t] = live * x_ref[comp, t, :, slot, :]
    def body(tile, _):
        for comp in range(comps):
            values = [x_ref[comp, t, tile] for t in range(days)]
            for t, total in enumerate(same_days(taps, values)):
                own_ref[comp * days + t, tile] = total
        return 0

    lax.fori_loop(0, tiles, body, 0, unroll=4)


def all_days(pair, place_ref, taps_ref, factor_ref, raw_ref, other_refs, read_other):
    comps, days = other_refs[0].shape[:2]
    taps = taps_of(taps_ref)
    coupling = coupling_of(factor_ref)
    order = order_of(pair, place_ref[1], days)
    filtered = []
    for comp in range(comps):
        totals = same_days(taps, [raw_ref[comp * days + order[s]] for s in range(days)])
        later = [read_other(other_refs[-1], comp, order[s]) for s in range(days)]
        add_later(taps, totals, later)
        if not pair:
            earlier = [read_other(other_refs[0], comp, s) for s in range(days)]
            add_earlier(taps, totals, earlier)
        filtered.append(totals)
    for a in range(comps):
        for t in range(days):
            value = coupling[a][0] * filtered[0][t] + coupling[a][1] * filtered[1][t]
            yield a * days + order[t], value


def edge_kernel(pair, place_ref, mask_ref, taps_ref, factor_ref, nb_ref, *refs):
    raw_refs, other_refs, packed_refs = refs[:2], refs[2:-2], refs[-2:]
    tiles = other_refs[0].shape[2]
    column = jnp.bitwise_and(lax.broadcasted_iota(jnp.int32, (tiles, LANES), 1), SIDE - 1)
    group = lax.shift_right_logical(column, jnp.int32(SPACE_HALF.bit_length() - 1))
    for raw_ref, packed_ref, (to_east, slot) in zip(
        raw_refs, packed_refs, edge_plan(place_ref, nb_ref)
    ):
        live = mask_ref[slot].astype(jnp.float32)
        packed = jnp.zeros((tiles, LANES), jnp.float32)
        for at, value in all_days(
            pair, place_ref, taps_ref, factor_ref, raw_ref, other_refs,
            lambda ref, c, s: live * ref[c, s, :, slot, :],
        ):
            shift = wrapped(jnp.where(to_east, LANES - SPACE_HALF * at, SPACE_HALF * at))
            spot = jnp.where(to_east, GROUPS - 1 - at, at)
            packed = jnp.where(group == spot, roll(value, shift), packed)
        packed_ref[...] = packed


def two_parts(x):
    coarse = x.astype(jnp.bfloat16)
    return coarse, (x - coarse.astype(jnp.float32)).astype(jnp.bfloat16)


def build_bands(taps_ref, bands_ref):
    shape = (2 * LANES, LANES)
    source = lax.broadcasted_iota(jnp.int32, shape, 0)
    target = lax.broadcasted_iota(jnp.int32, shape, 1)
    same = jnp.bitwise_and(source // SIDE, 1) == target // SIDE
    source_column = jnp.bitwise_and(source, SIDE - 1)
    outside = jnp.where(source_column >= SIDE // 2, source_column - SIDE, source_column + SIDE)
    position = jnp.where(source < LANES, source_column, outside)
    distance = jnp.abs(position - jnp.bitwise_and(target, SIDE - 1))
    bands = jnp.zeros(shape, jnp.float32)
    for lag in range(SPACE_HALF + 1):
        bands = jnp.where(same & (distance == lag), taps_ref[0, lag], bands)
    coarse, fine = two_parts(bands)
    bands_ref[: 2 * LANES, :LANES] = coarse
    bands_ref[: 2 * LANES, LANES:] = fine
    bands_ref[2 * LANES :, :LANES] = coarse
    bands_ref[2 * LANES :, LANES:] = jnp.zeros_like(fine)


def mix_kernel(pair, place_ref, mask_ref, taps_ref, factor_ref, space_ref, own_ref, *rest):
    *other_refs, mixed_ref, first_ref, second_ref, bands_ref = rest
    build_bands(space_ref, bands_ref)
    _, tiles, slots, _ = mixed_ref.shape
    comps, days = other_refs[0].shape[:2]
    _, sublane = iotas(slots)
    live = live_vector(mask_ref, sublane)
    taps = taps_of(taps_ref)
    weights = [[live * value for value in row] for row in coupling_of(factor_ref)]
    order = order_of(pair, place_ref[1], days)

    def body(tile, _):
        filtered = []
        for comp in range(comps):
            totals = [own_ref[comp * days + order[t], tile] for t in range(days)]
            add_later(taps, totals, [other_refs[-1][comp, order[s], tile] for s in range(days)])
            if not pair:
                add_earlier(taps, totals, [other_refs[0][comp, s, tile] for s in range(days)])
            filtered.append(totals)
        for a in range(comps):
            for t in range(days):
                mixed_ref[a * days + order[t], tile] = (
                    weights[a][0] * filtered[0][t] + weights[a][1] * filtered[1][t]
                )
        return 0

    lax.fori_loop(0, tiles, body, 0, unroll=4)
    for sent_ref, start in zip((first_ref, second_ref), strip_starts(place_ref, tiles)):
        for item in range(comps * days):
            sent_ref[item] = mixed_ref[item, pl.ds(start, PAIR_ROWS)]


def west_east(place_ref, first, second):
    flag = east_first(place_ref)
    return jnp.where(flag, second, first), jnp.where(flag, first, second)


def unpacked(item, west, east):
    column = jnp.bitwise_and(lax.broadcasted_iota(jnp.int32, west.shape, 1), SIDE - 1)
    return jnp.where(
        column >= SIDE // 2,
        roll(west, wrapped(SPACE_HALF * item)),
        roll(east, wrapped(LANES - SPACE_HALF * item)),
    )


def corner_kernel(place_ref, second_ref, first_ref, *refs):
    one_ref, two_ref = refs[-2:]
    slots = one_ref.shape[2]
    south = south_first(place_ref)
    for k, side in enumerate(west_east(place_ref, first_ref[...], second_ref[...])):
        top, bottom = side[:slots], side[-slots:]
        one_ref[0, k] = jnp.where(south, bottom, top)
        two_ref[0, k] = jnp.where(south, top, bottom)


def across(bands, tiles):
    slots = tiles[0][0].shape[0]
    centre_parts = two_parts(jnp.concatenate([centre for centre, _ in tiles], axis=0))
    halo_parts = two_parts(jnp.concatenate([halo for _, halo in tiles], axis=0))
    product = jnp.dot(
        jnp.concatenate([part for both in zip(centre_parts, halo_parts) for part in both], axis=1),
        bands,
        preferred_element_type=jnp.float32,
    )
    product = product[:, :LANES] + product[:, LANES:]
    return [product[slots * p : slots * (p + 1)] for p in range(len(tiles))]


def sides_of(nb, west, east, device, shape):
    slots = shape[0]
    column = jnp.bitwise_and(lax.broadcasted_iota(jnp.int32, shape, 1), SIDE - 1)
    target = jnp.where(column >= SIDE // 2, entry(nb, west, shape), entry(nb, east, shape))
    near = on_device(target, device, slots)
    return jnp.bitwise_and(target, slots - 1), near, (target >= 0) & ~near


def halo_of(source, far, plan):
    index, near, remote = plan
    halo = jnp.where(near, pick(source, index), 0.0)
    return jnp.where(remote, jnp.broadcast_to(far, halo.shape), halo)


def odd_rows(before, after):
    low = lax.broadcasted_iota(jnp.int32, before.shape, 1) < SIDE
    return roll(jnp.where(low, after, before), SIDE)


def inner_kernel(
    place_ref, mask_ref, taps_ref, nb_ref, bands_ref, mixed_ref, second_ref, first_ref,
    out_hbm, outer_ref, out_ref, far_ref, stored,
):
    count, tiles, slots, _ = mixed_ref.shape
    lane, sublane = iotas(slots)
    live = live_vector(mask_ref, sublane)
    taps = [taps_ref[1, lag] for lag in range(SPACE_HALF + 1)]
    plan = sides_of(nb_ref[...], WEST, EAST, place_ref[0], lane.shape)
    west, east = west_east(place_ref, first_ref[...], second_ref[...])
    together = far_ref.shape[0]

    def store(step):
        part = pl.ds(step * together, together)
        return pltpu.make_async_copy(out_ref.at[part], out_hbm.at[part], stored.at[step])

    def body(step, _):
        fetched = []
        for k in range(together):
            item = step * together + k
            far_ref[k] = unpacked(item, west, east)
            for tile in range(tiles):
                centre = mixed_ref[item, tile]
                fetched.append((centre, halo_of(centre, far_ref[k, tile : tile + 1], plan)))
        lines = across(bands_ref[...], fetched)
        zero = jnp.zeros(lane.shape, jnp.float32)
        for k in range(together):
            item = step * together + k
            rows = [zero] * PAIR_ROWS + lines[k * tiles : (k + 1) * tiles] + [zero] * PAIR_ROWS
            odd = [odd_rows(rows[p], rows[p + 1]) for p in range(len(rows) - 1)]
            for p in range(tiles):
                total = taps[0] * rows[p + 2]
                total = total + taps[1] * (odd[p + 1] + odd[p + 2])
                total = total + taps[2] * (rows[p + 1] + rows[p + 3])
                total = total + taps[3] * (odd[p] + odd[p + 3])
                total = total + taps[4] * (rows[p] + rows[p + 4])
                total = live * total
                out_ref[item, p] = total
                if p < PAIR_ROWS:
                    outer_ref[item, p] = total
                elif p >= tiles - PAIR_ROWS:
                    outer_ref[item, p - tiles + 2 * PAIR_ROWS] = total
        store(step).start()
        return 0

    lax.fori_loop(0, count // together, body, 0)
    for step in range(count // together):
        store(step).wait()


def outer_kernel(
    place_ref, mask_ref, taps_ref, nb_ref, bands_ref, outer_ref, first_ref, second_ref,
    _, out_hbm, out_ref, stored,
):
    count, _, slots, _ = outer_ref.shape
    tiles = out_hbm.shape[1]
    lane, sublane = iotas(slots)
    live = live_vector(mask_ref, sublane)
    taps = [taps_ref[1, lag] for lag in range(SPACE_HALF + 1)]
    nb = nb_ref[...]
    me = place_ref[0]
    fetched = []
    for north in (True, False):
        use_first = ~south_first(place_ref) if north else south_first(place_ref)

        def read(index, part, use_first=use_first):
            return jnp.where(use_first, first_ref[index, part], second_ref[index, part])

        target = entry(nb, NORTH if north else SOUTH, lane.shape)
        plan = sides_of(
            nb,
            NORTH_WEST if north else SOUTH_WEST,
            NORTH_EAST if north else SOUTH_EAST,
            me - REACH if north else me + REACH,
            lane.shape,
        )
        corner = [read(count, 0), read(count, 1)]
        for item in range(count):
            far = unpacked(jnp.int32(item), *corner)
            for part in range(PAIR_ROWS):
                source = read(item, part)
                centre = jnp.where(
                    target >= 0, pick(source, jnp.bitwise_and(target, slots - 1)), 0.0
                )
                row = slots - PAIR_ROWS + part if north else part
                fetched.append((centre, halo_of(source, far[row : row + 1], plan)))
    rows = across(bands_ref[...], fetched)
    zero = jnp.zeros(lane.shape, jnp.float32)
    copies = []
    for side in range(2):
        for item in range(count):
            at = (side * count + item) * PAIR_ROWS
            one, two = rows[at : at + PAIR_ROWS]
            close, far = (one, two) if side else (two, one)
            edge = odd_rows(zero, one) if side else odd_rows(two, zero)
            near = taps[1] * edge + taps[2] * close + taps[3] * odd_rows(one, two)
            near = near + taps[4] * far
            off = taps[3] * edge + taps[4] * close
            for part, value in enumerate((off, near) if side else (near, off)):
                out_ref[side, item, part] = (
                    outer_ref[item, side * PAIR_ROWS + part] + live * value
                )
        place = pl.ds(side * (tiles - PAIR_ROWS), PAIR_ROWS)
        copy = pltpu.make_async_copy(out_ref.at[side], out_hbm.at[:, place], stored.at[side])
        copy.start()
        copies.append(copy)
    for copy in copies:
        copy.wait()


def swap_both(first, second, index, length):
    blk, day = lax.axis_size("blk"), lax.axis_size("day")
    results = []
    for x, shift in ((first, 0), (second, 1)):
        partner = {}
        for at in range(shift, length + shift, 2):
            low, high = at % length, (at + 1) % length
            partner[low], partner[high] = high, low
        pairs = []
        for i in range(blk):
            at, step = index(i)
            across_chip = day == 2 and abs(partner[at] - at) > 1
            other = i if across_chip else i + (partner[at] - at) * step
            for core in range(day):
                pairs.append((i * day + core, other * day + (1 - core if across_chip else core)))
        results.append(lax.ppermute(x, ("blk", "day"), pairs))
    return results


def shards(input_field, active_mask, neighbours, time_taps, space_taps, coregion_factor):
    comps, days, slots, cells = input_field.shape
    count = comps * days
    tiles = cells // LANES
    blk = lax.axis_size("blk")
    day = lax.axis_size("day")
    pair = day == 2
    sides = 2
    place = jnp.stack([lax.axis_index("blk"), lax.axis_index("day")]).astype(jnp.int32)

    def in_tiles(x):
        return x.reshape(comps, days, slots, tiles, LANES).transpose(0, 1, 3, 2, 4)

    if pair:
        others = [lax.ppermute(input_field, "day", [(0, 1), (1, 0)])]
    else:
        up = [(i, i + 1) for i in range(day - 1)]
        others = [
            lax.ppermute(input_field, "day", up),
            lax.ppermute(input_field, "day", [(b, a) for a, b in up]),
        ]
    others = [in_tiles(x) for x in others]
    field = array(count, tiles, slots, LANES)

    own, *raw = pl.pallas_call(
        own_kernel,
        out_shape=(field,) + (array(count, tiles, LANES),) * 2,
        in_specs=[SMEM] * 5 + [WHOLE],
        out_specs=(WHOLE,) * 3,
        compiler_params=PARAMS,
        name="own_days",
    )(place, active_mask, time_taps, coregion_factor, neighbours, in_tiles(input_field))

    sent_count = count + 1
    sent_shape = array(sent_count, PAIR_ROWS, slots, LANES)
    packed = pl.pallas_call(
        functools.partial(edge_kernel, pair),
        out_shape=(array(tiles, LANES),) * 2,
        in_specs=[SMEM] * 5 + [WHOLE] * (2 + len(others)),
        out_specs=(WHOLE,) * 2,
        compiler_params=PARAMS,
        name="edges",
    )(place, active_mask, time_taps, coregion_factor, neighbours, *raw, *others)
    first, second = swap_both(*packed, lambda i: (i % REACH, 1), REACH)

    mixed, *sent, bands = pl.pallas_call(
        functools.partial(mix_kernel, pair),
        out_shape=(
            field,
            sent_shape,
            sent_shape,
            jax.ShapeDtypeStruct((4 * LANES, 2 * LANES), jnp.bfloat16),
        ),
        in_specs=[SMEM] * 5 + [WHOLE] * (1 + len(others)),
        out_specs=(WHOLE,) * 4,
        compiler_params=PARAMS,
        cost_estimate=pl.CostEstimate(
            flops=20 * field.size, bytes_accessed=12 * field.size, transcendentals=0
        ),
        name="mix",
    )(place, active_mask, time_taps, coregion_factor, space_taps, own, *others)

    sent = pl.pallas_call(
        corner_kernel,
        grid=(1,),
        out_shape=(sent_shape,) * sides,
        in_specs=[SMEM, WHOLE, WHOLE] + [pl.BlockSpec(memory_space=pl.ANY)] * (sides + 1),
        out_specs=(
            pl.BlockSpec((1, PAIR_ROWS, slots, LANES), lambda i: (sent_count - 1, 0, 0, 0)),
        )
        * sides,
        input_output_aliases={4 + side: side for side in range(sides)},
        compiler_params=PARAMS,
        name="corners",
    )(place, second, first, mixed, *sent)

    one, two = swap_both(*sent, lambda i: (i // REACH, REACH), blk // REACH)

    together = 2
    inner, outer = pl.pallas_call(
        inner_kernel,
        out_shape=(field, array(count, 2 * PAIR_ROWS, slots, LANES)),
        in_specs=[SMEM] * 3 + [WHOLE] * 5,
        out_specs=(IN_HBM, WHOLE),
        scratch_shapes=[
            pltpu.VMEM(field.shape, jnp.float32),
            pltpu.VMEM((together, tiles, LANES), jnp.float32),
            DMA((count // together,)),
        ],
        compiler_params=PARAMS,
        cost_estimate=pl.CostEstimate(
            flops=4 * field.size * LANES, bytes_accessed=8 * field.size, transcendentals=0
        ),
        name="inner_rows",
    )(place, active_mask, space_taps, neighbours, bands, mixed, second, first)

    result = pl.pallas_call(
        outer_kernel,
        out_shape=field,
        in_specs=[SMEM] * 3 + [WHOLE] * 5 + [IN_HBM],
        out_specs=IN_HBM,
        scratch_shapes=[
            pltpu.VMEM((2, count, PAIR_ROWS, slots, LANES), jnp.float32),
            DMA((2,)),
        ],
        input_output_aliases={8: 0},
        compiler_params=PARAMS,
        name="outer_rows",
    )(place, active_mask, space_taps, neighbours, bands, outer, one, two, inner)
    result = result.reshape(comps, days, tiles, slots, LANES).transpose(0, 1, 3, 2, 4)
    return result.reshape(input_field.shape)


def solution(mesh):
    in_specs = (P(None, "day", "blk", None), P("blk"), P("blk", None), P(), P(), P())
    out_specs = P(None, "day", "blk", None)
    return jax.shard_map(shards, mesh=mesh, in_specs=in_specs, out_specs=out_specs, check_vma=False)
```

```python
import functools

import jax
import jax.numpy as jnp
from jax import lax
from jax.experimental import pallas as pl
from jax.experimental.pallas import tpu as pltpu
from jax.sharding import PartitionSpec as P

SIDE = 64
SPACE_HALF = 4
TIME_HALF = 3
REACH = 4
LANES = 128
EAST, WEST, NORTH, SOUTH, NORTH_EAST, NORTH_WEST, SOUTH_EAST, SOUTH_WEST = range(8)
PAIR_ROWS = SPACE_HALF * SIDE // LANES
GROUPS = SIDE // SPACE_HALF
PARAMS = pltpu.CompilerParams(vmem_limit_bytes=12 * 1024 * 1024)
SMEM = pl.BlockSpec(memory_space=pltpu.SMEM)
WHOLE = pl.BlockSpec(memory_space=pltpu.VMEM)
IN_HBM = pl.BlockSpec(memory_space=pltpu.HBM)
DMA = pltpu.SemaphoreType.DMA


def array(*shape):
    return jax.ShapeDtypeStruct(shape, jnp.float32)


def iotas(slots):
    lane = lax.broadcasted_iota(jnp.int32, (slots, LANES), 1)
    sublane = lax.broadcasted_iota(jnp.int32, (slots, LANES), 0)
    return lane, sublane


def live_vector(mask_ref, sublane):
    live = jnp.zeros(sublane.shape, jnp.float32)
    for slot in range(sublane.shape[0]):
        live = jnp.where(sublane == slot, mask_ref[slot].astype(jnp.float32), live)
    return live


def entry(neighbours, direction, shape):
    return jnp.broadcast_to(neighbours[:, direction : direction + 1], shape)


def pick(source, index):
    return jnp.take_along_axis(source, index, axis=0)


def roll(x, shift):
    return pltpu.roll(x, shift % LANES if isinstance(shift, int) else shift, 1)


def wrapped(shift):
    return jnp.bitwise_and(shift, LANES - 1)


def device_of(target, slots):
    return lax.shift_right_arithmetic(target, jnp.int32(slots.bit_length() - 1))


def on_device(target, device, slots):
    return (target >= 0) & (device_of(target, slots) == device)


def taps_of(taps_ref):
    return [taps_ref[lag] for lag in range(TIME_HALF + 1)]


def order_of(pair, day, days):
    return [day * (days - 1 - 2 * s) + s if pair else s for s in range(days)]


def coupling_of(factor_ref):
    return [
        [
            factor_ref[a, 0] * factor_ref[b, 0] + factor_ref[a, 1] * factor_ref[b, 1]
            for b in range(2)
        ]
        for a in range(2)
    ]


def same_days(taps, values):
    totals = []
    for t in range(len(values)):
        total = taps[0] * values[t]
        for s in range(len(values)):
            if s != t:
                total = total + taps[abs(s - t)] * values[s]
        totals.append(total)
    return totals


def add_later(taps, totals, values):
    for t in range(len(totals)):
        for s in range(t + 1):
            totals[t] = totals[t] + taps[len(totals) + s - t] * values[s]


def add_earlier(taps, totals, values):
    for t in range(len(totals)):
        for s in range(t, len(totals)):
            totals[t] = totals[t] + taps[len(totals) + t - s] * values[s]


def east_first(place_ref):
    return jnp.bitwise_and(place_ref[0], 1) == 0


def south_first(place_ref):
    return jnp.bitwise_and(place_ref[0], REACH) == 0


def end_slot(nb_ref, me, east):
    slots = nb_ref.shape[0]
    step, directions = (
        (1, (EAST, NORTH_EAST, SOUTH_EAST)) if east else (-1, (WEST, NORTH_WEST, SOUTH_WEST))
    )
    found = jnp.int32(0)
    for slot in range(slots):
        for direction, shift in zip(directions, (0, -REACH, REACH)):
            target = nb_ref[slot, direction]
            hit = (target >= 0) & (device_of(target, slots) == me + step + shift)
            found = jnp.where(hit, slot, found)
    return found


def edge_plan(place_ref, nb_ref):
    me = place_ref[0]
    east, west = end_slot(nb_ref, me, True), end_slot(nb_ref, me, False)
    first = east_first(place_ref)
    return [(first, jnp.where(first, east, west)), (~first, jnp.where(first, west, east))]


def strip_starts(place_ref, tiles):
    last = tiles - PAIR_ROWS
    first = south_first(place_ref)
    return [jnp.where(first, last, 0), jnp.where(first, 0, last)]


def own_kernel(place_ref, mask_ref, taps_ref, _, nb_ref, x_ref, own_ref, *edge_refs):
    comps, days, tiles, slots, _ = x_ref.shape
    taps = taps_of(taps_ref)
    for edge_ref, (_, slot) in zip(edge_refs, edge_plan(place_ref, nb_ref)):
        live = mask_ref[slot].astype(jnp.float32)
        for comp in range(comps):
            for t in range(days):
                edge_ref[comp * days + t] = live * x_ref[comp, t, :, slot, :]
    def body(tile, _):
        for comp in range(comps):
            values = [x_ref[comp, t, tile] for t in range(days)]
            for t, total in enumerate(same_days(taps, values)):
                own_ref[comp * days + t, tile] = total
        return 0

    lax.fori_loop(0, tiles, body, 0, unroll=4)


def all_days(pair, place_ref, taps_ref, factor_ref, raw_ref, other_refs, read_other):
    comps, days = other_refs[0].shape[:2]
    taps = taps_of(taps_ref)
    coupling = coupling_of(factor_ref)
    order = order_of(pair, place_ref[1], days)
    filtered = []
    for comp in range(comps):
        totals = same_days(taps, [raw_ref[comp * days + order[s]] for s in range(days)])
        later = [read_other(other_refs[-1], comp, order[s]) for s in range(days)]
        add_later(taps, totals, later)
        if not pair:
            earlier = [read_other(other_refs[0], comp, s) for s in range(days)]
            add_earlier(taps, totals, earlier)
        filtered.append(totals)
    for a in range(comps):
        for t in range(days):
            value = coupling[a][0] * filtered[0][t] + coupling[a][1] * filtered[1][t]
            yield a * days + order[t], value


def edge_kernel(pair, place_ref, mask_ref, taps_ref, factor_ref, nb_ref, *refs):
    raw_refs, other_refs, packed_refs = refs[:2], refs[2:-2], refs[-2:]
    tiles = other_refs[0].shape[2]
    column = jnp.bitwise_and(lax.broadcasted_iota(jnp.int32, (tiles, LANES), 1), SIDE - 1)
    group = lax.shift_right_logical(column, jnp.int32(SPACE_HALF.bit_length() - 1))
    for raw_ref, packed_ref, (to_east, slot) in zip(
        raw_refs, packed_refs, edge_plan(place_ref, nb_ref)
    ):
        live = mask_ref[slot].astype(jnp.float32)
        packed = jnp.zeros((tiles, LANES), jnp.float32)
        for at, value in all_days(
            pair, place_ref, taps_ref, factor_ref, raw_ref, other_refs,
            lambda ref, c, s: live * ref[c, s, :, slot, :],
        ):
            shift = wrapped(LANES - SPACE_HALF * at)
            spot = jnp.where(to_east, GROUPS - 1 - at, jnp.bitwise_and(-at, GROUPS - 1))
            packed = jnp.where(group == spot, roll(value, shift), packed)
        packed_ref[...] = packed


def two_parts(x):
    coarse = x.astype(jnp.bfloat16)
    return coarse, (x - coarse.astype(jnp.float32)).astype(jnp.bfloat16)


def build_bands(taps_ref, bands_ref):
    shape = (2 * LANES, 2 * LANES)
    source = lax.broadcasted_iota(jnp.int32, shape, 0)
    target = lax.broadcasted_iota(jnp.int32, shape, 1)
    swapped = jnp.where(target < LANES, 0, SIDE)
    same = jnp.bitwise_and(jnp.bitwise_xor(jnp.bitwise_xor(source, target), swapped), SIDE) == 0
    source_column = jnp.bitwise_and(source, SIDE - 1)
    outside = jnp.where(source_column >= SIDE // 2, source_column - SIDE, source_column + SIDE)
    position = jnp.where(source < LANES, source_column, outside)
    distance = jnp.abs(position - jnp.bitwise_and(target, SIDE - 1))
    bands = jnp.zeros(shape, jnp.float32)
    for lag in range(SPACE_HALF + 1):
        bands = jnp.where(same & (distance == lag), taps_ref[0, lag], bands)
    coarse, fine = two_parts(bands)
    bands_ref[: 2 * LANES] = coarse
    bands_ref[2 * LANES : 4 * LANES] = coarse
    bands_ref[4 * LANES :] = fine


def mix_kernel(pair, place_ref, mask_ref, taps_ref, factor_ref, space_ref, own_ref, *rest):
    *other_refs, mixed_ref, first_ref, second_ref, bands_ref = rest
    build_bands(space_ref, bands_ref)
    _, tiles, slots, _ = mixed_ref.shape
    comps, days = other_refs[0].shape[:2]
    _, sublane = iotas(slots)
    live = live_vector(mask_ref, sublane)
    taps = taps_of(taps_ref)
    weights = [[live * value for value in row] for row in coupling_of(factor_ref)]
    order = order_of(pair, place_ref[1], days)

    def body(tile, _):
        filtered = []
        for comp in range(comps):
            totals = [own_ref[comp * days + order[t], tile] for t in range(days)]
            add_later(taps, totals, [other_refs[-1][comp, order[s], tile] for s in range(days)])
            if not pair:
                add_earlier(taps, totals, [other_refs[0][comp, s, tile] for s in range(days)])
            filtered.append(totals)
        for a in range(comps):
            for t in range(days):
                mixed_ref[a * days + order[t], tile] = (
                    weights[a][0] * filtered[0][t] + weights[a][1] * filtered[1][t]
                )
        return 0

    lax.fori_loop(0, tiles, body, 0, unroll=4)
    for sent_ref, start in zip((first_ref, second_ref), strip_starts(place_ref, tiles)):
        for item in range(comps * days):
            sent_ref[item] = mixed_ref[item, pl.ds(start, PAIR_ROWS)]


def west_east(place_ref, first, second):
    flag = east_first(place_ref)
    return jnp.where(flag, second, first), jnp.where(flag, first, second)


def unpacked(item, west, east):
    lane = lax.broadcasted_iota(jnp.int32, west.shape, 1)
    shift = SPACE_HALF * item
    from_west = jnp.bitwise_and(lane + shift, SIDE // 2) != 0
    return roll(jnp.where(from_west, west, east), shift)


def corner_kernel(place_ref, second_ref, first_ref, *refs):
    one_ref, two_ref = refs[-2:]
    slots = one_ref.shape[2]
    south = south_first(place_ref)
    for k, side in enumerate(west_east(place_ref, first_ref[...], second_ref[...])):
        top, bottom = side[:slots], side[-slots:]
        one_ref[0, k] = jnp.where(south, bottom, top)
        two_ref[0, k] = jnp.where(south, top, bottom)


def across(bands, tiles):
    slots = tiles[0][0].shape[0]
    centre, fine_centre = two_parts(jnp.concatenate([centre for centre, _ in tiles], axis=0))
    halo, fine_halo = two_parts(jnp.concatenate([halo for _, halo in tiles], axis=0))
    product = jnp.dot(
        jnp.concatenate([centre, halo, fine_centre, fine_halo, centre, halo], axis=1),
        bands,
        preferred_element_type=jnp.float32,
    )
    parts = [product[slots * p : slots * (p + 1)] for p in range(len(tiles))]
    return [(part[:, :LANES], part[:, LANES:]) for part in parts]


def sides_of(nb, west, east, device, shape):
    slots = shape[0]
    column = jnp.bitwise_and(lax.broadcasted_iota(jnp.int32, shape, 1), SIDE - 1)
    target = jnp.where(column >= SIDE // 2, entry(nb, west, shape), entry(nb, east, shape))
    near = on_device(target, device, slots)
    return jnp.bitwise_and(target, slots - 1), near, (target >= 0) & ~near


def halo_of(source, far, plan):
    index, near, remote = plan
    halo = jnp.where(near, pick(source, index), 0.0)
    return jnp.where(remote, jnp.broadcast_to(far, halo.shape), halo)


def odd_rows(before, after):
    return jnp.where(lax.broadcasted_iota(jnp.int32, before.shape, 1) < SIDE, before, after)


def inner_kernel(
    place_ref, mask_ref, taps_ref, nb_ref, bands_ref, mixed_ref, second_ref, first_ref,
    out_hbm, outer_ref, out_ref, far_ref, stored,
):
    count, tiles, slots, _ = mixed_ref.shape
    lane, sublane = iotas(slots)
    live = live_vector(mask_ref, sublane)
    taps = [taps_ref[1, lag] for lag in range(SPACE_HALF + 1)]
    plan = sides_of(nb_ref[...], WEST, EAST, place_ref[0], lane.shape)
    west, east = west_east(place_ref, first_ref[...], second_ref[...])
    together = far_ref.shape[0]

    def store(step):
        part = pl.ds(step * together, together)
        return pltpu.make_async_copy(out_ref.at[part], out_hbm.at[part], stored.at[step])

    def body(step, _):
        fetched = []
        for k in range(together):
            item = step * together + k
            far_ref[k] = unpacked(item, west, east)
            for tile in range(tiles):
                centre = mixed_ref[item, tile]
                fetched.append((centre, halo_of(centre, far_ref[k, tile : tile + 1], plan)))
        lines = across(bands_ref[...], fetched)
        zero = jnp.zeros(lane.shape, jnp.float32)
        for k in range(together):
            item = step * together + k
            outside = [(zero, zero)] * PAIR_ROWS
            pairs = outside + lines[k * tiles : (k + 1) * tiles] + outside
            rows = [row for row, _ in pairs]
            odd = [odd_rows(pairs[p][1], pairs[p + 1][1]) for p in range(len(pairs) - 1)]
            for p in range(tiles):
                total = taps[0] * rows[p + 2]
                total = total + taps[1] * (odd[p + 1] + odd[p + 2])
                total = total + taps[2] * (rows[p + 1] + rows[p + 3])
                total = total + taps[3] * (odd[p] + odd[p + 3])
                total = total + taps[4] * (rows[p] + rows[p + 4])
                total = live * total
                out_ref[item, p] = total
                if p < PAIR_ROWS:
                    outer_ref[item, p] = total
                elif p >= tiles - PAIR_ROWS:
                    outer_ref[item, p - tiles + 2 * PAIR_ROWS] = total
        store(step).start()
        return 0

    lax.fori_loop(0, count // together, body, 0)
    for step in range(count // together):
        store(step).wait()


def outer_kernel(
    place_ref, mask_ref, taps_ref, nb_ref, bands_ref, outer_ref, first_ref, second_ref,
    _, out_hbm, out_ref, stored,
):
    count, _, slots, _ = outer_ref.shape
    tiles = out_hbm.shape[1]
    lane, sublane = iotas(slots)
    live = live_vector(mask_ref, sublane)
    taps = [taps_ref[1, lag] for lag in range(SPACE_HALF + 1)]
    nb = nb_ref[...]
    me = place_ref[0]
    fetched = []
    for north in (True, False):
        use_first = ~south_first(place_ref) if north else south_first(place_ref)

        def read(index, part, use_first=use_first):
            return jnp.where(use_first, first_ref[index, part], second_ref[index, part])

        target = entry(nb, NORTH if north else SOUTH, lane.shape)
        plan = sides_of(
            nb,
            NORTH_WEST if north else SOUTH_WEST,
            NORTH_EAST if north else SOUTH_EAST,
            me - REACH if north else me + REACH,
            lane.shape,
        )
        corner = [read(count, 0), read(count, 1)]
        for item in range(count):
            far = unpacked(item, *corner)
            for part in range(PAIR_ROWS):
                source = read(item, part)
                centre = jnp.where(
                    target >= 0, pick(source, jnp.bitwise_and(target, slots - 1)), 0.0
                )
                row = slots - PAIR_ROWS + part if north else part
                fetched.append((centre, halo_of(source, far[row : row + 1], plan)))
    rows = across(bands_ref[...], fetched)
    zero = jnp.zeros(lane.shape, jnp.float32)
    copies = []
    for side in range(2):
        for item in range(count):
            at = (side * count + item) * PAIR_ROWS
            (one, swapped_one), (two, swapped_two) = rows[at : at + PAIR_ROWS]
            close, far = (one, two) if side else (two, one)
            edge = odd_rows(zero, swapped_one) if side else odd_rows(swapped_two, zero)
            near = taps[1] * edge + taps[2] * close
            near = near + taps[3] * odd_rows(swapped_one, swapped_two)
            near = near + taps[4] * far
            off = taps[3] * edge + taps[4] * close
            for part, value in enumerate((off, near) if side else (near, off)):
                out_ref[side, item, part] = (
                    outer_ref[item, side * PAIR_ROWS + part] + live * value
                )
        place = pl.ds(side * (tiles - PAIR_ROWS), PAIR_ROWS)
        copy = pltpu.make_async_copy(out_ref.at[side], out_hbm.at[:, place], stored.at[side])
        copy.start()
        copies.append(copy)
    for copy in copies:
        copy.wait()


def swap_both(first, second, index, length):
    blk, day = lax.axis_size("blk"), lax.axis_size("day")
    results = []
    for x, shift in ((first, 0), (second, 1)):
        partner = {}
        for at in range(shift, length + shift, 2):
            low, high = at % length, (at + 1) % length
            partner[low], partner[high] = high, low
        pairs = []
        for i in range(blk):
            at, step = index(i)
            across_chip = day == 2 and abs(partner[at] - at) > 1
            other = i if across_chip else i + (partner[at] - at) * step
            for core in range(day):
                pairs.append((i * day + core, other * day + (1 - core if across_chip else core)))
        results.append(lax.ppermute(x, ("blk", "day"), pairs))
    return results


def shards(input_field, active_mask, neighbours, time_taps, space_taps, coregion_factor):
    comps, days, slots, cells = input_field.shape
    count = comps * days
    tiles = cells // LANES
    blk = lax.axis_size("blk")
    day = lax.axis_size("day")
    pair = day == 2
    sides = 2
    place = jnp.stack([lax.axis_index("blk"), lax.axis_index("day")]).astype(jnp.int32)

    def in_tiles(x):
        return x.reshape(comps, days, slots, tiles, LANES).transpose(0, 1, 3, 2, 4)

    if pair:
        others = [lax.ppermute(input_field, "day", [(0, 1), (1, 0)])]
    else:
        up = [(i, i + 1) for i in range(day - 1)]
        others = [
            lax.ppermute(input_field, "day", up),
            lax.ppermute(input_field, "day", [(b, a) for a, b in up]),
        ]
    others = [in_tiles(x) for x in others]
    field = array(count, tiles, slots, LANES)

    own, *raw = pl.pallas_call(
        own_kernel,
        out_shape=(field,) + (array(count, tiles, LANES),) * 2,
        in_specs=[SMEM] * 5 + [WHOLE],
        out_specs=(WHOLE,) * 3,
        compiler_params=PARAMS,
        name="own_days",
    )(place, active_mask, time_taps, coregion_factor, neighbours, in_tiles(input_field))

    sent_count = count + 1
    sent_shape = array(sent_count, PAIR_ROWS, slots, LANES)
    packed = pl.pallas_call(
        functools.partial(edge_kernel, pair),
        out_shape=(array(tiles, LANES),) * 2,
        in_specs=[SMEM] * 5 + [WHOLE] * (2 + len(others)),
        out_specs=(WHOLE,) * 2,
        compiler_params=PARAMS,
        name="edges",
    )(place, active_mask, time_taps, coregion_factor, neighbours, *raw, *others)
    first, second = swap_both(*packed, lambda i: (i % REACH, 1), REACH)

    mixed, *sent, bands = pl.pallas_call(
        functools.partial(mix_kernel, pair),
        out_shape=(
            field,
            sent_shape,
            sent_shape,
            jax.ShapeDtypeStruct((6 * LANES, 2 * LANES), jnp.bfloat16),
        ),
        in_specs=[SMEM] * 5 + [WHOLE] * (1 + len(others)),
        out_specs=(WHOLE,) * 4,
        compiler_params=PARAMS,
        cost_estimate=pl.CostEstimate(
            flops=20 * field.size, bytes_accessed=12 * field.size, transcendentals=0
        ),
        name="mix",
    )(place, active_mask, time_taps, coregion_factor, space_taps, own, *others)

    sent = pl.pallas_call(
        corner_kernel,
        grid=(1,),
        out_shape=(sent_shape,) * sides,
        in_specs=[SMEM, WHOLE, WHOLE] + [pl.BlockSpec(memory_space=pl.ANY)] * (sides + 1),
        out_specs=(
            pl.BlockSpec((1, PAIR_ROWS, slots, LANES), lambda i: (sent_count - 1, 0, 0, 0)),
        )
        * sides,
        input_output_aliases={4 + side: side for side in range(sides)},
        compiler_params=PARAMS,
        name="corners",
    )(place, second, first, mixed, *sent)

    one, two = swap_both(*sent, lambda i: (i // REACH, REACH), blk // REACH)

    together = 2
    inner, outer = pl.pallas_call(
        inner_kernel,
        out_shape=(field, array(count, 2 * PAIR_ROWS, slots, LANES)),
        in_specs=[SMEM] * 3 + [WHOLE] * 5,
        out_specs=(IN_HBM, WHOLE),
        scratch_shapes=[
            pltpu.VMEM(field.shape, jnp.float32),
            pltpu.VMEM((together, tiles, LANES), jnp.float32),
            DMA((count // together,)),
        ],
        compiler_params=PARAMS,
        cost_estimate=pl.CostEstimate(
            flops=4 * field.size * LANES, bytes_accessed=8 * field.size, transcendentals=0
        ),
        name="inner_rows",
    )(place, active_mask, space_taps, neighbours, bands, mixed, second, first)

    result = pl.pallas_call(
        outer_kernel,
        out_shape=field,
        in_specs=[SMEM] * 3 + [WHOLE] * 5 + [IN_HBM],
        out_specs=IN_HBM,
        scratch_shapes=[
            pltpu.VMEM((2, count, PAIR_ROWS, slots, LANES), jnp.float32),
            DMA((2,)),
        ],
        input_output_aliases={8: 0},
        compiler_params=PARAMS,
        name="outer_rows",
    )(place, active_mask, space_taps, neighbours, bands, outer, one, two, inner)
    result = result.reshape(comps, days, tiles, slots, LANES).transpose(0, 1, 3, 2, 4)
    return result.reshape(input_field.shape)


def solution(mesh):
    in_specs = (P(None, "day", "blk", None), P("blk"), P("blk", None), P(), P(), P())
    out_specs = P(None, "day", "blk", None)
    return jax.shard_map(shards, mesh=mesh, in_specs=in_specs, out_specs=out_specs, check_vma=False)
```

```python
import functools

import jax
import jax.numpy as jnp
from jax import lax
from jax.experimental import pallas as pl
from jax.experimental.pallas import tpu as pltpu
from jax.sharding import PartitionSpec as P

SIDE = 64
SPACE_HALF = 4
TIME_HALF = 3
REACH = 4
LANES = 128
EAST, WEST, NORTH, SOUTH, NORTH_EAST, NORTH_WEST, SOUTH_EAST, SOUTH_WEST = range(8)
PAIR_ROWS = SPACE_HALF * SIDE // LANES
GROUPS = SIDE // SPACE_HALF
PARAMS = pltpu.CompilerParams(vmem_limit_bytes=12 * 1024 * 1024)
SMEM = pl.BlockSpec(memory_space=pltpu.SMEM)
WHOLE = pl.BlockSpec(memory_space=pltpu.VMEM)
IN_HBM = pl.BlockSpec(memory_space=pltpu.HBM)
DMA = pltpu.SemaphoreType.DMA


def array(*shape):
    return jax.ShapeDtypeStruct(shape, jnp.float32)


def iotas(slots):
    lane = lax.broadcasted_iota(jnp.int32, (slots, LANES), 1)
    sublane = lax.broadcasted_iota(jnp.int32, (slots, LANES), 0)
    return lane, sublane


def live_vector(mask_ref, sublane):
    live = jnp.zeros(sublane.shape, jnp.float32)
    for slot in range(sublane.shape[0]):
        live = jnp.where(sublane == slot, mask_ref[slot].astype(jnp.float32), live)
    return live


def entry(neighbours, direction, shape):
    return jnp.broadcast_to(neighbours[:, direction : direction + 1], shape)


def pick(source, index):
    return jnp.take_along_axis(source, index, axis=0)


def roll(x, shift):
    return pltpu.roll(x, shift % LANES if isinstance(shift, int) else shift, 1)


def wrapped(shift):
    return jnp.bitwise_and(shift, LANES - 1)


def device_of(target, slots):
    return lax.shift_right_arithmetic(target, jnp.int32(slots.bit_length() - 1))


def on_device(target, device, slots):
    return (target >= 0) & (device_of(target, slots) == device)


def taps_of(taps_ref):
    return [taps_ref[lag] for lag in range(TIME_HALF + 1)]


def order_of(pair, day, days):
    return [day * (days - 1 - 2 * s) + s if pair else s for s in range(days)]


def coupling_of(factor_ref):
    return [
        [
            factor_ref[a, 0] * factor_ref[b, 0] + factor_ref[a, 1] * factor_ref[b, 1]
            for b in range(2)
        ]
        for a in range(2)
    ]


def same_days(taps, values):
    totals = []
    for t in range(len(values)):
        total = taps[0] * values[t]
        for s in range(len(values)):
            if s != t:
                total = total + taps[abs(s - t)] * values[s]
        totals.append(total)
    return totals


def add_later(taps, totals, values):
    for t in range(len(totals)):
        for s in range(t + 1):
            totals[t] = totals[t] + taps[len(totals) + s - t] * values[s]


def add_earlier(taps, totals, values):
    for t in range(len(totals)):
        for s in range(t, len(totals)):
            totals[t] = totals[t] + taps[len(totals) + t - s] * values[s]


def east_first(place_ref):
    return jnp.bitwise_and(place_ref[0], 1) == 0


def south_first(place_ref):
    return jnp.bitwise_and(place_ref[0], REACH) == 0


def end_slot(nb_ref, me, east):
    slots = nb_ref.shape[0]
    step, directions = (
        (1, (EAST, NORTH_EAST, SOUTH_EAST)) if east else (-1, (WEST, NORTH_WEST, SOUTH_WEST))
    )
    found = jnp.int32(0)
    for slot in range(slots):
        for direction, shift in zip(directions, (0, -REACH, REACH)):
            target = nb_ref[slot, direction]
            hit = (target >= 0) & (device_of(target, slots) == me + step + shift)
            found = jnp.where(hit, slot, found)
    return found


def edge_plan(place_ref, nb_ref):
    me = place_ref[0]
    east, west = end_slot(nb_ref, me, True), end_slot(nb_ref, me, False)
    first = east_first(place_ref)
    return [(first, jnp.where(first, east, west)), (~first, jnp.where(first, west, east))]


def strip_starts(place_ref, tiles):
    last = tiles - PAIR_ROWS
    first = south_first(place_ref)
    return [jnp.where(first, last, 0), jnp.where(first, 0, last)]


def fold_kernel(x_ref, folded_ref):
    comps, days = x_ref.shape[:2]
    for comp in range(comps):
        folded_ref[comp] = x_ref[comp, 0, :1] + x_ref[comp, days - 1, :1]


def all_days(pair, place_ref, taps_ref, factor_ref, x_ref, other_refs, read):
    comps, days = other_refs[0].shape[:2]
    taps = taps_of(taps_ref)
    coupling = coupling_of(factor_ref)
    order = order_of(pair, place_ref[1], days)
    filtered = []
    for comp in range(comps):
        totals = same_days(taps, [read(x_ref, comp, order[s]) for s in range(days)])
        later = [read(other_refs[-1], comp, order[s]) for s in range(days)]
        add_later(taps, totals, later)
        if not pair:
            earlier = [read(other_refs[0], comp, s) for s in range(days)]
            add_earlier(taps, totals, earlier)
        filtered.append(totals)
    for a in range(comps):
        for t in range(days):
            value = coupling[a][0] * filtered[0][t] + coupling[a][1] * filtered[1][t]
            yield a * days + order[t], value


def edge_kernel(pair, place_ref, mask_ref, taps_ref, factor_ref, nb_ref, *refs):
    x_ref, *other_refs = refs[:-3]
    packed_refs = refs[-2:]
    tiles = other_refs[0].shape[2]
    column = jnp.bitwise_and(lax.broadcasted_iota(jnp.int32, (tiles, LANES), 1), SIDE - 1)
    group = lax.shift_right_logical(column, jnp.int32(SPACE_HALF.bit_length() - 1))
    for packed_ref, (to_east, slot) in zip(packed_refs, edge_plan(place_ref, nb_ref)):
        live = mask_ref[slot].astype(jnp.float32)
        packed = jnp.zeros((tiles, LANES), jnp.float32)
        for at, value in all_days(
            pair, place_ref, taps_ref, factor_ref, x_ref, other_refs,
            lambda ref, c, s: live * ref[c, s, :, slot, :],
        ):
            shift = wrapped(jnp.where(to_east, LANES - SPACE_HALF * at, SPACE_HALF * at))
            spot = jnp.where(to_east, GROUPS - 1 - at, at)
            packed = jnp.where(group == spot, roll(value, shift), packed)
        packed_ref[...] = packed


def two_parts(x):
    coarse = x.astype(jnp.bfloat16)
    return coarse, (x - coarse.astype(jnp.float32)).astype(jnp.bfloat16)


def build_bands(taps_ref, bands_ref):
    shape = (2 * LANES, LANES)
    source = lax.broadcasted_iota(jnp.int32, shape, 0)
    target = lax.broadcasted_iota(jnp.int32, shape, 1)
    same = jnp.bitwise_and(source // SIDE, 1) == target // SIDE
    source_column = jnp.bitwise_and(source, SIDE - 1)
    outside = jnp.where(source_column >= SIDE // 2, source_column - SIDE, source_column + SIDE)
    position = jnp.where(source < LANES, source_column, outside)
    distance = jnp.abs(position - jnp.bitwise_and(target, SIDE - 1))
    bands = jnp.zeros(shape, jnp.float32)
    for lag in range(SPACE_HALF + 1):
        bands = jnp.where(same & (distance == lag), taps_ref[0, lag], bands)
    coarse, fine = two_parts(bands)
    bands_ref[: 2 * LANES, :LANES] = coarse
    bands_ref[: 2 * LANES, LANES:] = fine
    bands_ref[2 * LANES :, :LANES] = coarse
    bands_ref[2 * LANES :, LANES:] = jnp.zeros_like(fine)


def mix_kernel(pair, place_ref, mask_ref, taps_ref, factor_ref, space_ref, x_ref, *rest):
    *other_refs, mixed_ref, first_ref, second_ref, bands_ref = rest
    build_bands(space_ref, bands_ref)
    _, tiles, slots, _ = mixed_ref.shape
    comps, days = other_refs[0].shape[:2]
    _, sublane = iotas(slots)
    live = live_vector(mask_ref, sublane)
    taps = taps_of(taps_ref)
    weights = [[live * value for value in row] for row in coupling_of(factor_ref)]
    order = order_of(pair, place_ref[1], days)

    def body(tile, _):
        filtered = []
        for comp in range(comps):
            totals = same_days(taps, [x_ref[comp, order[t], tile] for t in range(days)])
            add_later(taps, totals, [other_refs[-1][comp, order[s], tile] for s in range(days)])
            if not pair:
                add_earlier(taps, totals, [other_refs[0][comp, s, tile] for s in range(days)])
            filtered.append(totals)
        for a in range(comps):
            for t in range(days):
                mixed_ref[a * days + order[t], tile] = (
                    weights[a][0] * filtered[0][t] + weights[a][1] * filtered[1][t]
                )
        return 0

    lax.fori_loop(0, tiles, body, 0, unroll=4)
    for sent_ref, start in zip((first_ref, second_ref), strip_starts(place_ref, tiles)):
        for item in range(comps * days):
            sent_ref[item] = mixed_ref[item, pl.ds(start, PAIR_ROWS)]


def west_east(place_ref, first, second):
    flag = east_first(place_ref)
    return jnp.where(flag, second, first), jnp.where(flag, first, second)


def unpacked(item, west, east):
    column = jnp.bitwise_and(lax.broadcasted_iota(jnp.int32, west.shape, 1), SIDE - 1)
    return jnp.where(
        column >= SIDE // 2,
        roll(west, wrapped(SPACE_HALF * item)),
        roll(east, wrapped(LANES - SPACE_HALF * item)),
    )


def corner_kernel(place_ref, second_ref, first_ref, *refs):
    one_ref, two_ref = refs[-2:]
    slots = one_ref.shape[2]
    south = south_first(place_ref)
    for k, side in enumerate(west_east(place_ref, first_ref[...], second_ref[...])):
        top, bottom = side[:slots], side[-slots:]
        one_ref[0, k] = jnp.where(south, bottom, top)
        two_ref[0, k] = jnp.where(south, top, bottom)


def across(bands, tiles):
    slots = tiles[0][0].shape[0]
    centre_parts = two_parts(jnp.concatenate([centre for centre, _ in tiles], axis=0))
    halo_parts = two_parts(jnp.concatenate([halo for _, halo in tiles], axis=0))
    product = jnp.dot(
        jnp.concatenate([part for both in zip(centre_parts, halo_parts) for part in both], axis=1),
        bands,
        preferred_element_type=jnp.float32,
    )
    product = product[:, :LANES] + product[:, LANES:]
    return [product[slots * p : slots * (p + 1)] for p in range(len(tiles))]


def sides_of(nb, west, east, device, shape):
    slots = shape[0]
    column = jnp.bitwise_and(lax.broadcasted_iota(jnp.int32, shape, 1), SIDE - 1)
    target = jnp.where(column >= SIDE // 2, entry(nb, west, shape), entry(nb, east, shape))
    near = on_device(target, device, slots)
    return jnp.bitwise_and(target, slots - 1), near, (target >= 0) & ~near


def halo_of(source, far, plan):
    index, near, remote = plan
    halo = jnp.where(near, pick(source, index), 0.0)
    return jnp.where(remote, jnp.broadcast_to(far, halo.shape), halo)


def odd_rows(before, after):
    low = lax.broadcasted_iota(jnp.int32, before.shape, 1) < SIDE
    return roll(jnp.where(low, after, before), SIDE)


def inner_kernel(
    place_ref, mask_ref, taps_ref, nb_ref, bands_ref, mixed_ref, second_ref, first_ref,
    out_hbm, outer_ref, out_ref, far_ref, stored,
):
    count, tiles, slots, _ = mixed_ref.shape
    lane, sublane = iotas(slots)
    live = live_vector(mask_ref, sublane)
    taps = [taps_ref[1, lag] for lag in range(SPACE_HALF + 1)]
    plan = sides_of(nb_ref[...], WEST, EAST, place_ref[0], lane.shape)
    west, east = west_east(place_ref, first_ref[...], second_ref[...])
    together = far_ref.shape[0]

    def store(step):
        part = pl.ds(step * together, together)
        return pltpu.make_async_copy(out_ref.at[part], out_hbm.at[part], stored.at[step])

    def body(step, _):
        fetched = []
        for k in range(together):
            item = step * together + k
            far_ref[k] = unpacked(item, west, east)
            for tile in range(tiles):
                centre = mixed_ref[item, tile]
                fetched.append((centre, halo_of(centre, far_ref[k, tile : tile + 1], plan)))
        lines = across(bands_ref[...], fetched)
        zero = jnp.zeros(lane.shape, jnp.float32)
        for k in range(together):
            item = step * together + k
            rows = [zero] * PAIR_ROWS + lines[k * tiles : (k + 1) * tiles] + [zero] * PAIR_ROWS
            odd = [odd_rows(rows[p], rows[p + 1]) for p in range(len(rows) - 1)]
            for p in range(tiles):
                total = taps[0] * rows[p + 2]
                total = total + taps[1] * (odd[p + 1] + odd[p + 2])
                total = total + taps[2] * (rows[p + 1] + rows[p + 3])
                total = total + taps[3] * (odd[p] + odd[p + 3])
                total = total + taps[4] * (rows[p] + rows[p + 4])
                total = live * total
                out_ref[item, p] = total
                if p < PAIR_ROWS:
                    outer_ref[item, p] = total
                elif p >= tiles - PAIR_ROWS:
                    outer_ref[item, p - tiles + 2 * PAIR_ROWS] = total
        store(step).start()
        return 0

    lax.fori_loop(0, count // together, body, 0)
    for step in range(count // together):
        store(step).wait()


def outer_kernel(
    place_ref, mask_ref, taps_ref, nb_ref, bands_ref, outer_ref, first_ref, second_ref,
    _, out_hbm, out_ref, stored,
):
    count, _, slots, _ = outer_ref.shape
    tiles = out_hbm.shape[1]
    lane, sublane = iotas(slots)
    live = live_vector(mask_ref, sublane)
    taps = [taps_ref[1, lag] for lag in range(SPACE_HALF + 1)]
    nb = nb_ref[...]
    me = place_ref[0]
    fetched = []
    for north in (True, False):
        use_first = ~south_first(place_ref) if north else south_first(place_ref)

        def read(index, part, use_first=use_first):
            return jnp.where(use_first, first_ref[index, part], second_ref[index, part])

        target = entry(nb, NORTH if north else SOUTH, lane.shape)
        plan = sides_of(
            nb,
            NORTH_WEST if north else SOUTH_WEST,
            NORTH_EAST if north else SOUTH_EAST,
            me - REACH if north else me + REACH,
            lane.shape,
        )
        corner = [read(count, 0), read(count, 1)]
        for item in range(count):
            far = unpacked(jnp.int32(item), *corner)
            for part in range(PAIR_ROWS):
                source = read(item, part)
                centre = jnp.where(
                    target >= 0, pick(source, jnp.bitwise_and(target, slots - 1)), 0.0
                )
                row = slots - PAIR_ROWS + part if north else part
                fetched.append((centre, halo_of(source, far[row : row + 1], plan)))
    rows = across(bands_ref[...], fetched)
    zero = jnp.zeros(lane.shape, jnp.float32)
    copies = []
    for side in range(2):
        for item in range(count):
            at = (side * count + item) * PAIR_ROWS
            one, two = rows[at : at + PAIR_ROWS]
            close, far = (one, two) if side else (two, one)
            edge = odd_rows(zero, one) if side else odd_rows(two, zero)
            near = taps[1] * edge + taps[2] * close + taps[3] * odd_rows(one, two)
            near = near + taps[4] * far
            off = taps[3] * edge + taps[4] * close
            for part, value in enumerate((off, near) if side else (near, off)):
                out_ref[side, item, part] = (
                    outer_ref[item, side * PAIR_ROWS + part] + live * value
                )
        place = pl.ds(side * (tiles - PAIR_ROWS), PAIR_ROWS)
        copy = pltpu.make_async_copy(out_ref.at[side], out_hbm.at[:, place], stored.at[side])
        copy.start()
        copies.append(copy)
    for copy in copies:
        copy.wait()


def swap_both(first, second, index, length):
    blk, day = lax.axis_size("blk"), lax.axis_size("day")
    results = []
    for x, shift in ((first, 0), (second, 1)):
        partner = {}
        for at in range(shift, length + shift, 2):
            low, high = at % length, (at + 1) % length
            partner[low], partner[high] = high, low
        pairs = []
        for i in range(blk):
            at, step = index(i)
            across_chip = day == 2 and abs(partner[at] - at) > 1
            other = i if across_chip else i + (partner[at] - at) * step
            for core in range(day):
                pairs.append((i * day + core, other * day + (1 - core if across_chip else core)))
        results.append(lax.ppermute(x, ("blk", "day"), pairs))
    return results


def shards(input_field, active_mask, neighbours, time_taps, space_taps, coregion_factor):
    comps, days, slots, cells = input_field.shape
    count = comps * days
    tiles = cells // LANES
    blk = lax.axis_size("blk")
    day = lax.axis_size("day")
    pair = day == 2
    sides = 2
    place = jnp.stack([lax.axis_index("blk"), lax.axis_index("day")]).astype(jnp.int32)

    def in_tiles(x):
        return x.reshape(comps, days, slots, tiles, LANES).transpose(0, 1, 3, 2, 4)

    if pair:
        others = [lax.ppermute(input_field, "day", [(0, 1), (1, 0)])]
    else:
        up = [(i, i + 1) for i in range(day - 1)]
        others = [
            lax.ppermute(input_field, "day", up),
            lax.ppermute(input_field, "day", [(b, a) for a, b in up]),
        ]
    others = [in_tiles(x) for x in others]
    field = array(count, tiles, slots, LANES)

    x = in_tiles(input_field)
    folded = pl.pallas_call(
        fold_kernel,
        out_shape=array(comps, 1, slots, LANES),
        in_specs=[WHOLE],
        out_specs=WHOLE,
        compiler_params=PARAMS,
        name="fold",
    )(x)

    sent_count = count + 1
    sent_shape = array(sent_count, PAIR_ROWS, slots, LANES)
    packed = pl.pallas_call(
        functools.partial(edge_kernel, pair),
        out_shape=(array(tiles, LANES),) * 2,
        in_specs=[SMEM] * 5
        + [WHOLE] * (1 + len(others))
        + [pl.BlockSpec(memory_space=pl.ANY)],
        out_specs=(WHOLE,) * 2,
        compiler_params=PARAMS,
        name="edges",
    )(place, active_mask, time_taps, coregion_factor, neighbours, x, *others, folded)
    first, second = swap_both(*packed, lambda i: (i % REACH, 1), REACH)

    mixed, *sent, bands = pl.pallas_call(
        functools.partial(mix_kernel, pair),
        out_shape=(
            field,
            sent_shape,
            sent_shape,
            jax.ShapeDtypeStruct((4 * LANES, 2 * LANES), jnp.bfloat16),
        ),
        in_specs=[SMEM] * 5 + [WHOLE] * (1 + len(others)),
        out_specs=(WHOLE,) * 4,
        compiler_params=PARAMS,
        cost_estimate=pl.CostEstimate(
            flops=20 * field.size, bytes_accessed=12 * field.size, transcendentals=0
        ),
        name="mix",
    )(place, active_mask, time_taps, coregion_factor, space_taps, x, *others)

    sent = pl.pallas_call(
        corner_kernel,
        grid=(1,),
        out_shape=(sent_shape,) * sides,
        in_specs=[SMEM, WHOLE, WHOLE] + [pl.BlockSpec(memory_space=pl.ANY)] * (sides + 1),
        out_specs=(
            pl.BlockSpec((1, PAIR_ROWS, slots, LANES), lambda i: (sent_count - 1, 0, 0, 0)),
        )
        * sides,
        input_output_aliases={4 + side: side for side in range(sides)},
        compiler_params=PARAMS,
        name="corners",
    )(place, second, first, mixed, *sent)

    one, two = swap_both(*sent, lambda i: (i // REACH, REACH), blk // REACH)

    together = 2
    inner, outer = pl.pallas_call(
        inner_kernel,
        out_shape=(field, array(count, 2 * PAIR_ROWS, slots, LANES)),
        in_specs=[SMEM] * 3 + [WHOLE] * 5,
        out_specs=(IN_HBM, WHOLE),
        scratch_shapes=[
            pltpu.VMEM(field.shape, jnp.float32),
            pltpu.VMEM((together, tiles, LANES), jnp.float32),
            DMA((count // together,)),
        ],
        compiler_params=PARAMS,
        cost_estimate=pl.CostEstimate(
            flops=4 * field.size * LANES, bytes_accessed=8 * field.size, transcendentals=0
        ),
        name="inner_rows",
    )(place, active_mask, space_taps, neighbours, bands, mixed, second, first)

    result = pl.pallas_call(
        outer_kernel,
        out_shape=field,
        in_specs=[SMEM] * 3 + [WHOLE] * 5 + [IN_HBM],
        out_specs=IN_HBM,
        scratch_shapes=[
            pltpu.VMEM((2, count, PAIR_ROWS, slots, LANES), jnp.float32),
            DMA((2,)),
        ],
        input_output_aliases={8: 0},
        compiler_params=PARAMS,
        name="outer_rows",
    )(place, active_mask, space_taps, neighbours, bands, outer, one, two, inner)
    result = result.reshape(comps, days, tiles, slots, LANES).transpose(0, 1, 3, 2, 4)
    return result.reshape(input_field.shape)


def solution(mesh):
    in_specs = (P(None, "day", "blk", None), P("blk"), P("blk", None), P(), P(), P())
    out_specs = P(None, "day", "blk", None)
    return jax.shard_map(shards, mesh=mesh, in_specs=in_specs, out_specs=out_specs, check_vma=False)
```

```python
import functools

import jax
import jax.numpy as jnp
from jax import lax
from jax.experimental import pallas as pl
from jax.experimental.pallas import tpu as pltpu
from jax.sharding import PartitionSpec as P

SIDE = 64
SPACE_HALF = 4
TIME_HALF = 3
REACH = 4
LANES = 128
EAST, WEST, NORTH, SOUTH, NORTH_EAST, NORTH_WEST, SOUTH_EAST, SOUTH_WEST = range(8)
PAIR_ROWS = SPACE_HALF * SIDE // LANES
GROUPS = SIDE // SPACE_HALF
BESIDE, UPPER, LOWER, EAST_FLAG, SOUTH_FLAG, PLANS = 0, 3, 8, 13, 14, 15
PARAMS = pltpu.CompilerParams(vmem_limit_bytes=12 * 1024 * 1024)
SMEM = pl.BlockSpec(memory_space=pltpu.SMEM)
WHOLE = pl.BlockSpec(memory_space=pltpu.VMEM)
IN_HBM = pl.BlockSpec(memory_space=pltpu.HBM)
DMA = pltpu.SemaphoreType.DMA


def array(*shape):
    return jax.ShapeDtypeStruct(shape, jnp.float32)


def iotas(slots):
    lane = lax.broadcasted_iota(jnp.int32, (slots, LANES), 1)
    sublane = lax.broadcasted_iota(jnp.int32, (slots, LANES), 0)
    return lane, sublane


def live_vector(mask_ref, sublane):
    live = jnp.zeros(sublane.shape, jnp.float32)
    for slot in range(sublane.shape[0]):
        live = jnp.where(sublane == slot, mask_ref[slot].astype(jnp.float32), live)
    return live


def entry(neighbours, direction, shape):
    return jnp.broadcast_to(neighbours[:, direction : direction + 1], shape)


def pick(source, index):
    return jnp.take_along_axis(source, index, axis=0)


def roll(x, shift):
    return pltpu.roll(x, shift % LANES if isinstance(shift, int) else shift, 1)


def wrapped(shift):
    return jnp.bitwise_and(shift, LANES - 1)


def device_of(target, slots):
    return lax.shift_right_arithmetic(target, jnp.int32(slots.bit_length() - 1))


def on_device(target, device, slots):
    return (target >= 0) & (device_of(target, slots) == device)


def taps_of(taps_ref):
    return [taps_ref[lag] for lag in range(TIME_HALF + 1)]


def order_of(pair, day, days):
    return [day * (days - 1 - 2 * s) + s if pair else s for s in range(days)]


def coupling_of(factor_ref):
    return [
        [
            factor_ref[a, 0] * factor_ref[b, 0] + factor_ref[a, 1] * factor_ref[b, 1]
            for b in range(2)
        ]
        for a in range(2)
    ]


def same_days(taps, values):
    totals = []
    for t in range(len(values)):
        total = taps[0] * values[t]
        for s in range(len(values)):
            if s != t:
                total = total + taps[abs(s - t)] * values[s]
        totals.append(total)
    return totals


def add_later(taps, totals, values):
    for t in range(len(totals)):
        for s in range(t + 1):
            totals[t] = totals[t] + taps[len(totals) + s - t] * values[s]


def add_earlier(taps, totals, values):
    for t in range(len(totals)):
        for s in range(t, len(totals)):
            totals[t] = totals[t] + taps[len(totals) + t - s] * values[s]


def east_first(place_ref):
    return jnp.bitwise_and(place_ref[0], 1) == 0


def south_first(place_ref):
    return jnp.bitwise_and(place_ref[0], REACH) == 0


def end_slot(nb_ref, me, east):
    slots = nb_ref.shape[0]
    step, directions = (
        (1, (EAST, NORTH_EAST, SOUTH_EAST)) if east else (-1, (WEST, NORTH_WEST, SOUTH_WEST))
    )
    found = jnp.int32(0)
    for slot in range(slots):
        for direction, shift in zip(directions, (0, -REACH, REACH)):
            target = nb_ref[slot, direction]
            hit = (target >= 0) & (device_of(target, slots) == me + step + shift)
            found = jnp.where(hit, slot, found)
    return found


def edge_plan(place_ref, nb_ref):
    me = place_ref[0]
    east, west = end_slot(nb_ref, me, True), end_slot(nb_ref, me, False)
    first = east_first(place_ref)
    return [(first, jnp.where(first, east, west)), (~first, jnp.where(first, west, east))]


def strip_starts(place_ref, tiles):
    last = tiles - PAIR_ROWS
    first = south_first(place_ref)
    return [jnp.where(first, last, 0), jnp.where(first, 0, last)]


def own_kernel(place_ref, mask_ref, taps_ref, _, nb_ref, x_ref, own_ref, *edge_refs):
    comps, days, tiles, slots, _ = x_ref.shape
    taps = taps_of(taps_ref)
    for edge_ref, (_, slot) in zip(edge_refs, edge_plan(place_ref, nb_ref)):
        live = mask_ref[slot].astype(jnp.float32)
        for comp in range(comps):
            for t in range(days):
                edge_ref[comp * days + t] = live * x_ref[comp, t, :, slot, :]
    def body(tile, _):
        for comp in range(comps):
            values = [x_ref[comp, t, tile] for t in range(days)]
            for t, total in enumerate(same_days(taps, values)):
                own_ref[comp * days + t, tile] = total
        return 0

    lax.fori_loop(0, tiles, body, 0, unroll=4)


def all_days(pair, place_ref, taps_ref, factor_ref, raw_ref, other_refs, read_other):
    comps, days = other_refs[0].shape[:2]
    taps = taps_of(taps_ref)
    coupling = coupling_of(factor_ref)
    order = order_of(pair, place_ref[1], days)
    filtered = []
    for comp in range(comps):
        totals = same_days(taps, [raw_ref[comp * days + order[s]] for s in range(days)])
        later = [read_other(other_refs[-1], comp, order[s]) for s in range(days)]
        add_later(taps, totals, later)
        if not pair:
            earlier = [read_other(other_refs[0], comp, s) for s in range(days)]
            add_earlier(taps, totals, earlier)
        filtered.append(totals)
    for a in range(comps):
        for t in range(days):
            value = coupling[a][0] * filtered[0][t] + coupling[a][1] * filtered[1][t]
            yield a * days + order[t], value


def edge_kernel(pair, place_ref, mask_ref, taps_ref, factor_ref, nb_ref, *refs):
    raw_refs, other_refs, packed_refs = refs[:2], refs[2:-2], refs[-2:]
    tiles = other_refs[0].shape[2]
    column = jnp.bitwise_and(lax.broadcasted_iota(jnp.int32, (tiles, LANES), 1), SIDE - 1)
    group = lax.shift_right_logical(column, jnp.int32(SPACE_HALF.bit_length() - 1))
    for raw_ref, packed_ref, (to_east, slot) in zip(
        raw_refs, packed_refs, edge_plan(place_ref, nb_ref)
    ):
        live = mask_ref[slot].astype(jnp.float32)
        packed = jnp.zeros((tiles, LANES), jnp.float32)
        for at, value in all_days(
            pair, place_ref, taps_ref, factor_ref, raw_ref, other_refs,
            lambda ref, c, s: live * ref[c, s, :, slot, :],
        ):
            shift = wrapped(jnp.where(to_east, LANES - SPACE_HALF * at, SPACE_HALF * at))
            spot = jnp.where(to_east, GROUPS - 1 - at, at)
            packed = jnp.where(group == spot, roll(value, shift), packed)
        packed_ref[...] = packed


def two_parts(x):
    coarse = x.astype(jnp.bfloat16)
    return coarse, (x - coarse.astype(jnp.float32)).astype(jnp.bfloat16)


def build_plans(place_ref, mask_ref, space_ref, nb_ref, level_ref, plan_ref):
    shape = level_ref.shape[1:]
    slots = shape[0]
    nb = nb_ref[...]
    me = place_ref[0]
    for lag in range(SPACE_HALF + 1):
        level_ref[lag] = jnp.full(shape, space_ref[1, lag], jnp.float32)
    level_ref[SPACE_HALF + 1] = live_vector(mask_ref, iotas(slots)[1])

    def put_sides(at, west, east, device):
        index, near, remote = sides_of(nb, west, east, device, shape)
        plan_ref[at] = index
        plan_ref[at + 1] = near.astype(jnp.int32)
        plan_ref[at + 2] = remote.astype(jnp.int32)

    put_sides(BESIDE, WEST, EAST, me)
    put_sides(UPPER, NORTH_WEST, NORTH_EAST, me - REACH)
    put_sides(LOWER, SOUTH_WEST, SOUTH_EAST, me + REACH)
    for at, direction in ((UPPER, NORTH), (LOWER, SOUTH)):
        target = entry(nb, direction, shape)
        plan_ref[at + 3] = jnp.bitwise_and(target, slots - 1)
        plan_ref[at + 4] = (target >= 0).astype(jnp.int32)
    plan_ref[EAST_FLAG] = jnp.full(shape, jnp.where(east_first(place_ref), 1, 0), jnp.int32)
    plan_ref[SOUTH_FLAG] = jnp.full(shape, jnp.where(south_first(place_ref), 1, 0), jnp.int32)


def plan_at(plan_ref, at):
    return plan_ref[at], plan_ref[at + 1] != 0, plan_ref[at + 2] != 0


def flag_of(plan_ref, at, rows):
    return jnp.broadcast_to(plan_ref[at, :1], (rows, LANES)) != 0


def build_bands(taps_ref, bands_ref):
    shape = (2 * LANES, LANES)
    source = lax.broadcasted_iota(jnp.int32, shape, 0)
    target = lax.broadcasted_iota(jnp.int32, shape, 1)
    same = jnp.bitwise_and(source // SIDE, 1) == target // SIDE
    source_column = jnp.bitwise_and(source, SIDE - 1)
    outside = jnp.where(source_column >= SIDE // 2, source_column - SIDE, source_column + SIDE)
    position = jnp.where(source < LANES, source_column, outside)
    distance = jnp.abs(position - jnp.bitwise_and(target, SIDE - 1))
    bands = jnp.zeros(shape, jnp.float32)
    for lag in range(SPACE_HALF + 1):
        bands = jnp.where(same & (distance == lag), taps_ref[0, lag], bands)
    coarse, fine = two_parts(bands)
    bands_ref[: 2 * LANES, :LANES] = coarse
    bands_ref[: 2 * LANES, LANES:] = fine
    bands_ref[2 * LANES :, :LANES] = coarse
    bands_ref[2 * LANES :, LANES:] = jnp.zeros_like(fine)


def mix_kernel(
    pair, place_ref, mask_ref, taps_ref, factor_ref, space_ref, nb_ref, own_ref, *rest
):
    *other_refs, mixed_ref, first_ref, second_ref, bands_ref, level_ref, plan_ref = rest
    build_bands(space_ref, bands_ref)
    build_plans(place_ref, mask_ref, space_ref, nb_ref, level_ref, plan_ref)
    _, tiles, slots, _ = mixed_ref.shape
    comps, days = other_refs[0].shape[:2]
    _, sublane = iotas(slots)
    live = live_vector(mask_ref, sublane)
    taps = taps_of(taps_ref)
    weights = [[live * value for value in row] for row in coupling_of(factor_ref)]
    order = order_of(pair, place_ref[1], days)

    def body(tile, _):
        filtered = []
        for comp in range(comps):
            totals = [own_ref[comp * days + order[t], tile] for t in range(days)]
            add_later(taps, totals, [other_refs[-1][comp, order[s], tile] for s in range(days)])
            if not pair:
                add_earlier(taps, totals, [other_refs[0][comp, s, tile] for s in range(days)])
            filtered.append(totals)
        for a in range(comps):
            for t in range(days):
                mixed_ref[a * days + order[t], tile] = (
                    weights[a][0] * filtered[0][t] + weights[a][1] * filtered[1][t]
                )
        return 0

    lax.fori_loop(0, tiles, body, 0, unroll=4)
    for sent_ref, start in zip((first_ref, second_ref), strip_starts(place_ref, tiles)):
        for item in range(comps * days):
            sent_ref[item] = mixed_ref[item, pl.ds(start, PAIR_ROWS)]


def west_east(plan_ref, first, second):
    flag = flag_of(plan_ref, EAST_FLAG, first.shape[0])
    return jnp.where(flag, second, first), jnp.where(flag, first, second)


def unpacked(item, west, east):
    column = jnp.bitwise_and(lax.broadcasted_iota(jnp.int32, west.shape, 1), SIDE - 1)
    return jnp.where(
        column >= SIDE // 2,
        roll(west, wrapped(SPACE_HALF * item)),
        roll(east, wrapped(LANES - SPACE_HALF * item)),
    )


def corner_kernel(plan_ref, second_ref, first_ref, *refs):
    one_ref, two_ref = refs[-2:]
    slots = one_ref.shape[2]
    south = flag_of(plan_ref, SOUTH_FLAG, slots)
    for k, side in enumerate(west_east(plan_ref, first_ref[...], second_ref[...])):
        top, bottom = side[:slots], side[-slots:]
        one_ref[0, k] = jnp.where(south, bottom, top)
        two_ref[0, k] = jnp.where(south, top, bottom)


def across(bands, tiles):
    slots = tiles[0][0].shape[0]
    centre_parts = two_parts(jnp.concatenate([centre for centre, _ in tiles], axis=0))
    halo_parts = two_parts(jnp.concatenate([halo for _, halo in tiles], axis=0))
    product = jnp.dot(
        jnp.concatenate([part for both in zip(centre_parts, halo_parts) for part in both], axis=1),
        bands,
        preferred_element_type=jnp.float32,
    )
    product = product[:, :LANES] + product[:, LANES:]
    return [product[slots * p : slots * (p + 1)] for p in range(len(tiles))]


def sides_of(nb, west, east, device, shape):
    slots = shape[0]
    column = jnp.bitwise_and(lax.broadcasted_iota(jnp.int32, shape, 1), SIDE - 1)
    target = jnp.where(column >= SIDE // 2, entry(nb, west, shape), entry(nb, east, shape))
    near = on_device(target, device, slots)
    return jnp.bitwise_and(target, slots - 1), near, (target >= 0) & ~near


def halo_of(source, far, plan):
    index, near, remote = plan
    halo = jnp.where(near, pick(source, index), 0.0)
    return jnp.where(remote, jnp.broadcast_to(far, halo.shape), halo)


def odd_rows(before, after):
    low = lax.broadcasted_iota(jnp.int32, before.shape, 1) < SIDE
    return roll(jnp.where(low, after, before), SIDE)


def inner_kernel(
    level_ref, plan_ref, bands_ref, mixed_ref, second_ref, first_ref,
    out_hbm, outer_ref, out_ref, far_ref, stored,
):
    count, tiles, slots, _ = mixed_ref.shape
    lane, sublane = iotas(slots)
    live = level_ref[SPACE_HALF + 1]
    taps = [level_ref[lag] for lag in range(SPACE_HALF + 1)]
    plan = plan_at(plan_ref, BESIDE)
    west, east = west_east(plan_ref, first_ref[...], second_ref[...])
    together = far_ref.shape[0]

    def store(step):
        part = pl.ds(step * together, together)
        return pltpu.make_async_copy(out_ref.at[part], out_hbm.at[part], stored.at[step])

    def body(step, _):
        fetched = []
        for k in range(together):
            item = step * together + k
            far_ref[k] = unpacked(item, west, east)
            for tile in range(tiles):
                centre = mixed_ref[item, tile]
                fetched.append((centre, halo_of(centre, far_ref[k, tile : tile + 1], plan)))
        lines = across(bands_ref[...], fetched)
        zero = jnp.zeros(lane.shape, jnp.float32)
        for k in range(together):
            item = step * together + k
            rows = [zero] * PAIR_ROWS + lines[k * tiles : (k + 1) * tiles] + [zero] * PAIR_ROWS
            odd = [odd_rows(rows[p], rows[p + 1]) for p in range(len(rows) - 1)]
            for p in range(tiles):
                total = taps[0] * rows[p + 2]
                total = total + taps[1] * (odd[p + 1] + odd[p + 2])
                total = total + taps[2] * (rows[p + 1] + rows[p + 3])
                total = total + taps[3] * (odd[p] + odd[p + 3])
                total = total + taps[4] * (rows[p] + rows[p + 4])
                total = live * total
                out_ref[item, p] = total
                if p < PAIR_ROWS:
                    outer_ref[item, p] = total
                elif p >= tiles - PAIR_ROWS:
                    outer_ref[item, p - tiles + 2 * PAIR_ROWS] = total
        store(step).start()
        return 0

    lax.fori_loop(0, count // together, body, 0)
    for step in range(count // together):
        store(step).wait()


def outer_kernel(
    level_ref, plan_ref, bands_ref, outer_ref, first_ref, second_ref,
    _, out_hbm, out_ref, stored,
):
    count, _, slots, _ = outer_ref.shape
    tiles = out_hbm.shape[1]
    lane, sublane = iotas(slots)
    live = level_ref[SPACE_HALF + 1]
    taps = [level_ref[lag] for lag in range(SPACE_HALF + 1)]
    south = plan_ref[SOUTH_FLAG] != 0
    fetched = []
    for north in (True, False):
        use_first = ~south if north else south

        def read(index, part, use_first=use_first):
            return jnp.where(use_first, first_ref[index, part], second_ref[index, part])

        at = UPPER if north else LOWER
        plan = plan_at(plan_ref, at)
        index, present = plan_ref[at + 3], plan_ref[at + 4] != 0
        corner = [read(count, 0), read(count, 1)]
        for item in range(count):
            far = unpacked(jnp.int32(item), *corner)
            for part in range(PAIR_ROWS):
                source = read(item, part)
                centre = jnp.where(present, pick(source, index), 0.0)
                row = slots - PAIR_ROWS + part if north else part
                fetched.append((centre, halo_of(source, far[row : row + 1], plan)))
    rows = across(bands_ref[...], fetched)
    zero = jnp.zeros(lane.shape, jnp.float32)
    copies = []
    for side in range(2):
        for item in range(count):
            at = (side * count + item) * PAIR_ROWS
            one, two = rows[at : at + PAIR_ROWS]
            close, far = (one, two) if side else (two, one)
            edge = odd_rows(zero, one) if side else odd_rows(two, zero)
            near = taps[1] * edge + taps[2] * close + taps[3] * odd_rows(one, two)
            near = near + taps[4] * far
            off = taps[3] * edge + taps[4] * close
            for part, value in enumerate((off, near) if side else (near, off)):
                out_ref[side, item, part] = (
                    outer_ref[item, side * PAIR_ROWS + part] + live * value
                )
        place = pl.ds(side * (tiles - PAIR_ROWS), PAIR_ROWS)
        copy = pltpu.make_async_copy(out_ref.at[side], out_hbm.at[:, place], stored.at[side])
        copy.start()
        copies.append(copy)
    for copy in copies:
        copy.wait()


def swap_both(first, second, index, length):
    blk, day = lax.axis_size("blk"), lax.axis_size("day")
    results = []
    for x, shift in ((first, 0), (second, 1)):
        partner = {}
        for at in range(shift, length + shift, 2):
            low, high = at % length, (at + 1) % length
            partner[low], partner[high] = high, low
        pairs = []
        for i in range(blk):
            at, step = index(i)
            across_chip = day == 2 and abs(partner[at] - at) > 1
            other = i if across_chip else i + (partner[at] - at) * step
            for core in range(day):
                pairs.append((i * day + core, other * day + (1 - core if across_chip else core)))
        results.append(lax.ppermute(x, ("blk", "day"), pairs))
    return results


def shards(input_field, active_mask, neighbours, time_taps, space_taps, coregion_factor):
    comps, days, slots, cells = input_field.shape
    count = comps * days
    tiles = cells // LANES
    blk = lax.axis_size("blk")
    day = lax.axis_size("day")
    pair = day == 2
    sides = 2
    place = jnp.stack([lax.axis_index("blk"), lax.axis_index("day")]).astype(jnp.int32)

    def in_tiles(x):
        return x.reshape(comps, days, slots, tiles, LANES).transpose(0, 1, 3, 2, 4)

    if pair:
        others = [lax.ppermute(input_field, "day", [(0, 1), (1, 0)])]
    else:
        up = [(i, i + 1) for i in range(day - 1)]
        others = [
            lax.ppermute(input_field, "day", up),
            lax.ppermute(input_field, "day", [(b, a) for a, b in up]),
        ]
    others = [in_tiles(x) for x in others]
    field = array(count, tiles, slots, LANES)

    own, *raw = pl.pallas_call(
        own_kernel,
        out_shape=(field,) + (array(count, tiles, LANES),) * 2,
        in_specs=[SMEM] * 5 + [WHOLE],
        out_specs=(WHOLE,) * 3,
        compiler_params=PARAMS,
        name="own_days",
    )(place, active_mask, time_taps, coregion_factor, neighbours, in_tiles(input_field))

    sent_count = count + 1
    sent_shape = array(sent_count, PAIR_ROWS, slots, LANES)
    packed = pl.pallas_call(
        functools.partial(edge_kernel, pair),
        out_shape=(array(tiles, LANES),) * 2,
        in_specs=[SMEM] * 5 + [WHOLE] * (2 + len(others)),
        out_specs=(WHOLE,) * 2,
        compiler_params=PARAMS,
        name="edges",
    )(place, active_mask, time_taps, coregion_factor, neighbours, *raw, *others)
    first, second = swap_both(*packed, lambda i: (i % REACH, 1), REACH)

    mixed, *sent, bands, level, plan = pl.pallas_call(
        functools.partial(mix_kernel, pair),
        out_shape=(
            field,
            sent_shape,
            sent_shape,
            jax.ShapeDtypeStruct((4 * LANES, 2 * LANES), jnp.bfloat16),
            array(SPACE_HALF + 2, slots, LANES),
            jax.ShapeDtypeStruct((PLANS, slots, LANES), jnp.int32),
        ),
        in_specs=[SMEM] * 5 + [WHOLE] * (2 + len(others)),
        out_specs=(WHOLE,) * 6,
        compiler_params=PARAMS,
        cost_estimate=pl.CostEstimate(
            flops=20 * field.size, bytes_accessed=12 * field.size, transcendentals=0
        ),
        name="mix",
    )(place, active_mask, time_taps, coregion_factor, space_taps, neighbours, own, *others)

    sent = pl.pallas_call(
        corner_kernel,
        grid=(1,),
        out_shape=(sent_shape,) * sides,
        in_specs=[WHOLE] * 3 + [pl.BlockSpec(memory_space=pl.ANY)] * (sides + 1),
        out_specs=(
            pl.BlockSpec((1, PAIR_ROWS, slots, LANES), lambda i: (sent_count - 1, 0, 0, 0)),
        )
        * sides,
        input_output_aliases={4 + side: side for side in range(sides)},
        compiler_params=PARAMS,
        name="corners",
    )(plan, second, first, mixed, *sent)

    one, two = swap_both(*sent, lambda i: (i // REACH, REACH), blk // REACH)

    together = 2
    inner, outer = pl.pallas_call(
        inner_kernel,
        out_shape=(field, array(count, 2 * PAIR_ROWS, slots, LANES)),
        in_specs=[WHOLE] * 6,
        out_specs=(IN_HBM, WHOLE),
        scratch_shapes=[
            pltpu.VMEM(field.shape, jnp.float32),
            pltpu.VMEM((together, tiles, LANES), jnp.float32),
            DMA((count // together,)),
        ],
        compiler_params=PARAMS,
        cost_estimate=pl.CostEstimate(
            flops=4 * field.size * LANES, bytes_accessed=8 * field.size, transcendentals=0
        ),
        name="inner_rows",
    )(level, plan, bands, mixed, second, first)

    result = pl.pallas_call(
        outer_kernel,
        out_shape=field,
        in_specs=[WHOLE] * 6 + [IN_HBM],
        out_specs=IN_HBM,
        scratch_shapes=[
            pltpu.VMEM((2, count, PAIR_ROWS, slots, LANES), jnp.float32),
            DMA((2,)),
        ],
        input_output_aliases={6: 0},
        compiler_params=PARAMS,
        name="outer_rows",
    )(level, plan, bands, outer, one, two, inner)
    result = result.reshape(comps, days, tiles, slots, LANES).transpose(0, 1, 3, 2, 4)
    return result.reshape(input_field.shape)


def solution(mesh):
    in_specs = (P(None, "day", "blk", None), P("blk"), P("blk", None), P(), P(), P())
    out_specs = P(None, "day", "blk", None)
    return jax.shard_map(shards, mesh=mesh, in_specs=in_specs, out_specs=out_specs, check_vma=False)
```

```python
import functools

import jax
import jax.numpy as jnp
from jax import lax
from jax.experimental import pallas as pl
from jax.experimental.pallas import tpu as pltpu
from jax.sharding import PartitionSpec as P

SIDE = 64
SPACE_HALF = 4
TIME_HALF = 3
REACH = 4
LANES = 128
EAST, WEST, NORTH, SOUTH, NORTH_EAST, NORTH_WEST, SOUTH_EAST, SOUTH_WEST = range(8)
PAIR_ROWS = SPACE_HALF * SIDE // LANES
GROUPS = SIDE // SPACE_HALF
BESIDE, UPPER, LOWER, EAST_FLAG, SOUTH_FLAG, PLANS = 0, 3, 8, 13, 14, 15
PICK, COUPLING, TAPS, LATER, EARLIER, EAST_LEVEL, VALUES = 0, 16, 20, 24, 33, 42, 43
PARAMS = pltpu.CompilerParams(vmem_limit_bytes=12 * 1024 * 1024)
SMEM = pl.BlockSpec(memory_space=pltpu.SMEM)
WHOLE = pl.BlockSpec(memory_space=pltpu.VMEM)
IN_HBM = pl.BlockSpec(memory_space=pltpu.HBM)
DMA = pltpu.SemaphoreType.DMA


def array(*shape):
    return jax.ShapeDtypeStruct(shape, jnp.float32)


def iotas(slots):
    lane = lax.broadcasted_iota(jnp.int32, (slots, LANES), 1)
    sublane = lax.broadcasted_iota(jnp.int32, (slots, LANES), 0)
    return lane, sublane


def live_vector(mask_ref, sublane):
    live = jnp.zeros(sublane.shape, jnp.float32)
    for slot in range(sublane.shape[0]):
        live = jnp.where(sublane == slot, mask_ref[slot].astype(jnp.float32), live)
    return live


def entry(neighbours, direction, shape):
    return jnp.broadcast_to(neighbours[:, direction : direction + 1], shape)


def pick(source, index):
    return jnp.take_along_axis(source, index, axis=0)


def roll(x, shift):
    return pltpu.roll(x, shift % LANES if isinstance(shift, int) else shift, 1)


def wrapped(shift):
    return jnp.bitwise_and(shift, LANES - 1)


def device_of(target, slots):
    return lax.shift_right_arithmetic(target, jnp.int32(slots.bit_length() - 1))


def on_device(target, device, slots):
    return (target >= 0) & (device_of(target, slots) == device)


def taps_of(taps_ref):
    return [taps_ref[lag] for lag in range(TIME_HALF + 1)]


def order_of(pair, day, days):
    return [day * (days - 1 - 2 * s) + s if pair else s for s in range(days)]


def coupling_of(factor_ref):
    return [
        [
            factor_ref[a, 0] * factor_ref[b, 0] + factor_ref[a, 1] * factor_ref[b, 1]
            for b in range(2)
        ]
        for a in range(2)
    ]


def same_days(taps, values):
    totals = []
    for t in range(len(values)):
        total = taps[0] * values[t]
        for s in range(len(values)):
            if s != t:
                total = total + taps[abs(s - t)] * values[s]
        totals.append(total)
    return totals


def add_later(taps, totals, values):
    for t in range(len(totals)):
        for s in range(t + 1):
            totals[t] = totals[t] + taps[len(totals) + s - t] * values[s]


def add_earlier(taps, totals, values):
    for t in range(len(totals)):
        for s in range(t, len(totals)):
            totals[t] = totals[t] + taps[len(totals) + t - s] * values[s]


def east_first(place_ref):
    return jnp.bitwise_and(place_ref[0], 1) == 0


def south_first(place_ref):
    return jnp.bitwise_and(place_ref[0], REACH) == 0


def end_slot(nb_ref, me, east):
    slots = nb_ref.shape[0]
    step, directions = (
        (1, (EAST, NORTH_EAST, SOUTH_EAST)) if east else (-1, (WEST, NORTH_WEST, SOUTH_WEST))
    )
    found = jnp.int32(0)
    for slot in range(slots):
        for direction, shift in zip(directions, (0, -REACH, REACH)):
            target = nb_ref[slot, direction]
            hit = (target >= 0) & (device_of(target, slots) == me + step + shift)
            found = jnp.where(hit, slot, found)
    return found


def edge_plan(place_ref, nb_ref):
    me = place_ref[0]
    east, west = end_slot(nb_ref, me, True), end_slot(nb_ref, me, False)
    first = east_first(place_ref)
    return [(first, jnp.where(first, east, west)), (~first, jnp.where(first, west, east))]


def strip_starts(place_ref, tiles):
    last = tiles - PAIR_ROWS
    first = south_first(place_ref)
    return [jnp.where(first, last, 0), jnp.where(first, 0, last)]


def write_values(pair, place_ref, mask_ref, taps, factor_ref, ends, value_ref):
    shape = value_ref.shape[1:]
    slots = shape[0]
    days = len(taps) - 1

    def put(at, value):
        value_ref[at] = jnp.full(shape, value, jnp.float32)

    for k, (_, slot) in enumerate(ends):
        live = mask_ref[slot].astype(jnp.float32)
        for s in range(slots):
            put(PICK + k * slots + s, jnp.where(slot == s, live, 0.0))
    for a, row in enumerate(coupling_of(factor_ref)):
        for b, value in enumerate(row):
            put(COUPLING + 2 * a + b, value)
    for lag, value in enumerate(taps):
        put(TAPS + lag, value)
    for t in range(days):
        for s in range(days):
            later = taps[days + s - t] if s <= t else 0.0
            earlier = taps[days + t - s] if s >= t else 0.0
            if pair:
                later = jnp.where(place_ref[1] == 0, later, earlier)
            put(LATER + t * days + s, later)
            put(EARLIER + t * days + s, earlier)
    put(EAST_LEVEL, jnp.where(east_first(place_ref), 1.0, 0.0))


def own_kernel(
    pair, place_ref, mask_ref, taps_ref, factor_ref, nb_ref, x_ref, own_ref, *refs
):
    *edge_refs, value_ref = refs
    comps, days, tiles, slots, _ = x_ref.shape
    taps = taps_of(taps_ref)
    ends = edge_plan(place_ref, nb_ref)
    write_values(pair, place_ref, mask_ref, taps, factor_ref, ends, value_ref)
    for edge_ref, (_, slot) in zip(edge_refs, ends):
        live = mask_ref[slot].astype(jnp.float32)
        for comp in range(comps):
            for t in range(days):
                edge_ref[comp * days + t] = live * x_ref[comp, t, :, slot, :]
    def body(tile, _):
        for comp in range(comps):
            values = [x_ref[comp, t, tile] for t in range(days)]
            for t, total in enumerate(same_days(taps, values)):
                own_ref[comp * days + t, tile] = total
        return 0

    lax.fori_loop(0, tiles, body, 0, unroll=4)


def edge_kernel(pair, value_ref, *refs):
    raw_refs, other_refs, packed_refs = refs[:2], refs[2:-2], refs[-2:]
    comps, days, tiles, slots, _ = other_refs[0].shape
    column = jnp.bitwise_and(lax.broadcasted_iota(jnp.int32, (tiles, LANES), 1), SIDE - 1)
    group = lax.shift_right_logical(column, jnp.int32(SPACE_HALF.bit_length() - 1))

    def level(at):
        return jnp.concatenate([value_ref[at]] * (tiles // slots), axis=0)

    taps = [level(TAPS + lag) for lag in range(TIME_HALF + 1)]
    sources = [(other_refs[-1], LATER)] + ([] if pair else [(other_refs[0], EARLIER)])
    filtered = [[], []]
    for comp in range(comps):
        totals = [
            same_days(taps, [raw_ref[comp * days + s] for s in range(days)]) for raw_ref in raw_refs
        ]
        for source, base in sources:
            for s in range(days):
                edges = [None, None]
                for slot in range(slots):
                    value = source[comp, s, :, slot, :]
                    for k in range(2):
                        term = level(PICK + k * slots + slot) * value
                        edges[k] = term if edges[k] is None else edges[k] + term
                for t in range(days):
                    factor = level(base + t * days + s)
                    for k in range(2):
                        totals[k][t] = totals[k][t] + factor * edges[k]
        for k in range(2):
            filtered[k].append(totals[k])
    for k, packed_ref in enumerate(packed_refs):
        to_east = (level(EAST_LEVEL) > 0.5) if k == 0 else (level(EAST_LEVEL) < 0.5)
        packed = jnp.zeros((tiles, LANES), jnp.float32)
        for a in range(comps):
            for t in range(days):
                at = a * days + t
                value = level(COUPLING + 2 * a) * filtered[k][0][t]
                value = value + level(COUPLING + 2 * a + 1) * filtered[k][1][t]
                spot = jnp.where(to_east, GROUPS - 1 - at, -at % GROUPS)
                packed = jnp.where(group == spot, roll(value, -SPACE_HALF * at), packed)
        packed_ref[...] = packed


def two_parts(x):
    coarse = x.astype(jnp.bfloat16)
    return coarse, (x - coarse.astype(jnp.float32)).astype(jnp.bfloat16)


def build_plans(place_ref, mask_ref, space_ref, nb_ref, level_ref, plan_ref):
    shape = level_ref.shape[1:]
    slots = shape[0]
    nb = nb_ref[...]
    me = place_ref[0]
    for lag in range(SPACE_HALF + 1):
        level_ref[lag] = jnp.full(shape, space_ref[1, lag], jnp.float32)
    level_ref[SPACE_HALF + 1] = live_vector(mask_ref, iotas(slots)[1])

    def put_sides(at, west, east, device):
        index, near, remote = sides_of(nb, west, east, device, shape)
        plan_ref[at] = index
        plan_ref[at + 1] = near.astype(jnp.int32)
        plan_ref[at + 2] = remote.astype(jnp.int32)

    put_sides(BESIDE, WEST, EAST, me)
    put_sides(UPPER, NORTH_WEST, NORTH_EAST, me - REACH)
    put_sides(LOWER, SOUTH_WEST, SOUTH_EAST, me + REACH)
    for at, direction in ((UPPER, NORTH), (LOWER, SOUTH)):
        target = entry(nb, direction, shape)
        plan_ref[at + 3] = jnp.bitwise_and(target, slots - 1)
        plan_ref[at + 4] = (target >= 0).astype(jnp.int32)
    plan_ref[EAST_FLAG] = jnp.full(shape, jnp.where(east_first(place_ref), 1, 0), jnp.int32)
    plan_ref[SOUTH_FLAG] = jnp.full(shape, jnp.where(south_first(place_ref), 1, 0), jnp.int32)


def plan_at(plan_ref, at):
    return plan_ref[at], plan_ref[at + 1] != 0, plan_ref[at + 2] != 0


def flag_of(plan_ref, at, rows):
    return jnp.broadcast_to(plan_ref[at, :1], (rows, LANES)) != 0


def build_bands(taps_ref, bands_ref):
    shape = (2 * LANES, LANES)
    source = lax.broadcasted_iota(jnp.int32, shape, 0)
    target = lax.broadcasted_iota(jnp.int32, shape, 1)
    same = jnp.bitwise_and(source // SIDE, 1) == target // SIDE
    source_column = jnp.bitwise_and(source, SIDE - 1)
    outside = jnp.where(source_column >= SIDE // 2, source_column - SIDE, source_column + SIDE)
    position = jnp.where(source < LANES, source_column, outside)
    distance = jnp.abs(position - jnp.bitwise_and(target, SIDE - 1))
    bands = jnp.zeros(shape, jnp.float32)
    for lag in range(SPACE_HALF + 1):
        bands = jnp.where(same & (distance == lag), taps_ref[0, lag], bands)
    coarse, fine = two_parts(bands)
    bands_ref[: 2 * LANES, :LANES] = coarse
    bands_ref[: 2 * LANES, LANES:] = fine
    bands_ref[2 * LANES :, :LANES] = coarse
    bands_ref[2 * LANES :, LANES:] = jnp.zeros_like(fine)


def mix_kernel(
    pair, place_ref, mask_ref, taps_ref, factor_ref, space_ref, nb_ref, own_ref, *rest
):
    *other_refs, mixed_ref, first_ref, second_ref, bands_ref, level_ref, plan_ref = rest
    build_bands(space_ref, bands_ref)
    build_plans(place_ref, mask_ref, space_ref, nb_ref, level_ref, plan_ref)
    _, tiles, slots, _ = mixed_ref.shape
    comps, days = other_refs[0].shape[:2]
    _, sublane = iotas(slots)
    live = live_vector(mask_ref, sublane)
    taps = taps_of(taps_ref)
    weights = [[live * value for value in row] for row in coupling_of(factor_ref)]
    order = order_of(pair, place_ref[1], days)

    def body(tile, _):
        filtered = []
        for comp in range(comps):
            totals = [own_ref[comp * days + order[t], tile] for t in range(days)]
            add_later(taps, totals, [other_refs[-1][comp, order[s], tile] for s in range(days)])
            if not pair:
                add_earlier(taps, totals, [other_refs[0][comp, s, tile] for s in range(days)])
            filtered.append(totals)
        for a in range(comps):
            for t in range(days):
                mixed_ref[a * days + order[t], tile] = (
                    weights[a][0] * filtered[0][t] + weights[a][1] * filtered[1][t]
                )
        return 0

    lax.fori_loop(0, tiles, body, 0, unroll=4)
    for sent_ref, start in zip((first_ref, second_ref), strip_starts(place_ref, tiles)):
        for item in range(comps * days):
            sent_ref[item] = mixed_ref[item, pl.ds(start, PAIR_ROWS)]


def west_east(plan_ref, first, second):
    flag = flag_of(plan_ref, EAST_FLAG, first.shape[0])
    return jnp.where(flag, second, first), jnp.where(flag, first, second)


def unpacked(item, west, east):
    lane = lax.broadcasted_iota(jnp.int32, west.shape, 1)
    shift = SPACE_HALF * item
    from_west = jnp.bitwise_and(lane + shift, SIDE // 2) != 0
    return roll(jnp.where(from_west, west, east), shift)


def corner_kernel(plan_ref, second_ref, first_ref, *refs):
    one_ref, two_ref = refs[-2:]
    slots = one_ref.shape[2]
    south = flag_of(plan_ref, SOUTH_FLAG, slots)
    for k, side in enumerate(west_east(plan_ref, first_ref[...], second_ref[...])):
        top, bottom = side[:slots], side[-slots:]
        one_ref[0, k] = jnp.where(south, bottom, top)
        two_ref[0, k] = jnp.where(south, top, bottom)


def across(bands, tiles):
    slots = tiles[0][0].shape[0]
    centre_parts = two_parts(jnp.concatenate([centre for centre, _ in tiles], axis=0))
    halo_parts = two_parts(jnp.concatenate([halo for _, halo in tiles], axis=0))
    product = jnp.dot(
        jnp.concatenate([part for both in zip(centre_parts, halo_parts) for part in both], axis=1),
        bands,
        preferred_element_type=jnp.float32,
    )
    product = product[:, :LANES] + product[:, LANES:]
    return [product[slots * p : slots * (p + 1)] for p in range(len(tiles))]


def sides_of(nb, west, east, device, shape):
    slots = shape[0]
    column = jnp.bitwise_and(lax.broadcasted_iota(jnp.int32, shape, 1), SIDE - 1)
    target = jnp.where(column >= SIDE // 2, entry(nb, west, shape), entry(nb, east, shape))
    near = on_device(target, device, slots)
    return jnp.bitwise_and(target, slots - 1), near, (target >= 0) & ~near


def halo_of(source, far, plan):
    index, near, remote = plan
    halo = jnp.where(near, pick(source, index), 0.0)
    return jnp.where(remote, jnp.broadcast_to(far, halo.shape), halo)


def odd_rows(before, after):
    low = lax.broadcasted_iota(jnp.int32, before.shape, 1) < SIDE
    return roll(jnp.where(low, after, before), SIDE)


def inner_kernel(
    level_ref, plan_ref, bands_ref, mixed_ref, second_ref, first_ref,
    out_hbm, outer_ref, out_ref, far_ref, stored,
):
    count, tiles, slots, _ = mixed_ref.shape
    lane, sublane = iotas(slots)
    live = level_ref[SPACE_HALF + 1]
    taps = [level_ref[lag] for lag in range(SPACE_HALF + 1)]
    plan = plan_at(plan_ref, BESIDE)
    west, east = west_east(plan_ref, first_ref[...], second_ref[...])
    together = far_ref.shape[0]

    def store(step):
        part = pl.ds(step * together, together)
        return pltpu.make_async_copy(out_ref.at[part], out_hbm.at[part], stored.at[step])

    def body(step, _):
        fetched = []
        for k in range(together):
            item = step * together + k
            far_ref[k] = unpacked(item, west, east)
            for tile in range(tiles):
                centre = mixed_ref[item, tile]
                fetched.append((centre, halo_of(centre, far_ref[k, tile : tile + 1], plan)))
        lines = across(bands_ref[...], fetched)
        zero = jnp.zeros(lane.shape, jnp.float32)
        for k in range(together):
            item = step * together + k
            rows = [zero] * PAIR_ROWS + lines[k * tiles : (k + 1) * tiles] + [zero] * PAIR_ROWS
            odd = [odd_rows(rows[p], rows[p + 1]) for p in range(len(rows) - 1)]
            for p in range(tiles):
                total = taps[0] * rows[p + 2]
                total = total + taps[1] * (odd[p + 1] + odd[p + 2])
                total = total + taps[2] * (rows[p + 1] + rows[p + 3])
                total = total + taps[3] * (odd[p] + odd[p + 3])
                total = total + taps[4] * (rows[p] + rows[p + 4])
                total = live * total
                out_ref[item, p] = total
                if p < PAIR_ROWS:
                    outer_ref[item, p] = total
                elif p >= tiles - PAIR_ROWS:
                    outer_ref[item, p - tiles + 2 * PAIR_ROWS] = total
        store(step).start()
        return 0

    lax.fori_loop(0, count // together, body, 0)
    for step in range(count // together):
        store(step).wait()


def outer_kernel(
    level_ref, plan_ref, bands_ref, outer_ref, first_ref, second_ref,
    _, out_hbm, out_ref, stored,
):
    count, _, slots, _ = outer_ref.shape
    tiles = out_hbm.shape[1]
    lane, sublane = iotas(slots)
    live = level_ref[SPACE_HALF + 1]
    taps = [level_ref[lag] for lag in range(SPACE_HALF + 1)]
    south = plan_ref[SOUTH_FLAG] != 0
    fetched = []
    for north in (True, False):
        use_first = ~south if north else south

        def read(index, part, use_first=use_first):
            return jnp.where(use_first, first_ref[index, part], second_ref[index, part])

        at = UPPER if north else LOWER
        plan = plan_at(plan_ref, at)
        index, present = plan_ref[at + 3], plan_ref[at + 4] != 0
        corner = [read(count, 0), read(count, 1)]
        for item in range(count):
            far = unpacked(item, *corner)
            for part in range(PAIR_ROWS):
                source = read(item, part)
                centre = jnp.where(present, pick(source, index), 0.0)
                row = slots - PAIR_ROWS + part if north else part
                fetched.append((centre, halo_of(source, far[row : row + 1], plan)))
    rows = across(bands_ref[...], fetched)
    zero = jnp.zeros(lane.shape, jnp.float32)
    copies = []
    for side in range(2):
        for item in range(count):
            at = (side * count + item) * PAIR_ROWS
            one, two = rows[at : at + PAIR_ROWS]
            close, far = (one, two) if side else (two, one)
            edge = odd_rows(zero, one) if side else odd_rows(two, zero)
            near = taps[1] * edge + taps[2] * close + taps[3] * odd_rows(one, two)
            near = near + taps[4] * far
            off = taps[3] * edge + taps[4] * close
            for part, value in enumerate((off, near) if side else (near, off)):
                out_ref[side, item, part] = (
                    outer_ref[item, side * PAIR_ROWS + part] + live * value
                )
        place = pl.ds(side * (tiles - PAIR_ROWS), PAIR_ROWS)
        copy = pltpu.make_async_copy(out_ref.at[side], out_hbm.at[:, place], stored.at[side])
        copy.start()
        copies.append(copy)
    for copy in copies:
        copy.wait()


def swap_both(first, second, index, length):
    blk, day = lax.axis_size("blk"), lax.axis_size("day")
    results = []
    for x, shift in ((first, 0), (second, 1)):
        partner = {}
        for at in range(shift, length + shift, 2):
            low, high = at % length, (at + 1) % length
            partner[low], partner[high] = high, low
        pairs = []
        for i in range(blk):
            at, step = index(i)
            across_chip = day == 2 and abs(partner[at] - at) > 1
            other = i if across_chip else i + (partner[at] - at) * step
            for core in range(day):
                pairs.append((i * day + core, other * day + (1 - core if across_chip else core)))
        results.append(lax.ppermute(x, ("blk", "day"), pairs))
    return results


def shards(input_field, active_mask, neighbours, time_taps, space_taps, coregion_factor):
    comps, days, slots, cells = input_field.shape
    count = comps * days
    tiles = cells // LANES
    blk = lax.axis_size("blk")
    day = lax.axis_size("day")
    pair = day == 2
    sides = 2
    place = jnp.stack([lax.axis_index("blk"), lax.axis_index("day")]).astype(jnp.int32)

    def in_tiles(x):
        return x.reshape(comps, days, slots, tiles, LANES).transpose(0, 1, 3, 2, 4)

    if pair:
        others = [lax.ppermute(input_field, "day", [(0, 1), (1, 0)])]
    else:
        up = [(i, i + 1) for i in range(day - 1)]
        others = [
            lax.ppermute(input_field, "day", up),
            lax.ppermute(input_field, "day", [(b, a) for a, b in up]),
        ]
    others = [in_tiles(x) for x in others]
    field = array(count, tiles, slots, LANES)

    own, *raw, values = pl.pallas_call(
        functools.partial(own_kernel, pair),
        out_shape=(field,)
        + (array(count, tiles, LANES),) * 2
        + (array(VALUES, slots, LANES),),
        in_specs=[SMEM] * 5 + [WHOLE],
        out_specs=(WHOLE,) * 4,
        compiler_params=PARAMS,
        name="own_days",
    )(place, active_mask, time_taps, coregion_factor, neighbours, in_tiles(input_field))

    sent_count = count + 1
    sent_shape = array(sent_count, PAIR_ROWS, slots, LANES)
    packed = pl.pallas_call(
        functools.partial(edge_kernel, pair),
        out_shape=(array(tiles, LANES),) * 2,
        in_specs=[WHOLE] * (3 + len(others)),
        out_specs=(WHOLE,) * 2,
        compiler_params=PARAMS,
        name="edges",
    )(values, *raw, *others)
    first, second = swap_both(*packed, lambda i: (i % REACH, 1), REACH)

    mixed, *sent, bands, level, plan = pl.pallas_call(
        functools.partial(mix_kernel, pair),
        out_shape=(
            field,
            sent_shape,
            sent_shape,
            jax.ShapeDtypeStruct((4 * LANES, 2 * LANES), jnp.bfloat16),
            array(SPACE_HALF + 2, slots, LANES),
            jax.ShapeDtypeStruct((PLANS, slots, LANES), jnp.int32),
        ),
        in_specs=[SMEM] * 5 + [WHOLE] * (2 + len(others)),
        out_specs=(WHOLE,) * 6,
        compiler_params=PARAMS,
        cost_estimate=pl.CostEstimate(
            flops=20 * field.size, bytes_accessed=12 * field.size, transcendentals=0
        ),
        name="mix",
    )(place, active_mask, time_taps, coregion_factor, space_taps, neighbours, own, *others)

    sent = pl.pallas_call(
        corner_kernel,
        grid=(1,),
        out_shape=(sent_shape,) * sides,
        in_specs=[WHOLE] * 3 + [pl.BlockSpec(memory_space=pl.ANY)] * (sides + 1),
        out_specs=(
            pl.BlockSpec((1, PAIR_ROWS, slots, LANES), lambda i: (sent_count - 1, 0, 0, 0)),
        )
        * sides,
        input_output_aliases={4 + side: side for side in range(sides)},
        compiler_params=PARAMS,
        name="corners",
    )(plan, second, first, mixed, *sent)

    one, two = swap_both(*sent, lambda i: (i // REACH, REACH), blk // REACH)

    together = 2
    inner, outer = pl.pallas_call(
        inner_kernel,
        out_shape=(field, array(count, 2 * PAIR_ROWS, slots, LANES)),
        in_specs=[WHOLE] * 6,
        out_specs=(IN_HBM, WHOLE),
        scratch_shapes=[
            pltpu.VMEM(field.shape, jnp.float32),
            pltpu.VMEM((together, tiles, LANES), jnp.float32),
            DMA((count // together,)),
        ],
        compiler_params=PARAMS,
        cost_estimate=pl.CostEstimate(
            flops=4 * field.size * LANES, bytes_accessed=8 * field.size, transcendentals=0
        ),
        name="inner_rows",
    )(level, plan, bands, mixed, second, first)

    result = pl.pallas_call(
        outer_kernel,
        out_shape=field,
        in_specs=[WHOLE] * 6 + [IN_HBM],
        out_specs=IN_HBM,
        scratch_shapes=[
            pltpu.VMEM((2, count, PAIR_ROWS, slots, LANES), jnp.float32),
            DMA((2,)),
        ],
        input_output_aliases={6: 0},
        compiler_params=PARAMS,
        name="outer_rows",
    )(level, plan, bands, outer, one, two, inner)
    result = result.reshape(comps, days, tiles, slots, LANES).transpose(0, 1, 3, 2, 4)
    return result.reshape(input_field.shape)


def solution(mesh):
    in_specs = (P(None, "day", "blk", None), P("blk"), P("blk", None), P(), P(), P())
    out_specs = P(None, "day", "blk", None)
    return jax.shard_map(shards, mesh=mesh, in_specs=in_specs, out_specs=out_specs, check_vma=False)
```

```python
import functools

import jax
import jax.numpy as jnp
from jax import lax
from jax.experimental import pallas as pl
from jax.experimental.pallas import tpu as pltpu
from jax.sharding import PartitionSpec as P

SIDE = 64
SPACE_HALF = 4
TIME_HALF = 3
REACH = 4
LANES = 128
EAST, WEST, NORTH, SOUTH, NORTH_EAST, NORTH_WEST, SOUTH_EAST, SOUTH_WEST = range(8)
PAIR_ROWS = SPACE_HALF * SIDE // LANES
GROUPS = SIDE // SPACE_HALF
BESIDE, UPPER, LOWER, EAST_FLAG, SOUTH_FLAG, PLANS = 0, 3, 8, 13, 14, 15
PICK, COUPLING, TAPS, LATER, EARLIER, EAST_LEVEL, VALUES = 0, 16, 20, 24, 33, 42, 43
PARAMS = pltpu.CompilerParams(vmem_limit_bytes=12 * 1024 * 1024)
SMEM = pl.BlockSpec(memory_space=pltpu.SMEM)
WHOLE = pl.BlockSpec(memory_space=pltpu.VMEM)
IN_HBM = pl.BlockSpec(memory_space=pltpu.HBM)
DMA = pltpu.SemaphoreType.DMA


def array(*shape):
    return jax.ShapeDtypeStruct(shape, jnp.float32)


def iotas(slots):
    lane = lax.broadcasted_iota(jnp.int32, (slots, LANES), 1)
    sublane = lax.broadcasted_iota(jnp.int32, (slots, LANES), 0)
    return lane, sublane


def live_vector(mask_ref, sublane):
    live = jnp.zeros(sublane.shape, jnp.float32)
    for slot in range(sublane.shape[0]):
        live = jnp.where(sublane == slot, mask_ref[slot].astype(jnp.float32), live)
    return live


def entry(neighbours, direction, shape):
    return jnp.broadcast_to(neighbours[:, direction : direction + 1], shape)


def pick(source, index):
    return jnp.take_along_axis(source, index, axis=0)


def roll(x, shift):
    return pltpu.roll(x, shift % LANES if isinstance(shift, int) else shift, 1)


def wrapped(shift):
    return jnp.bitwise_and(shift, LANES - 1)


def device_of(target, slots):
    return lax.shift_right_arithmetic(target, jnp.int32(slots.bit_length() - 1))


def on_device(target, device, slots):
    return (target >= 0) & (device_of(target, slots) == device)


def taps_of(taps_ref):
    return [taps_ref[lag] for lag in range(TIME_HALF + 1)]


def order_of(pair, day, days):
    return [day * (days - 1 - 2 * s) + s if pair else s for s in range(days)]


def coupling_of(factor_ref):
    return [
        [
            factor_ref[a, 0] * factor_ref[b, 0] + factor_ref[a, 1] * factor_ref[b, 1]
            for b in range(2)
        ]
        for a in range(2)
    ]


def same_days(taps, values):
    totals = []
    for t in range(len(values)):
        total = taps[0] * values[t]
        for s in range(len(values)):
            if s != t:
                total = total + taps[abs(s - t)] * values[s]
        totals.append(total)
    return totals


def add_later(taps, totals, values):
    for t in range(len(totals)):
        for s in range(t + 1):
            totals[t] = totals[t] + taps[len(totals) + s - t] * values[s]


def add_earlier(taps, totals, values):
    for t in range(len(totals)):
        for s in range(t, len(totals)):
            totals[t] = totals[t] + taps[len(totals) + t - s] * values[s]


def east_first(place_ref):
    return jnp.bitwise_and(place_ref[0], 1) == 0


def south_first(place_ref):
    return jnp.bitwise_and(place_ref[0], REACH) == 0


def end_slot(nb_ref, me, east):
    slots = nb_ref.shape[0]
    step, directions = (
        (1, (EAST, NORTH_EAST, SOUTH_EAST)) if east else (-1, (WEST, NORTH_WEST, SOUTH_WEST))
    )
    found = jnp.int32(0)
    for slot in range(slots):
        for direction, shift in zip(directions, (0, -REACH, REACH)):
            target = nb_ref[slot, direction]
            hit = (target >= 0) & (device_of(target, slots) == me + step + shift)
            found = jnp.where(hit, slot, found)
    return found


def edge_plan(place_ref, nb_ref):
    me = place_ref[0]
    east, west = end_slot(nb_ref, me, True), end_slot(nb_ref, me, False)
    first = east_first(place_ref)
    return [(first, jnp.where(first, east, west)), (~first, jnp.where(first, west, east))]


def strip_starts(place_ref, tiles):
    last = tiles - PAIR_ROWS
    first = south_first(place_ref)
    return [jnp.where(first, last, 0), jnp.where(first, 0, last)]


def write_values(pair, place_ref, mask_ref, taps, factor_ref, ends, value_ref):
    shape = value_ref.shape[1:]
    slots = shape[0]
    days = len(taps) - 1

    def put(at, value):
        value_ref[at] = jnp.full(shape, value, jnp.float32)

    for k, (_, slot) in enumerate(ends):
        live = mask_ref[slot].astype(jnp.float32)
        for s in range(slots):
            put(PICK + k * slots + s, jnp.where(slot == s, live, 0.0))
    for a, row in enumerate(coupling_of(factor_ref)):
        for b, value in enumerate(row):
            put(COUPLING + 2 * a + b, value)
    for lag, value in enumerate(taps):
        put(TAPS + lag, value)
    for t in range(days):
        for s in range(days):
            later = taps[days + s - t] if s <= t else 0.0
            earlier = taps[days + t - s] if s >= t else 0.0
            if pair:
                later = jnp.where(place_ref[1] == 0, later, earlier)
            put(LATER + t * days + s, later)
            put(EARLIER + t * days + s, earlier)
    put(EAST_LEVEL, jnp.where(east_first(place_ref), 1.0, 0.0))


def own_kernel(
    pair, place_ref, mask_ref, taps_ref, factor_ref, nb_ref, x_ref, *refs
):
    *edge_refs, value_ref = refs
    comps, days, tiles, slots, _ = x_ref.shape
    taps = taps_of(taps_ref)
    ends = edge_plan(place_ref, nb_ref)
    write_values(pair, place_ref, mask_ref, taps, factor_ref, ends, value_ref)
    for edge_ref, (_, slot) in zip(edge_refs, ends):
        live = mask_ref[slot].astype(jnp.float32)
        for comp in range(comps):
            for t in range(days):
                edge_ref[comp * days + t] = live * x_ref[comp, t, :, slot, :]


def edge_kernel(pair, value_ref, *refs):
    raw_refs, other_refs, packed_refs = refs[:2], refs[2:-2], refs[-2:]
    comps, days, tiles, slots, _ = other_refs[0].shape
    column = jnp.bitwise_and(lax.broadcasted_iota(jnp.int32, (tiles, LANES), 1), SIDE - 1)
    group = lax.shift_right_logical(column, jnp.int32(SPACE_HALF.bit_length() - 1))

    def level(at):
        return jnp.concatenate([value_ref[at]] * (tiles // slots), axis=0)

    taps = [level(TAPS + lag) for lag in range(TIME_HALF + 1)]
    sources = [(other_refs[-1], LATER)] + ([] if pair else [(other_refs[0], EARLIER)])
    filtered = [[], []]
    for comp in range(comps):
        totals = [
            same_days(taps, [raw_ref[comp * days + s] for s in range(days)]) for raw_ref in raw_refs
        ]
        for source, base in sources:
            for s in range(days):
                edges = [None, None]
                for slot in range(slots):
                    value = source[comp, s, :, slot, :]
                    for k in range(2):
                        term = level(PICK + k * slots + slot) * value
                        edges[k] = term if edges[k] is None else edges[k] + term
                for t in range(days):
                    factor = level(base + t * days + s)
                    for k in range(2):
                        totals[k][t] = totals[k][t] + factor * edges[k]
        for k in range(2):
            filtered[k].append(totals[k])
    for k, packed_ref in enumerate(packed_refs):
        to_east = (level(EAST_LEVEL) > 0.5) if k == 0 else (level(EAST_LEVEL) < 0.5)
        packed = jnp.zeros((tiles, LANES), jnp.float32)
        for a in range(comps):
            for t in range(days):
                at = a * days + t
                value = level(COUPLING + 2 * a) * filtered[k][0][t]
                value = value + level(COUPLING + 2 * a + 1) * filtered[k][1][t]
                spot = jnp.where(to_east, GROUPS - 1 - at, -at % GROUPS)
                packed = jnp.where(group == spot, roll(value, -SPACE_HALF * at), packed)
        packed_ref[...] = packed


def two_parts(x):
    coarse = x.astype(jnp.bfloat16)
    return coarse, (x - coarse.astype(jnp.float32)).astype(jnp.bfloat16)


def build_plans(place_ref, mask_ref, space_ref, nb_ref, level_ref, plan_ref):
    shape = level_ref.shape[1:]
    slots = shape[0]
    nb = nb_ref[...]
    me = place_ref[0]
    for lag in range(SPACE_HALF + 1):
        level_ref[lag] = jnp.full(shape, space_ref[1, lag], jnp.float32)
    level_ref[SPACE_HALF + 1] = live_vector(mask_ref, iotas(slots)[1])

    def put_sides(at, west, east, device):
        index, near, remote = sides_of(nb, west, east, device, shape)
        plan_ref[at] = index
        plan_ref[at + 1] = near.astype(jnp.int32)
        plan_ref[at + 2] = remote.astype(jnp.int32)

    put_sides(BESIDE, WEST, EAST, me)
    put_sides(UPPER, NORTH_WEST, NORTH_EAST, me - REACH)
    put_sides(LOWER, SOUTH_WEST, SOUTH_EAST, me + REACH)
    for at, direction in ((UPPER, NORTH), (LOWER, SOUTH)):
        target = entry(nb, direction, shape)
        plan_ref[at + 3] = jnp.bitwise_and(target, slots - 1)
        plan_ref[at + 4] = (target >= 0).astype(jnp.int32)
    plan_ref[EAST_FLAG] = jnp.full(shape, jnp.where(east_first(place_ref), 1, 0), jnp.int32)
    plan_ref[SOUTH_FLAG] = jnp.full(shape, jnp.where(south_first(place_ref), 1, 0), jnp.int32)


def plan_at(plan_ref, at):
    return plan_ref[at], plan_ref[at + 1] != 0, plan_ref[at + 2] != 0


def flag_of(plan_ref, at, rows):
    return jnp.broadcast_to(plan_ref[at, :1], (rows, LANES)) != 0


def build_bands(taps_ref, bands_ref):
    shape = (2 * LANES, LANES)
    source = lax.broadcasted_iota(jnp.int32, shape, 0)
    target = lax.broadcasted_iota(jnp.int32, shape, 1)
    same = jnp.bitwise_and(source // SIDE, 1) == target // SIDE
    source_column = jnp.bitwise_and(source, SIDE - 1)
    outside = jnp.where(source_column >= SIDE // 2, source_column - SIDE, source_column + SIDE)
    position = jnp.where(source < LANES, source_column, outside)
    distance = jnp.abs(position - jnp.bitwise_and(target, SIDE - 1))
    bands = jnp.zeros(shape, jnp.float32)
    for lag in range(SPACE_HALF + 1):
        bands = jnp.where(same & (distance == lag), taps_ref[0, lag], bands)
    coarse, fine = two_parts(bands)
    bands_ref[: 2 * LANES, :LANES] = coarse
    bands_ref[: 2 * LANES, LANES:] = fine
    bands_ref[2 * LANES :, :LANES] = coarse
    bands_ref[2 * LANES :, LANES:] = jnp.zeros_like(fine)


def mix_kernel(
    pair, place_ref, mask_ref, taps_ref, factor_ref, space_ref, nb_ref, x_ref, *rest
):
    *other_refs, mixed_ref, first_ref, second_ref, bands_ref, level_ref, plan_ref = rest
    build_bands(space_ref, bands_ref)
    build_plans(place_ref, mask_ref, space_ref, nb_ref, level_ref, plan_ref)
    _, tiles, slots, _ = mixed_ref.shape
    comps, days = other_refs[0].shape[:2]
    _, sublane = iotas(slots)
    live = live_vector(mask_ref, sublane)
    taps = taps_of(taps_ref)
    weights = [[live * value for value in row] for row in coupling_of(factor_ref)]
    order = order_of(pair, place_ref[1], days)

    def body(tile, _):
        filtered = []
        for comp in range(comps):
            totals = same_days(taps, [x_ref[comp, order[t], tile] for t in range(days)])
            add_later(taps, totals, [other_refs[-1][comp, order[s], tile] for s in range(days)])
            if not pair:
                add_earlier(taps, totals, [other_refs[0][comp, s, tile] for s in range(days)])
            filtered.append(totals)
        for a in range(comps):
            for t in range(days):
                mixed_ref[a * days + order[t], tile] = (
                    weights[a][0] * filtered[0][t] + weights[a][1] * filtered[1][t]
                )
        return 0

    lax.fori_loop(0, tiles, body, 0, unroll=4)
    for sent_ref, start in zip((first_ref, second_ref), strip_starts(place_ref, tiles)):
        for item in range(comps * days):
            sent_ref[item] = mixed_ref[item, pl.ds(start, PAIR_ROWS)]


def west_east(plan_ref, first, second):
    flag = flag_of(plan_ref, EAST_FLAG, first.shape[0])
    return jnp.where(flag, second, first), jnp.where(flag, first, second)


def unpacked(item, west, east):
    lane = lax.broadcasted_iota(jnp.int32, west.shape, 1)
    shift = SPACE_HALF * item
    from_west = jnp.bitwise_and(lane + shift, SIDE // 2) != 0
    return roll(jnp.where(from_west, west, east), shift)


def corner_kernel(plan_ref, second_ref, first_ref, *refs):
    one_ref, two_ref = refs[-2:]
    slots = one_ref.shape[2]
    south = flag_of(plan_ref, SOUTH_FLAG, slots)
    for k, side in enumerate(west_east(plan_ref, first_ref[...], second_ref[...])):
        top, bottom = side[:slots], side[-slots:]
        one_ref[0, k] = jnp.where(south, bottom, top)
        two_ref[0, k] = jnp.where(south, top, bottom)


def across(bands, tiles):
    slots = tiles[0][0].shape[0]
    centre_parts = two_parts(jnp.concatenate([centre for centre, _ in tiles], axis=0))
    halo_parts = two_parts(jnp.concatenate([halo for _, halo in tiles], axis=0))
    product = jnp.dot(
        jnp.concatenate([part for both in zip(centre_parts, halo_parts) for part in both], axis=1),
        bands,
        preferred_element_type=jnp.float32,
    )
    product = product[:, :LANES] + product[:, LANES:]
    return [product[slots * p : slots * (p + 1)] for p in range(len(tiles))]


def sides_of(nb, west, east, device, shape):
    slots = shape[0]
    column = jnp.bitwise_and(lax.broadcasted_iota(jnp.int32, shape, 1), SIDE - 1)
    target = jnp.where(column >= SIDE // 2, entry(nb, west, shape), entry(nb, east, shape))
    near = on_device(target, device, slots)
    return jnp.bitwise_and(target, slots - 1), near, (target >= 0) & ~near


def halo_of(source, far, plan):
    index, near, remote = plan
    halo = jnp.where(near, pick(source, index), 0.0)
    return jnp.where(remote, jnp.broadcast_to(far, halo.shape), halo)


def odd_rows(before, after):
    low = lax.broadcasted_iota(jnp.int32, before.shape, 1) < SIDE
    return roll(jnp.where(low, after, before), SIDE)


def inner_kernel(
    level_ref, plan_ref, bands_ref, mixed_ref, second_ref, first_ref,
    out_hbm, outer_ref, out_ref, far_ref, stored,
):
    count, tiles, slots, _ = mixed_ref.shape
    lane, sublane = iotas(slots)
    live = level_ref[SPACE_HALF + 1]
    taps = [level_ref[lag] for lag in range(SPACE_HALF + 1)]
    plan = plan_at(plan_ref, BESIDE)
    west, east = west_east(plan_ref, first_ref[...], second_ref[...])
    together = far_ref.shape[0]

    def store(step):
        part = pl.ds(step * together, together)
        return pltpu.make_async_copy(out_ref.at[part], out_hbm.at[part], stored.at[step])

    def body(step, _):
        fetched = []
        for k in range(together):
            item = step * together + k
            far_ref[k] = unpacked(item, west, east)
            for tile in range(tiles):
                centre = mixed_ref[item, tile]
                fetched.append((centre, halo_of(centre, far_ref[k, tile : tile + 1], plan)))
        lines = across(bands_ref[...], fetched)
        zero = jnp.zeros(lane.shape, jnp.float32)
        for k in range(together):
            item = step * together + k
            rows = [zero] * PAIR_ROWS + lines[k * tiles : (k + 1) * tiles] + [zero] * PAIR_ROWS
            odd = [odd_rows(rows[p], rows[p + 1]) for p in range(len(rows) - 1)]
            for p in range(tiles):
                total = taps[0] * rows[p + 2]
                total = total + taps[1] * (odd[p + 1] + odd[p + 2])
                total = total + taps[2] * (rows[p + 1] + rows[p + 3])
                total = total + taps[3] * (odd[p] + odd[p + 3])
                total = total + taps[4] * (rows[p] + rows[p + 4])
                total = live * total
                out_ref[item, p] = total
                if p < PAIR_ROWS:
                    outer_ref[item, p] = total
                elif p >= tiles - PAIR_ROWS:
                    outer_ref[item, p - tiles + 2 * PAIR_ROWS] = total
        store(step).start()
        return 0

    lax.fori_loop(0, count // together, body, 0)
    for step in range(count // together):
        store(step).wait()


def outer_kernel(
    level_ref, plan_ref, bands_ref, outer_ref, first_ref, second_ref,
    _, out_hbm, out_ref, stored,
):
    count, _, slots, _ = outer_ref.shape
    tiles = out_hbm.shape[1]
    lane, sublane = iotas(slots)
    live = level_ref[SPACE_HALF + 1]
    taps = [level_ref[lag] for lag in range(SPACE_HALF + 1)]
    south = plan_ref[SOUTH_FLAG] != 0
    fetched = []
    for north in (True, False):
        use_first = ~south if north else south

        def read(index, part, use_first=use_first):
            return jnp.where(use_first, first_ref[index, part], second_ref[index, part])

        at = UPPER if north else LOWER
        plan = plan_at(plan_ref, at)
        index, present = plan_ref[at + 3], plan_ref[at + 4] != 0
        corner = [read(count, 0), read(count, 1)]
        for item in range(count):
            far = unpacked(item, *corner)
            for part in range(PAIR_ROWS):
                source = read(item, part)
                centre = jnp.where(present, pick(source, index), 0.0)
                row = slots - PAIR_ROWS + part if north else part
                fetched.append((centre, halo_of(source, far[row : row + 1], plan)))
    rows = across(bands_ref[...], fetched)
    zero = jnp.zeros(lane.shape, jnp.float32)
    copies = []
    for side in range(2):
        for item in range(count):
            at = (side * count + item) * PAIR_ROWS
            one, two = rows[at : at + PAIR_ROWS]
            close, far = (one, two) if side else (two, one)
            edge = odd_rows(zero, one) if side else odd_rows(two, zero)
            near = taps[1] * edge + taps[2] * close + taps[3] * odd_rows(one, two)
            near = near + taps[4] * far
            off = taps[3] * edge + taps[4] * close
            for part, value in enumerate((off, near) if side else (near, off)):
                out_ref[side, item, part] = (
                    outer_ref[item, side * PAIR_ROWS + part] + live * value
                )
        place = pl.ds(side * (tiles - PAIR_ROWS), PAIR_ROWS)
        copy = pltpu.make_async_copy(out_ref.at[side], out_hbm.at[:, place], stored.at[side])
        copy.start()
        copies.append(copy)
    for copy in copies:
        copy.wait()


def swap_both(first, second, index, length):
    blk, day = lax.axis_size("blk"), lax.axis_size("day")
    results = []
    for x, shift in ((first, 0), (second, 1)):
        partner = {}
        for at in range(shift, length + shift, 2):
            low, high = at % length, (at + 1) % length
            partner[low], partner[high] = high, low
        pairs = []
        for i in range(blk):
            at, step = index(i)
            across_chip = day == 2 and abs(partner[at] - at) > 1
            other = i if across_chip else i + (partner[at] - at) * step
            for core in range(day):
                pairs.append((i * day + core, other * day + (1 - core if across_chip else core)))
        results.append(lax.ppermute(x, ("blk", "day"), pairs))
    return results


def shards(input_field, active_mask, neighbours, time_taps, space_taps, coregion_factor):
    comps, days, slots, cells = input_field.shape
    count = comps * days
    tiles = cells // LANES
    blk = lax.axis_size("blk")
    day = lax.axis_size("day")
    pair = day == 2
    sides = 2
    place = jnp.stack([lax.axis_index("blk"), lax.axis_index("day")]).astype(jnp.int32)

    def in_tiles(x):
        return x.reshape(comps, days, slots, tiles, LANES).transpose(0, 1, 3, 2, 4)

    if pair:
        others = [lax.ppermute(input_field, "day", [(0, 1), (1, 0)])]
    else:
        up = [(i, i + 1) for i in range(day - 1)]
        others = [
            lax.ppermute(input_field, "day", up),
            lax.ppermute(input_field, "day", [(b, a) for a, b in up]),
        ]
    others = [in_tiles(x) for x in others]
    field = array(count, tiles, slots, LANES)

    x = in_tiles(input_field)
    *raw, values = pl.pallas_call(
        functools.partial(own_kernel, pair),
        out_shape=(array(count, tiles, LANES),) * 2
        + (array(VALUES, slots, LANES),),
        in_specs=[SMEM] * 5 + [WHOLE],
        out_specs=(WHOLE,) * 3,
        compiler_params=PARAMS,
        name="own_days",
    )(place, active_mask, time_taps, coregion_factor, neighbours, x)

    sent_count = count + 1
    sent_shape = array(sent_count, PAIR_ROWS, slots, LANES)
    packed = pl.pallas_call(
        functools.partial(edge_kernel, pair),
        out_shape=(array(tiles, LANES),) * 2,
        in_specs=[WHOLE] * (3 + len(others)),
        out_specs=(WHOLE,) * 2,
        compiler_params=PARAMS,
        name="edges",
    )(values, *raw, *others)
    first, second = swap_both(*packed, lambda i: (i % REACH, 1), REACH)

    mixed, *sent, bands, level, plan = pl.pallas_call(
        functools.partial(mix_kernel, pair),
        out_shape=(
            field,
            sent_shape,
            sent_shape,
            jax.ShapeDtypeStruct((4 * LANES, 2 * LANES), jnp.bfloat16),
            array(SPACE_HALF + 2, slots, LANES),
            jax.ShapeDtypeStruct((PLANS, slots, LANES), jnp.int32),
        ),
        in_specs=[SMEM] * 5 + [WHOLE] * (2 + len(others)),
        out_specs=(WHOLE,) * 6,
        compiler_params=PARAMS,
        cost_estimate=pl.CostEstimate(
            flops=20 * field.size, bytes_accessed=12 * field.size, transcendentals=0
        ),
        name="mix",
    )(place, active_mask, time_taps, coregion_factor, space_taps, neighbours, x, *others)

    sent = pl.pallas_call(
        corner_kernel,
        grid=(1,),
        out_shape=(sent_shape,) * sides,
        in_specs=[WHOLE] * 3 + [pl.BlockSpec(memory_space=pl.ANY)] * (sides + 1),
        out_specs=(
            pl.BlockSpec((1, PAIR_ROWS, slots, LANES), lambda i: (sent_count - 1, 0, 0, 0)),
        )
        * sides,
        input_output_aliases={4 + side: side for side in range(sides)},
        compiler_params=PARAMS,
        name="corners",
    )(plan, second, first, mixed, *sent)

    one, two = swap_both(*sent, lambda i: (i // REACH, REACH), blk // REACH)

    together = 2
    inner, outer = pl.pallas_call(
        inner_kernel,
        out_shape=(field, array(count, 2 * PAIR_ROWS, slots, LANES)),
        in_specs=[WHOLE] * 6,
        out_specs=(IN_HBM, WHOLE),
        scratch_shapes=[
            pltpu.VMEM(field.shape, jnp.float32),
            pltpu.VMEM((together, tiles, LANES), jnp.float32),
            DMA((count // together,)),
        ],
        compiler_params=PARAMS,
        cost_estimate=pl.CostEstimate(
            flops=4 * field.size * LANES, bytes_accessed=8 * field.size, transcendentals=0
        ),
        name="inner_rows",
    )(level, plan, bands, mixed, second, first)

    result = pl.pallas_call(
        outer_kernel,
        out_shape=field,
        in_specs=[WHOLE] * 6 + [IN_HBM],
        out_specs=IN_HBM,
        scratch_shapes=[
            pltpu.VMEM((2, count, PAIR_ROWS, slots, LANES), jnp.float32),
            DMA((2,)),
        ],
        input_output_aliases={6: 0},
        compiler_params=PARAMS,
        name="outer_rows",
    )(level, plan, bands, outer, one, two, inner)
    result = result.reshape(comps, days, tiles, slots, LANES).transpose(0, 1, 3, 2, 4)
    return result.reshape(input_field.shape)


def solution(mesh):
    in_specs = (P(None, "day", "blk", None), P("blk"), P("blk", None), P(), P(), P())
    out_specs = P(None, "day", "blk", None)
    return jax.shard_map(shards, mesh=mesh, in_specs=in_specs, out_specs=out_specs, check_vma=False)
```

```python
import functools

import jax
import jax.numpy as jnp
from jax import lax
from jax.experimental import pallas as pl
from jax.experimental.pallas import tpu as pltpu
from jax.sharding import PartitionSpec as P

SIDE = 64
SPACE_HALF = 4
TIME_HALF = 3
REACH = 4
LANES = 128
EAST, WEST, NORTH, SOUTH, NORTH_EAST, NORTH_WEST, SOUTH_EAST, SOUTH_WEST = range(8)
PAIR_ROWS = SPACE_HALF * SIDE // LANES
GROUPS = SIDE // SPACE_HALF
BESIDE, UPPER, LOWER, EAST_FLAG, SOUTH_FLAG, PLANS = 0, 3, 8, 13, 14, 15
PICK, COUPLING, TAPS, LATER, EARLIER, EAST_LEVEL, VALUES = 0, 16, 20, 24, 33, 42, 43
PARAMS = pltpu.CompilerParams(vmem_limit_bytes=12 * 1024 * 1024)
SMEM = pl.BlockSpec(memory_space=pltpu.SMEM)
WHOLE = pl.BlockSpec(memory_space=pltpu.VMEM)
IN_HBM = pl.BlockSpec(memory_space=pltpu.HBM)
DMA = pltpu.SemaphoreType.DMA


def array(*shape):
    return jax.ShapeDtypeStruct(shape, jnp.float32)


def iotas(slots):
    lane = lax.broadcasted_iota(jnp.int32, (slots, LANES), 1)
    sublane = lax.broadcasted_iota(jnp.int32, (slots, LANES), 0)
    return lane, sublane


def live_vector(mask_ref, sublane):
    live = jnp.zeros(sublane.shape, jnp.float32)
    for slot in range(sublane.shape[0]):
        live = jnp.where(sublane == slot, mask_ref[slot].astype(jnp.float32), live)
    return live


def entry(neighbours, direction, shape):
    return jnp.broadcast_to(neighbours[:, direction : direction + 1], shape)


def pick(source, index):
    return jnp.take_along_axis(source, index, axis=0)


def roll(x, shift):
    return pltpu.roll(x, shift % LANES if isinstance(shift, int) else shift, 1)


def wrapped(shift):
    return jnp.bitwise_and(shift, LANES - 1)


def device_of(target, slots):
    return lax.shift_right_arithmetic(target, jnp.int32(slots.bit_length() - 1))


def on_device(target, device, slots):
    return (target >= 0) & (device_of(target, slots) == device)


def taps_of(taps_ref):
    return [taps_ref[lag] for lag in range(TIME_HALF + 1)]


def order_of(pair, day, days):
    return [day * (days - 1 - 2 * s) + s if pair else s for s in range(days)]


def coupling_of(factor_ref):
    return [
        [
            factor_ref[a, 0] * factor_ref[b, 0] + factor_ref[a, 1] * factor_ref[b, 1]
            for b in range(2)
        ]
        for a in range(2)
    ]


def same_days(taps, values):
    totals = []
    for t in range(len(values)):
        total = taps[0] * values[t]
        for s in range(len(values)):
            if s != t:
                total = total + taps[abs(s - t)] * values[s]
        totals.append(total)
    return totals


def add_later(taps, totals, values):
    for t in range(len(totals)):
        for s in range(t + 1):
            totals[t] = totals[t] + taps[len(totals) + s - t] * values[s]


def add_earlier(taps, totals, values):
    for t in range(len(totals)):
        for s in range(t, len(totals)):
            totals[t] = totals[t] + taps[len(totals) + t - s] * values[s]


def east_first(place_ref):
    return jnp.bitwise_and(place_ref[0], 1) == 0


def south_first(place_ref):
    return jnp.bitwise_and(place_ref[0], REACH) == 0


def end_slot(nb_ref, me, east):
    slots = nb_ref.shape[0]
    step, directions = (
        (1, (EAST, NORTH_EAST, SOUTH_EAST)) if east else (-1, (WEST, NORTH_WEST, SOUTH_WEST))
    )
    found = jnp.int32(0)
    for slot in range(slots):
        for direction, shift in zip(directions, (0, -REACH, REACH)):
            target = nb_ref[slot, direction]
            hit = (target >= 0) & (device_of(target, slots) == me + step + shift)
            found = jnp.where(hit, slot, found)
    return found


def edge_plan(place_ref, nb_ref):
    me = place_ref[0]
    east, west = end_slot(nb_ref, me, True), end_slot(nb_ref, me, False)
    first = east_first(place_ref)
    return [(first, jnp.where(first, east, west)), (~first, jnp.where(first, west, east))]


def strip_starts(place_ref, tiles):
    last = tiles - PAIR_ROWS
    first = south_first(place_ref)
    return [jnp.where(first, last, 0), jnp.where(first, 0, last)]


def write_values(pair, place_ref, mask_ref, taps, factor_ref, ends, value_ref):
    shape = value_ref.shape[1:]
    slots = shape[0]
    days = len(taps) - 1

    def put(at, value):
        value_ref[at] = jnp.full(shape, value, jnp.float32)

    for k, (_, slot) in enumerate(ends):
        live = mask_ref[slot].astype(jnp.float32)
        for s in range(slots):
            put(PICK + k * slots + s, jnp.where(slot == s, live, 0.0))
    for a, row in enumerate(coupling_of(factor_ref)):
        for b, value in enumerate(row):
            put(COUPLING + 2 * a + b, value)
    for lag, value in enumerate(taps):
        put(TAPS + lag, value)
    for t in range(days):
        for s in range(days):
            later = taps[days + s - t] if s <= t else 0.0
            earlier = taps[days + t - s] if s >= t else 0.0
            if pair:
                later = jnp.where(place_ref[1] == 0, later, earlier)
            put(LATER + t * days + s, later)
            put(EARLIER + t * days + s, earlier)
    put(EAST_LEVEL, jnp.where(east_first(place_ref), 1.0, 0.0))


def own_kernel(
    pair, place_ref, mask_ref, taps_ref, factor_ref, nb_ref, x_ref, own_ref, *refs
):
    *edge_refs, value_ref = refs
    comps, days, tiles, slots, _ = x_ref.shape
    taps = taps_of(taps_ref)
    ends = edge_plan(place_ref, nb_ref)
    write_values(pair, place_ref, mask_ref, taps, factor_ref, ends, value_ref)
    for edge_ref, (_, slot) in zip(edge_refs, ends):
        live = mask_ref[slot].astype(jnp.float32)
        for comp in range(comps):
            for t in range(days):
                edge_ref[comp * days + t] = live * x_ref[comp, t, :, slot, :]
    def body(tile, _):
        for comp in range(comps):
            values = [x_ref[comp, t, tile] for t in range(days)]
            for t, total in enumerate(same_days(taps, values)):
                own_ref[comp * days + t, tile] = total
        return 0

    lax.fori_loop(0, tiles, body, 0, unroll=4)


def edge_kernel(pair, value_ref, *refs):
    raw_refs, other_refs, packed_refs = refs[:2], refs[2:-2], refs[-2:]
    comps, days, tiles, slots, _ = other_refs[0].shape
    column = jnp.bitwise_and(lax.broadcasted_iota(jnp.int32, (tiles, LANES), 1), SIDE - 1)
    group = lax.shift_right_logical(column, jnp.int32(SPACE_HALF.bit_length() - 1))

    def level(at):
        return jnp.concatenate([value_ref[at]] * (tiles // slots), axis=0)

    taps = [level(TAPS + lag) for lag in range(TIME_HALF + 1)]
    sources = [(other_refs[-1], LATER)] + ([] if pair else [(other_refs[0], EARLIER)])
    filtered = [[], []]
    for comp in range(comps):
        totals = [
            same_days(taps, [raw_ref[comp * days + s] for s in range(days)]) for raw_ref in raw_refs
        ]
        for source, base in sources:
            for s in range(days):
                edges = [None, None]
                for slot in range(slots):
                    value = source[comp, s, :, slot, :]
                    for k in range(2):
                        term = level(PICK + k * slots + slot) * value
                        edges[k] = term if edges[k] is None else edges[k] + term
                for t in range(days):
                    factor = level(base + t * days + s)
                    for k in range(2):
                        totals[k][t] = totals[k][t] + factor * edges[k]
        for k in range(2):
            filtered[k].append(totals[k])
    for k, packed_ref in enumerate(packed_refs):
        to_east = (level(EAST_LEVEL) > 0.5) if k == 0 else (level(EAST_LEVEL) < 0.5)
        packed = jnp.zeros((tiles, LANES), jnp.float32)
        for a in range(comps):
            for t in range(days):
                at = a * days + t
                value = level(COUPLING + 2 * a) * filtered[k][0][t]
                value = value + level(COUPLING + 2 * a + 1) * filtered[k][1][t]
                spot = jnp.where(to_east, GROUPS - 1 - at, -at % GROUPS)
                packed = jnp.where(group == spot, roll(value, -SPACE_HALF * at), packed)
        packed_ref[...] = packed


def two_parts(x):
    coarse = x.astype(jnp.bfloat16)
    return coarse, (x - coarse.astype(jnp.float32)).astype(jnp.bfloat16)


def build_plans(place_ref, mask_ref, space_ref, nb_ref, level_ref, plan_ref):
    shape = level_ref.shape[1:]
    slots = shape[0]
    nb = nb_ref[...]
    me = place_ref[0]
    for lag in range(SPACE_HALF + 1):
        level_ref[lag] = jnp.full(shape, space_ref[1, lag], jnp.float32)
    level_ref[SPACE_HALF + 1] = live_vector(mask_ref, iotas(slots)[1])

    def put_sides(at, west, east, device):
        index, near, remote = sides_of(nb, west, east, device, shape)
        plan_ref[at] = index
        plan_ref[at + 1] = near.astype(jnp.int32)
        plan_ref[at + 2] = remote.astype(jnp.int32)

    put_sides(BESIDE, WEST, EAST, me)
    put_sides(UPPER, NORTH_WEST, NORTH_EAST, me - REACH)
    put_sides(LOWER, SOUTH_WEST, SOUTH_EAST, me + REACH)
    for at, direction in ((UPPER, NORTH), (LOWER, SOUTH)):
        target = entry(nb, direction, shape)
        plan_ref[at + 3] = jnp.bitwise_and(target, slots - 1)
        plan_ref[at + 4] = (target >= 0).astype(jnp.int32)
    plan_ref[EAST_FLAG] = jnp.full(shape, jnp.where(east_first(place_ref), 1, 0), jnp.int32)
    plan_ref[SOUTH_FLAG] = jnp.full(shape, jnp.where(south_first(place_ref), 1, 0), jnp.int32)


def plan_at(plan_ref, at):
    return plan_ref[at], plan_ref[at + 1] != 0, plan_ref[at + 2] != 0


def flag_of(plan_ref, at, rows):
    return jnp.broadcast_to(plan_ref[at, :1], (rows, LANES)) != 0


def build_bands(taps_ref, bands_ref):
    shape = (2 * LANES, LANES)
    source = lax.broadcasted_iota(jnp.int32, shape, 0)
    target = lax.broadcasted_iota(jnp.int32, shape, 1)
    same = jnp.bitwise_and(source // SIDE, 1) == target // SIDE
    source_column = jnp.bitwise_and(source, SIDE - 1)
    outside = jnp.where(source_column >= SIDE // 2, source_column - SIDE, source_column + SIDE)
    position = jnp.where(source < LANES, source_column, outside)
    distance = jnp.abs(position - jnp.bitwise_and(target, SIDE - 1))
    bands = jnp.zeros(shape, jnp.float32)
    for lag in range(SPACE_HALF + 1):
        bands = jnp.where(same & (distance == lag), taps_ref[0, lag], bands)
    coarse, fine = two_parts(bands)
    bands_ref[: 2 * LANES, :LANES] = coarse
    bands_ref[: 2 * LANES, LANES:] = fine
    bands_ref[2 * LANES :, :LANES] = coarse
    bands_ref[2 * LANES :, LANES:] = jnp.zeros_like(fine)


def mix_kernel(
    pair, place_ref, mask_ref, taps_ref, factor_ref, space_ref, nb_ref, own_ref, *rest
):
    *other_refs, mixed_ref, first_ref, second_ref, bands_ref, level_ref, plan_ref = rest
    build_bands(space_ref, bands_ref)
    build_plans(place_ref, mask_ref, space_ref, nb_ref, level_ref, plan_ref)
    _, tiles, slots, _ = mixed_ref.shape
    comps, days = other_refs[0].shape[:2]
    _, sublane = iotas(slots)
    live = live_vector(mask_ref, sublane)
    taps = taps_of(taps_ref)
    weights = [[live * value for value in row] for row in coupling_of(factor_ref)]
    order = order_of(pair, place_ref[1], days)

    def body(tile, _):
        filtered = []
        for comp in range(comps):
            totals = [own_ref[comp * days + order[t], tile] for t in range(days)]
            add_later(taps, totals, [other_refs[-1][comp, order[s], tile] for s in range(days)])
            if not pair:
                add_earlier(taps, totals, [other_refs[0][comp, s, tile] for s in range(days)])
            filtered.append(totals)
        for a in range(comps):
            for t in range(days):
                mixed_ref[a * days + order[t], tile] = (
                    weights[a][0] * filtered[0][t] + weights[a][1] * filtered[1][t]
                )
        return 0

    lax.fori_loop(0, tiles, body, 0, unroll=4)
    for sent_ref, start in zip((first_ref, second_ref), strip_starts(place_ref, tiles)):
        for item in range(comps * days):
            sent_ref[item] = mixed_ref[item, pl.ds(start, PAIR_ROWS)]


def west_east(plan_ref, first, second):
    flag = flag_of(plan_ref, EAST_FLAG, first.shape[0])
    return jnp.where(flag, second, first), jnp.where(flag, first, second)


def unpacked(item, west, east):
    lane = lax.broadcasted_iota(jnp.int32, west.shape, 1)
    shift = SPACE_HALF * item
    from_west = jnp.bitwise_and(lane + shift, SIDE // 2) != 0
    return roll(jnp.where(from_west, west, east), shift)


def corner_kernel(plan_ref, second_ref, first_ref, *refs):
    one_ref, two_ref = refs[-2:]
    slots = one_ref.shape[2]
    south = flag_of(plan_ref, SOUTH_FLAG, slots)
    for k, side in enumerate(west_east(plan_ref, first_ref[...], second_ref[...])):
        top, bottom = side[:slots], side[-slots:]
        one_ref[0, k] = jnp.where(south, bottom, top)
        two_ref[0, k] = jnp.where(south, top, bottom)


def across(bands, tiles):
    slots = tiles[0][0].shape[0]
    centre_parts = two_parts(jnp.concatenate([centre for centre, _ in tiles], axis=0))
    halo_parts = two_parts(jnp.concatenate([halo for _, halo in tiles], axis=0))
    product = jnp.dot(
        jnp.concatenate([part for both in zip(centre_parts, halo_parts) for part in both], axis=1),
        bands,
        preferred_element_type=jnp.float32,
    )
    product = product[:, :LANES] + product[:, LANES:]
    return [product[slots * p : slots * (p + 1)] for p in range(len(tiles))]


def sides_of(nb, west, east, device, shape):
    slots = shape[0]
    column = jnp.bitwise_and(lax.broadcasted_iota(jnp.int32, shape, 1), SIDE - 1)
    target = jnp.where(column >= SIDE // 2, entry(nb, west, shape), entry(nb, east, shape))
    near = on_device(target, device, slots)
    return jnp.bitwise_and(target, slots - 1), near, (target >= 0) & ~near


def halo_of(source, far, plan):
    index, near, remote = plan
    halo = jnp.where(near, pick(source, index), 0.0)
    return jnp.where(remote, jnp.broadcast_to(far, halo.shape), halo)


def odd_rows(before, after):
    low = lax.broadcasted_iota(jnp.int32, before.shape, 1) < SIDE
    return roll(jnp.where(low, after, before), SIDE)


def inner_kernel(
    level_ref, plan_ref, bands_ref, mixed_ref, second_ref, first_ref,
    out_hbm, outer_ref, out_ref, far_ref, stored,
):
    count, tiles, slots, _ = mixed_ref.shape
    lane, sublane = iotas(slots)
    live = level_ref[SPACE_HALF + 1]
    taps = [level_ref[lag] for lag in range(SPACE_HALF + 1)]
    plan = plan_at(plan_ref, BESIDE)
    west, east = west_east(plan_ref, first_ref[...], second_ref[...])
    together = far_ref.shape[0]

    def store(step):
        part = pl.ds(step * together, together)
        return pltpu.make_async_copy(out_ref.at[part], out_hbm.at[part], stored.at[step])

    def body(step, _):
        fetched = []
        for k in range(together):
            item = step * together + k
            far_ref[k] = unpacked(item, west, east)
            for tile in range(tiles):
                centre = mixed_ref[item, tile]
                fetched.append((centre, halo_of(centre, far_ref[k, tile : tile + 1], plan)))
        lines = across(bands_ref[...], fetched)
        zero = jnp.zeros(lane.shape, jnp.float32)
        for k in range(together):
            item = step * together + k
            rows = [zero] * PAIR_ROWS + lines[k * tiles : (k + 1) * tiles] + [zero] * PAIR_ROWS
            odd = [odd_rows(rows[p], rows[p + 1]) for p in range(len(rows) - 1)]
            for p in range(tiles):
                total = taps[0] * rows[p + 2]
                total = total + taps[1] * (odd[p + 1] + odd[p + 2])
                total = total + taps[2] * (rows[p + 1] + rows[p + 3])
                total = total + taps[3] * (odd[p] + odd[p + 3])
                total = total + taps[4] * (rows[p] + rows[p + 4])
                total = live * total
                out_ref[item, p] = total
                if p < PAIR_ROWS:
                    outer_ref[item, p] = total
                elif p >= tiles - PAIR_ROWS:
                    outer_ref[item, p - tiles + 2 * PAIR_ROWS] = total
        store(step).start()
        return 0

    lax.fori_loop(0, count // together, body, 0)
    for step in range(count // together):
        store(step).wait()


def outer_kernel(
    level_ref, plan_ref, bands_ref, outer_ref, first_ref, second_ref,
    _, out_hbm, out_ref, stored,
):
    count, _, slots, _ = outer_ref.shape
    tiles = out_hbm.shape[1]
    lane, sublane = iotas(slots)
    live = level_ref[SPACE_HALF + 1]
    taps = [level_ref[lag] for lag in range(SPACE_HALF + 1)]
    south = plan_ref[SOUTH_FLAG] != 0
    fetched = []
    for north in (True, False):
        use_first = ~south if north else south

        def read(index, part, use_first=use_first):
            return jnp.where(use_first, first_ref[index, part], second_ref[index, part])

        at = UPPER if north else LOWER
        plan = plan_at(plan_ref, at)
        index, present = plan_ref[at + 3], plan_ref[at + 4] != 0
        corner = [read(count, 0), read(count, 1)]
        for item in range(count):
            far = unpacked(item, *corner)
            for part in range(PAIR_ROWS):
                source = read(item, part)
                centre = jnp.where(present, pick(source, index), 0.0)
                row = slots - PAIR_ROWS + part if north else part
                fetched.append((centre, halo_of(source, far[row : row + 1], plan)))
    rows = across(bands_ref[...], fetched)
    zero = jnp.zeros(lane.shape, jnp.float32)
    copies = []
    for side in range(2):
        for item in range(count):
            at = (side * count + item) * PAIR_ROWS
            one, two = rows[at : at + PAIR_ROWS]
            close, far = (one, two) if side else (two, one)
            edge = odd_rows(zero, one) if side else odd_rows(two, zero)
            near = taps[1] * edge + taps[2] * close + taps[3] * odd_rows(one, two)
            near = near + taps[4] * far
            off = taps[3] * edge + taps[4] * close
            for part, value in enumerate((off, near) if side else (near, off)):
                out_ref[side, item, part] = (
                    outer_ref[item, side * PAIR_ROWS + part] + live * value
                )
        place = pl.ds(side * (tiles - PAIR_ROWS), PAIR_ROWS)
        copy = pltpu.make_async_copy(out_ref.at[side], out_hbm.at[:, place], stored.at[side])
        copy.start()
        copies.append(copy)
    for copy in copies:
        copy.wait()


def swap_both(first, second, index, length):
    blk, day = lax.axis_size("blk"), lax.axis_size("day")
    results = []
    for x, shift in ((first, 0), (second, 1)):
        partner = {}
        for at in range(shift, length + shift, 2):
            low, high = at % length, (at + 1) % length
            partner[low], partner[high] = high, low
        pairs = []
        for i in range(blk):
            at, step = index(i)
            across_chip = day == 2 and abs(partner[at] - at) > 1
            other = i if across_chip else i + (partner[at] - at) * step
            for core in range(day):
                pairs.append((i * day + core, other * day + (1 - core if across_chip else core)))
        results.append(lax.ppermute(x, ("blk", "day"), pairs))
    return results


def shards(input_field, active_mask, neighbours, time_taps, space_taps, coregion_factor):
    comps, days, slots, cells = input_field.shape
    count = comps * days
    tiles = cells // LANES
    blk = lax.axis_size("blk")
    day = lax.axis_size("day")
    pair = day == 2
    sides = 2
    place = jnp.stack([lax.axis_index("blk"), lax.axis_index("day")]).astype(jnp.int32)

    def in_tiles(x):
        return x.reshape(comps, days, slots, tiles, LANES).transpose(0, 1, 3, 2, 4)

    if pair:
        others = [lax.ppermute(input_field, "day", [(0, 1), (1, 0)])]
    else:
        up = [(i, i + 1) for i in range(day - 1)]
        others = [
            lax.ppermute(input_field, "day", up),
            lax.ppermute(input_field, "day", [(b, a) for a, b in up]),
        ]
    others = [in_tiles(x) for x in others]
    field = array(count, tiles, slots, LANES)

    own, *raw, values = pl.pallas_call(
        functools.partial(own_kernel, pair),
        out_shape=(field,)
        + (array(count, tiles, LANES),) * 2
        + (array(VALUES, slots, LANES),),
        in_specs=[SMEM] * 5 + [WHOLE],
        out_specs=(WHOLE,) * 4,
        compiler_params=PARAMS,
        name="own_days",
    )(place, active_mask, time_taps, coregion_factor, neighbours, in_tiles(input_field))

    sent_count = count + 1
    sent_shape = array(sent_count, PAIR_ROWS, slots, LANES)
    packed = pl.pallas_call(
        functools.partial(edge_kernel, pair),
        out_shape=(array(tiles, LANES),) * 2,
        in_specs=[WHOLE] * (3 + len(others)),
        out_specs=(WHOLE,) * 2,
        compiler_params=PARAMS,
        name="edges",
    )(values, *raw, *others)
    first, second = swap_both(*packed, lambda i: (i % REACH, 1), REACH)

    mixed, *sent, bands, level, plan = pl.pallas_call(
        functools.partial(mix_kernel, pair),
        out_shape=(
            field,
            sent_shape,
            sent_shape,
            jax.ShapeDtypeStruct((4 * LANES, 2 * LANES), jnp.bfloat16),
            array(SPACE_HALF + 2, slots, LANES),
            jax.ShapeDtypeStruct((PLANS, slots, LANES), jnp.int32),
        ),
        in_specs=[SMEM] * 5 + [WHOLE] * (2 + len(others)),
        out_specs=(WHOLE,) * 6,
        compiler_params=PARAMS,
        cost_estimate=pl.CostEstimate(
            flops=20 * field.size, bytes_accessed=12 * field.size, transcendentals=0
        ),
        name="mix",
    )(place, active_mask, time_taps, coregion_factor, space_taps, neighbours, own, *others)

    sent = pl.pallas_call(
        corner_kernel,
        grid=(1,),
        out_shape=(sent_shape,) * sides,
        in_specs=[WHOLE] * 3 + [pl.BlockSpec(memory_space=pl.ANY)] * (sides + 1),
        out_specs=(
            pl.BlockSpec((1, PAIR_ROWS, slots, LANES), lambda i: (sent_count - 1, 0, 0, 0)),
        )
        * sides,
        input_output_aliases={4 + side: side for side in range(sides)},
        compiler_params=PARAMS,
        name="corners",
    )(plan, second, first, mixed, *sent)

    one, two = swap_both(*sent, lambda i: (i // REACH, REACH), blk // REACH)

    together = 3
    inner, outer = pl.pallas_call(
        inner_kernel,
        out_shape=(field, array(count, 2 * PAIR_ROWS, slots, LANES)),
        in_specs=[WHOLE] * 6,
        out_specs=(IN_HBM, WHOLE),
        scratch_shapes=[
            pltpu.VMEM(field.shape, jnp.float32),
            pltpu.VMEM((together, tiles, LANES), jnp.float32),
            DMA((count // together,)),
        ],
        compiler_params=PARAMS,
        cost_estimate=pl.CostEstimate(
            flops=4 * field.size * LANES, bytes_accessed=8 * field.size, transcendentals=0
        ),
        name="inner_rows",
    )(level, plan, bands, mixed, second, first)

    result = pl.pallas_call(
        outer_kernel,
        out_shape=field,
        in_specs=[WHOLE] * 6 + [IN_HBM],
        out_specs=IN_HBM,
        scratch_shapes=[
            pltpu.VMEM((2, count, PAIR_ROWS, slots, LANES), jnp.float32),
            DMA((2,)),
        ],
        input_output_aliases={6: 0},
        compiler_params=PARAMS,
        name="outer_rows",
    )(level, plan, bands, outer, one, two, inner)
    result = result.reshape(comps, days, tiles, slots, LANES).transpose(0, 1, 3, 2, 4)
    return result.reshape(input_field.shape)


def solution(mesh):
    in_specs = (P(None, "day", "blk", None), P("blk"), P("blk", None), P(), P(), P())
    out_specs = P(None, "day", "blk", None)
    return jax.shard_map(shards, mesh=mesh, in_specs=in_specs, out_specs=out_specs, check_vma=False)
```
